32 devices in a mesh: grp: 2 (over x), tile: 8 (over z, y), wave: 2 (over core).
Axes of the slice: x: 2, y: 2, z: 4, core: 2. Of those that a mesh axis runs over, the one named last changes fastest.
Arguments:
- residual: float32 [16, 8, 2, 8, 128], P(('grp', 'tile'), 'wave'), parts along dimension 0, may hold values from -210 to 210
- kernel: bfloat16 [16, 8, 9, 2, 128, 128], P(('grp', 'tile'), 'wave'), parts along dimension 0, may hold values from -0.125 to 0.125
- offsets: float32 [16, 8, 2, 128], P(('grp', 'tile'), 'wave'), parts along dimension 0, may hold values from 0 to 1
- neighbor: int32 [16, 8, 9], P(('grp', 'tile'), 'wave'), parts along dimension 0, may hold values from 0 to 8, each once within a row
- frequency: int32 [16], P('grp'), parts along dimension 0, may hold values from 0 to 7, each once
- lattice_x: int32 [128], replicated, may hold values from 0 to 127, each once
- lattice_y: int32 [128], replicated, may hold values from 0 to 127, each once
- spectral_weight: float32 [8, 128, 128], replicated, may hold values from 0.1 to 3
Outputs:
- image_two: float32 [16, 8, 2, 8, 128], P(('grp', 'tile'), 'wave'), parts along dimension 0
- arnoldi: float32 [8, 8], P('grp'), parts along dimension 0
The draws below stay inside these ranges and needn't reach their ends.
There are 2 independent parts, one for each index of `grp`. The reference program is written for one: setup_inputs(seed, part) draws one part's arguments, and reference() takes and returns one part's arrays. A program takes and returns all parts, laid end to end along the dimension named above; an argument that names none is the same for every part. Nothing has to cross between parts.
Inputs may be any that keep to these rules, and one draw needn't show every extreme that they name: `neighbor`: each row names each of the nine neighbour slots once. `frequency`: each index appears once. `lattice_x`: each index appears once. `lattice_y`: each index appears once.
All inputs are finite; a program needn't handle non-finite values.
Results may differ from the reference program's by a relative error of at most 0.013.
Values may be sent and summed in bfloat16 or wider, within the bound.
No kernel may reach another device: no remote copies, remote signals or barrier semaphores. Data moves between devices by JAX's collectives and lax.ppermute only.
A program may use at most 64 MiB of HBM per device.

```python
import math
import jax
import jax.numpy as jnp
from jax import lax

PANELS_T = 128
VECTORS = 8
MODES_X = 128
MODES_Y = 128
FREQUENCIES = 8
GRID_X = 8
GRID_Y = 8
PANELS = 8192


def draw_residual(key, part):
    key_a, key_b = jax.random.split(key, 2)
    full_shape = (GRID_X, GRID_Y, 2, VECTORS, PANELS_T)
    column = jnp.arange(GRID_X, dtype=jnp.float32)[:, None, None, None, None] / max(GRID_X - 1, 1)
    spread = 10.0 ** jax.random.uniform(key_b, (GRID_X, GRID_Y, 1, 1, PANELS_T), dtype=jnp.float32)
    rising = 3.0 ** column
    values = jnp.clip(jax.random.normal(key_a, full_shape, dtype=jnp.float32), -4.0, 4.0)
    return values * rising * spread


def level_of(key, shape, cuts, least, top_value):
    gain = 1.0
    for dim, parts in cuts:
        heights = jax.random.uniform(jax.random.fold_in(jax.random.fold_in(key, 6), dim), (parts,), jnp.float32, least / len(cuts), top_value / len(cuts))
        gain = gain * jnp.repeat(jnp.exp(heights), shape[dim] // parts).reshape((-1,) + (1,) * (len(shape) - 1 - dim))
    return gain


def gaussian(own_key, shape, scale, most, cuts=(), kind=jnp.bfloat16):
    gain = level_of(own_key, shape, cuts, -0.22, 0.18) if cuts else 1.0
    entries = jax.random.normal(own_key, shape, jnp.float32) * scale * gain
    return jnp.minimum(jnp.maximum(entries, -most), most).astype(kind)


def setup_inputs(seed: int = 0, part: int = 0) -> dict:
    key_list = jax.random.split(jax.random.key(seed), 9)
    part_keys = jax.random.split(jax.random.fold_in(key_list[8], part), 9)
    return {
        "residual": draw_residual(jax.random.fold_in(jax.random.fold_in(key_list[8], part), 71), part),
        "kernel": gaussian(part_keys[1], (GRID_X, GRID_Y, 9, 2, PANELS_T, PANELS_T), (18 * PANELS_T) ** -0.5, 0.125, ((0, 8), (1, 2))),
        "offsets": jnp.clip(1.0 * jax.random.uniform(part_keys[2], (GRID_X, GRID_Y, 2, PANELS_T), jnp.float32) ** level_of(part_keys[2], (GRID_X, GRID_Y, 2, PANELS_T), ((0, 8), (1, 2)), -0.2, 0.2), 0.0, 1.0),
        "neighbor": jax.vmap(lambda own: jax.random.permutation(own, 9))(jax.random.split(part_keys[3], GRID_X * GRID_Y)).reshape((GRID_X, GRID_Y, 9)).astype(jnp.int32),
        "frequency": jax.random.permutation(part_keys[4], FREQUENCIES).astype(jnp.int32),
        "lattice_x": jax.random.permutation(key_list[5], MODES_X).astype(jnp.int32),
        "lattice_y": jax.random.permutation(key_list[6], MODES_Y).astype(jnp.int32),
        "spectral_weight": jnp.clip(jnp.exp(jax.random.uniform(key_list[7], (FREQUENCIES, MODES_X, MODES_Y), jnp.float32, math.log(0.1), math.log(3.0))), 0.1, 3.0),
    }


two_pi = 2.0 * math.pi
eps_norm = 1e-06

def phase_table(position, harmonic):
    phase_angle = two_pi * (position[:, None] * harmonic[None, :])
    return (jnp.cos(phase_angle).astype(jnp.bfloat16), jnp.sin(phase_angle).astype(jnp.bfloat16))

def project_rows(cosine_cols, sine_cols, twisted):
    row_count = cosine_cols.shape[1]
    stacked = jnp.concatenate([cosine_cols, sine_cols], 1)
    gram_matrix = lax.dot_general(stacked, twisted, (((0,), (0,)), ((), ())), preferred_element_type=jnp.float32)
    gram_matrix = gram_matrix.reshape(2, row_count, 2, -1)
    coef_real = gram_matrix[0, :, 0] + gram_matrix[1, :, 1]
    coef_imag = gram_matrix[0, :, 1] - gram_matrix[1, :, 0]
    return jnp.stack([coef_real, coef_imag], 1)

def expand_rows(cosine_cols, sine_cols, scaled):
    row_count = scaled.shape[0]
    upper_rows = scaled.reshape(row_count, -1)
    lower_rows = jnp.stack([-scaled[:, 1], scaled[:, 0]], 1).reshape(row_count, -1)
    matrix = jnp.concatenate([upper_rows, lower_rows], 0)
    stacked = jnp.concatenate([cosine_cols, sine_cols], 1)
    return jnp.dot(stacked, matrix, preferred_element_type=jnp.float32)

def twist_density(panel_density, cosine_y, sine_y):
    density_real = panel_density[:, 0, :, None].astype(jnp.float32)
    density_imag = panel_density[:, 1, :, None].astype(jnp.float32)
    wave_cos = cosine_y.astype(jnp.float32)[:, None, :]
    wave_sin = sine_y.astype(jnp.float32)[:, None, :]
    part_real = wave_cos * density_real + wave_sin * density_imag
    part_imag = wave_cos * density_imag - wave_sin * density_real
    return jnp.stack([part_real, part_imag], 1).reshape(panel_density.shape[0], -1).astype(jnp.bfloat16)

def finish(summed, cosine_y, sine_y, vectors):
    shaped = summed.reshape(summed.shape[0], 2, vectors, -1)
    wave_cos = cosine_y.astype(jnp.float32)[:, None, :]
    wave_sin = sine_y.astype(jnp.float32)[:, None, :]
    far_real = lax.optimization_barrier(jnp.sum(shaped[:, 0] * wave_cos - shaped[:, 1] * wave_sin, -1))
    far_imag = lax.optimization_barrier(jnp.sum(shaped[:, 0] * wave_sin + shaped[:, 1] * wave_cos, -1))
    return jnp.stack([far_real, far_imag], 1)

def combine_near(product, vectors):
    first_half = product[:, 0]
    second = product[:, 1]
    near_real = first_half[:, :vectors] - second[:, vectors:]
    near_imag = second[:, :vectors] + first_half[:, vectors:]
    return jnp.stack([near_real, near_imag], 1)

def panel_sum(values):
    return lax.optimization_barrier(jnp.sum(values, axis=(0, 1, 3)))

def reference(residual, kernel, offsets, neighbor, frequency, lattice_x, lattice_y, spectral_weight):
    column = jnp.arange(GRID_X, dtype=jnp.float32)
    row_index = jnp.arange(GRID_Y, dtype=jnp.float32)
    position_x = ((column[:, None, None] + offsets[:, :, 0, :]) / GRID_X).reshape(-1)
    position_y = ((row_index[None, :, None] + offsets[:, :, 1, :]) / GRID_Y).reshape(-1)
    harmonic_x = (lattice_x - MODES_X // 2).astype(jnp.float32)
    harmonic_y = (lattice_y - MODES_Y // 2).astype(jnp.float32)
    cosine_x, sine_x = phase_table(position_x, harmonic_x)
    cosine_y, sine_y = phase_table(position_y, harmonic_y)
    weight_rows = jnp.take(spectral_weight, frequency[:VECTORS].astype(jnp.int32), axis=0)
    factor = weight_rows * (1.0 / math.sqrt(MODES_X * MODES_Y * PANELS))
    factor_wide = jnp.transpose(factor, (1, 0, 2)).reshape(MODES_X, VECTORS * MODES_Y)[:, None, :]

    def near_field(density):
        candidates = []
        for slot_index in range(9):
            shift_x = slot_index // 3 - 1
            shift_y = slot_index % 3 - 1
            candidates.append(jnp.roll(density, (-shift_x, -shift_y), axis=(0, 1)))
        stacked = jnp.stack(candidates, 2).reshape(GRID_X * GRID_Y, 9, -1)
        picked = jnp.take_along_axis(stacked, neighbor.reshape(GRID_X * GRID_Y, 9, 1), axis=1)
        picked = picked.reshape(GRID_X * GRID_Y, 9, 2 * VECTORS, PANELS_T)
        blocks = kernel.reshape(GRID_X * GRID_Y, 9, 2, PANELS_T, PANELS_T)
        product = jnp.einsum('tjmp,tjcpq->tcmq', picked.astype(jnp.float32), blocks.astype(jnp.float32))
        return combine_near(product, VECTORS).reshape(GRID_X, GRID_Y, 2, VECTORS, PANELS_T)

    def far_field(density):
        panel_density = jnp.transpose(density, (0, 1, 4, 2, 3)).reshape(PANELS, 2, VECTORS)
        twisted = twist_density(panel_density, cosine_y, sine_y)
        coeffs = project_rows(cosine_x, sine_x, twisted)
        scaled = (coeffs * factor_wide).astype(jnp.bfloat16)
        summed = expand_rows(cosine_x, sine_x, scaled)
        far_panel = finish(summed, cosine_y, sine_y, VECTORS)
        return far_panel.reshape(GRID_X, GRID_Y, PANELS_T, 2, VECTORS).transpose(0, 1, 3, 4, 2)

    def apply_operator(density):
        return 0.5 * density.astype(jnp.float32) + near_field(density) + far_field(density)
    squares = panel_sum(residual[:, :, 0] * residual[:, :, 0] + residual[:, :, 1] * residual[:, :, 1])
    basis_scale = jnp.sqrt(squares / PANELS + eps_norm)
    basis_one = (residual / basis_scale[None, None, None, :, None]).astype(jnp.bfloat16)
    image_one = apply_operator(basis_one)
    basis_real = basis_one[:, :, 0].astype(jnp.float32)
    basis_imag = basis_one[:, :, 1].astype(jnp.float32)
    image_real = image_one[:, :, 0]
    image_imag = image_one[:, :, 1]
    coef_real = panel_sum(basis_real * image_real + basis_imag * image_imag) / PANELS
    coef_imag = panel_sum(basis_real * image_imag - basis_imag * image_real) / PANELS
    wide_real = coef_real[None, None, :, None]
    wide_imag = coef_imag[None, None, :, None]
    update_real = image_real - (wide_real * basis_real - wide_imag * basis_imag)
    update_imag = image_imag - (wide_real * basis_imag + wide_imag * basis_real)
    update_sq = panel_sum(update_real * update_real + update_imag * update_imag)
    update_scale = jnp.sqrt(update_sq / PANELS + eps_norm)
    next_basis = (jnp.stack([update_real, update_imag], 2) / update_scale[None, None, None, :, None]).astype(jnp.bfloat16)
    image_two = apply_operator(next_basis)
    arnoldi = jnp.stack([basis_scale, coef_real, coef_imag, update_scale])
    return (image_two, arnoldi)
```

```python
import math

import jax
import jax.numpy as jnp
from jax import lax
from jax.experimental import pallas as pl
from jax.experimental.pallas import tpu as pltpu
from jax.sharding import PartitionSpec as P

eps_norm = 1e-06
f32 = jnp.float32
bf16 = jnp.bfloat16
lanes = 128
vmem_bytes = 56 * 1024 * 1024

sine_terms = (6.283185160087918, -10.3354137577709, 5.100062753380459, -1.1960903419427114, 0.1544402466966843)
cosine_terms = (0.9999999534659573, -4.93479285858416, 4.058411912342187, -1.331880149557601, 0.21969677520430975)


def horner(terms, value):
    total = jnp.full_like(value, terms[-1])
    for term in terms[-2::-1]:
        total = total * value + term
    return total


def cos_sin(turns):
    turn = turns - jnp.round(turns)
    square = turn * turn
    double = turn * horner(sine_terms, square)
    return 1.0 - 0.5 * (double * double), double * horner(cosine_terms, square)


class Layout:
    def __init__(self, strips, tiles_y, vectors, modes):
        self.strips, self.tiles_y, self.vectors = strips, tiles_y, vectors
        self.tiles = strips * tiles_y
        self.columns, self.waves = lax.axis_size("tile"), lax.axis_size("wave")
        self.devices = self.columns * self.waves
        self.count_x, self.count_y = self.columns * strips, self.waves * tiles_y
        self.panels = self.count_x * self.count_y * lanes
        self.local = self.tiles * lanes
        self.rows = self.tiles * 2 * vectors
        self.offset_rows = -(-6 * self.tiles // 16) * 16
        self.half = modes // 2
        self.quarter = modes // 4
        chip_bits = (self.columns - 1).bit_length()
        wave_bits = (self.waves - 1).bit_length()
        assert self.columns == 1 << chip_bits and self.waves == 1 << wave_bits
        other = 1 if wave_bits else 0
        self.chip_masks = [(1 << b) * self.waves + other for b in reversed(range(chip_bits))]
        self.masks = self.chip_masks + [1 << b for b in reversed(range(wave_bits))]
        self.wave_bits = wave_bits
        self.phase_row = 2 * self.quarter + 5

    def me(self):
        return lax.axis_index("tile") * self.waves + lax.axis_index("wave")

    def device_of(self, block):
        device = self.me()
        for k, mask in enumerate(self.masks):
            device = device ^ (((block >> k) & 1) * mask)
        return device

    def block_of(self, device):
        rest = device ^ self.me()
        block = 0
        for k, mask in enumerate(self.chip_masks):
            bit = (rest >> (mask.bit_length() - 1)) & 1
            block = block | (bit << k)
            rest = rest ^ (bit * mask)
        for b in range(self.wave_bits):
            bit = (rest >> (self.wave_bits - 1 - b)) & 1
            block = block | (bit << (len(self.chip_masks) + b))
        return block


def gather_blocks(array, layout):
    array = array[None]
    for mask in layout.masks:
        pairs = [(i, i ^ mask) for i in range(layout.devices)]
        array = jnp.concatenate([array, lax.ppermute(array, ("tile", "wave"), pairs)])
    return array


def pack_kernel(layout, residual, offsets, out):
    rows = layout.rows
    out[:rows, :] = residual[...].astype(bf16)
    value = offsets[...]
    first = value.astype(bf16)
    value = value - first.astype(f32)
    second = value.astype(bf16)
    third = (value - second.astype(f32)).astype(bf16)
    pieces = [first.astype(f32), second.astype(f32), third.astype(f32)]
    pad = layout.offset_rows - 6 * layout.tiles
    if pad:
        pieces.append(jnp.zeros((pad, lanes), f32))
    out[rows:, :] = jnp.concatenate(pieces, 0).astype(bf16)


def split_dot(weights, value, dims):
    total = 0.0
    for _ in range(3):
        part = value.astype(bf16)
        total = total + lax.dot_general(weights, part, dims, preferred_element_type=f32)
        value = value - part.astype(f32)
    return total


def spectral_kernel(layout, scale, frequency, lattice_x, lattice_y, weight, out, guess):
    size = 2 * layout.half
    spot = lax.broadcasted_iota(jnp.int32, (size, size), 0)
    wanted = jnp.where(spot < layout.half, spot + layout.half, size - 1 - spot)
    pick_x = jnp.where(wanted == lattice_x[...], 1.0, 0.0).astype(bf16)
    pick_y = jnp.where(wanted == lattice_y[...], 1.0, 0.0).astype(bf16)
    rows = []
    for v in range(layout.vectors):
        table = weight[frequency[v]] * scale
        moved = split_dot(pick_x, table, (((1,), (0,)), ((), ())))
        moved = split_dot(pick_y, moved, (((1,), (1,)), ((), ())))
        out[v] = moved
        mean = jnp.sum(jnp.sum(moved, 0, keepdims=True), 1, keepdims=True)
        rows.append(jnp.broadcast_to(0.5 + mean, (1, lanes)))
    guess[...] = jnp.concatenate(rows + rows, 0)


def make_tables(layout, block, offsets_of, table_x, table_y):
    tiles, half, quarter = layout.tiles, layout.half, layout.quarter
    device = layout.device_of(block)
    column, row_index = device // layout.waves, device % layout.waves
    pieces = offsets_of(block)
    offset = pieces[: 2 * tiles] + pieces[2 * tiles : 4 * tiles] + pieces[4 * tiles : 6 * tiles]
    eight = lax.broadcasted_iota(jnp.int32, (8, lanes), 0).astype(f32)
    coarse_y = jnp.where(eight < 4, quarter / 2 + 0.5 + 8 * eight, jnp.where(eight < 5, quarter / 2.0, 0.5))
    for i in range(tiles):
        g = (column * layout.strips + i // layout.tiles_y).astype(f32)
        h = (row_index * layout.tiles_y + i % layout.tiles_y).astype(f32)
        x = jnp.broadcast_to((offset[2 * i : 2 * i + 1] + g) * (1.0 / layout.count_x), (8, lanes))
        y = jnp.broadcast_to((offset[2 * i + 1 : 2 * i + 2] + h) * (1.0 / layout.count_y), (8, lanes))
        fine_xc, fine_xs = cos_sin(eight * x)
        big_xc, big_xs = cos_sin((8 * eight + 0.5) * x)
        fine_yc, fine_ys = cos_sin(eight * y)
        big_yc, big_ys = cos_sin(coarse_y * y + jnp.where(eight == 5, 0.5, 0.0) * x)
        shift_c, shift_s = big_yc[4:5], big_ys[4:5]
        span = slice(i * lanes, (i + 1) * lanes)
        for e, sign in ((0, 1.0), (1, -1.0)):
            both_c = big_xc * shift_c - sign * (big_xs * shift_s)
            both_s = big_xs * shift_c + sign * (big_xc * shift_s)
            cosines, sines = [], []
            for a in range(half // 8):
                c, s = both_c[a : a + 1], both_s[a : a + 1]
                cosines.append(c * fine_xc - s * fine_xs)
                sines.append(s * fine_xc + c * fine_xs)
            table_x[block, 2 * half * e : 2 * half * (e + 1), span] = jnp.concatenate(cosines + sines, 0).astype(bf16)
        cosines, sines = [], []
        for a in range(quarter // 8):
            c, s = big_yc[a : a + 1], big_ys[a : a + 1]
            cosines.append(c * fine_yc - s * fine_ys)
            sines.append(s * fine_yc + c * fine_ys)
        last = jnp.concatenate([big_yc[5:6], big_ys[5:6], jnp.zeros((6, lanes), f32)], 0)
        table_y[block, :, span] = jnp.concatenate(cosines + sines + [last], 0)


def twist(layout, block, density, table_y, out):
    vectors, group = layout.vectors, 2 * layout.quarter
    for i in range(layout.tiles):
        span = slice(i * lanes, (i + 1) * lanes)
        values = density[block, i * 2 * vectors : (i + 1) * 2 * vectors, :].astype(f32)
        waves = table_y[block, :group, span]
        c, s = table_y[block, group : group + 1, span], table_y[block, group + 1 : group + 2, span]
        real, imag = values[:vectors], values[vectors:]
        turned = (real * c - imag * s, imag * c + real * s)
        for part in range(2):
            for v in range(vectors):
                start = (part * vectors + v) * group
                out[start : start + group, span] = (turned[part][v : v + 1] * waves).astype(bf16)


def project(layout, density, table_x, table_y, twisted, total, before):
    def step(block, carry):
        before(block)
        twist(layout, block, density, table_y, twisted)
        product = lax.dot_general(
            twisted[...], table_x[block], (((1,), (1,)), ((), ())), preferred_element_type=f32
        )
        total[...] += product
        return carry

    total[...] = jnp.zeros_like(total)
    lax.fori_loop(0, layout.devices, step, 0)


def swap(value):
    return pltpu.roll(value, lanes // 2, 1)


def weigh(layout, total, weight, scaled):
    vectors, quarter = layout.vectors, layout.quarter
    low = lax.broadcasted_iota(jnp.int32, (quarter, lanes), 1) < layout.half
    sign = jnp.where(low, -1.0, 1.0)
    for v in range(vectors):
        table = weight[v]
        part = [table[k * quarter : (k + 1) * quarter] for k in range(4)]
        choices = ((part[1], part[3]), (part[2], part[0]), (part[0], part[2]), (part[3], part[1]))
        for e in range(2):
            span = slice(e * lanes, (e + 1) * lanes)
            real = v * 2 * quarter
            imag = (vectors + v) * 2 * quarter
            cos_r = total[real : real + quarter, span]
            sin_r = swap(total[real + quarter : real + 2 * quarter, span]) * sign
            cos_i = total[imag : imag + quarter, span]
            sin_i = swap(total[imag + quarter : imag + 2 * quarter, span]) * sign
            out = []
            for k, (mr, mi) in enumerate(((cos_r + sin_r, cos_i + sin_i), (cos_r - sin_r, cos_i - sin_i))):
                chosen = jnp.where(low, *choices[2 * e + k])
                turned = swap(chosen)
                plus, minus = chosen + turned, chosen - turned
                out.append((plus * mr + minus * swap(mi), plus * mi - minus * swap(mr)))
            for start, k in ((real, 0), (imag, 1)):
                scaled[start : start + quarter, span] = (out[0][k] + out[1][k]).astype(bf16)
                scaled[start + quarter : start + 2 * quarter, span] = swap(sign * (out[0][k] - out[1][k])).astype(bf16)


def expand(layout, scaled, table_x, table_y, summed):
    vectors, group = layout.vectors, 2 * layout.quarter
    summed[...] = jnp.dot(scaled[...], table_x[0], preferred_element_type=f32)
    result = []
    for i in range(layout.tiles):
        span = slice(i * lanes, (i + 1) * lanes)
        waves = table_y[0, :group, span]
        rows = []
        for k in range(2 * vectors):
            rows.append(jnp.sum(summed[k * group : (k + 1) * group, span] * waves, 0, keepdims=True))
        real, imag = jnp.concatenate(rows[:vectors], 0), jnp.concatenate(rows[vectors:], 0)
        c, s = table_y[0, group : group + 1, span], table_y[0, group + 1 : group + 2, span]
        result.append(jnp.concatenate([real * c + imag * s, imag * c - real * s], 0))
    return result


def near(layout, i, neighbor, density, kernel):
    vectors = layout.vectors
    g = lax.axis_index("tile") * layout.strips + i // layout.tiles_y
    h = lax.axis_index("wave") * layout.tiles_y + i % layout.tiles_y
    by_real, by_imag = 0.0, 0.0
    for j in range(9):
        slot = neighbor[i, j]
        step_x = lax.div(slot, 3)
        gx = lax.rem(g + step_x - 1 + layout.count_x, layout.count_x)
        hy = lax.rem(h + slot - 3 * step_x - 1 + layout.count_y, layout.count_y)
        block = layout.block_of(lax.div(gx, layout.strips) * layout.waves + lax.div(hy, layout.tiles_y))
        tile = lax.rem(gx, layout.strips) * layout.tiles_y + lax.rem(hy, layout.tiles_y)
        start = pl.multiple_of(tile * 2 * vectors, 2 * vectors)
        values = density[block, pl.ds(start, 2 * vectors), :]
        by_real += jnp.dot(values, kernel[i, j, 0], preferred_element_type=f32)
        by_imag += jnp.dot(values, kernel[i, j, 1], preferred_element_type=f32)
    return jnp.concatenate(
        [by_real[:vectors] - by_imag[vectors:], by_imag[:vectors] + by_real[vectors:]], 0
    )


def first_kernel(layout, neighbor, density, kernel, weight, guess, basis, image, table_x, table_y, twisted, total, scaled, summed):
    rows, tall = layout.rows, 2 * layout.vectors

    def tables(block):
        make_tables(layout, block, lambda b: density[b, rows:, :].astype(f32), table_x, table_y)

    project(layout, density, table_x, table_y, twisted, total, tables)
    weigh(layout, total, weight, scaled)
    far = expand(layout, scaled, table_x, table_y, summed)
    for i in range(layout.tiles):
        span = slice(i * tall, (i + 1) * tall)
        own = density[0, span, :].astype(f32)
        value = 0.5 * own + near(layout, i, neighbor, density, kernel) + far[i]
        image[span, :] = value
        basis[span, :] = (value - guess[...] * own).astype(bf16)


def second_kernel(layout, neighbor, density, start, kernel, weight, guess, image, table_x, table_y, result, scalars, twisted, total, scaled, summed):
    vectors, tall, tiles = layout.vectors, 2 * layout.vectors, layout.tiles
    project(layout, density, table_x, table_y, twisted, total, lambda block: None)
    weigh(layout, total, weight, scaled)
    far = expand(layout, scaled, table_x, table_y, summed)

    def pieces(device):
        block = layout.block_of(device)
        for i in range(tiles):
            r = start[block, i * tall : (i + 1) * tall, :].astype(f32)
            z = density[block, i * tall : (i + 1) * tall, :].astype(f32)
            yield r[:vectors], r[vectors:], z[:vectors], z[vectors:]

    def products(device, sums):
        squares, real, imag = sums
        for rr, ri, zr, zi in pieces(device):
            squares = squares + rr * rr + ri * ri
            real = real + rr * zr + ri * zi
            imag = imag + rr * zi - ri * zr
        return squares, real, imag

    zero = jnp.zeros((vectors, lanes), f32)
    sums = lax.fori_loop(0, layout.devices, products, (zero, zero, zero))
    squares, real, imag = [jnp.sum(s, 1, keepdims=True) * (1.0 / layout.panels) for s in sums]
    scale_sq = squares + eps_norm
    hint = guess[:vectors, :1]
    more_real = (real - hint * eps_norm) / scale_sq
    more_imag = imag / scale_sq
    wide_real = jnp.broadcast_to(more_real, (vectors, lanes))
    wide_imag = jnp.broadcast_to(more_imag, (vectors, lanes))

    def lengths(device, total_sq):
        for rr, ri, zr, zi in pieces(device):
            ur = zr - (wide_real * rr - wide_imag * ri)
            ui = zi - (wide_real * ri + wide_imag * rr)
            total_sq = total_sq + ur * ur + ui * ui
        return total_sq

    update_sq = jnp.sum(lax.fori_loop(0, layout.devices, lengths, zero), 1, keepdims=True)
    scale = jnp.sqrt(scale_sq)
    update_scale = jnp.sqrt(update_sq * (1.0 / layout.panels) / scale_sq + eps_norm)
    inverse = jnp.broadcast_to(1.0 / (scale * update_scale), (vectors, lanes))
    spot = lax.broadcasted_iota(jnp.int32, (vectors, lanes), 0)
    lane = lax.broadcasted_iota(jnp.int32, (vectors, lanes), 1)
    rows = [
        jnp.sum(jnp.where(spot == lane, jnp.broadcast_to(value, (vectors, lanes)), 0.0), 0, keepdims=True)
        for value in (scale, hint + more_real, more_imag, update_scale)
    ]
    scalars[...] = jnp.concatenate(rows, 0)[:, :vectors]
    for i in range(tiles):
        first = i * tall
        own = density[0, first : first + tall, :].astype(f32)
        value = 0.5 * own + near(layout, i, neighbor, density, kernel) + far[i]
        wr, wi = image[first : first + vectors, :], image[first + vectors : first + tall, :]
        result[first : first + vectors, :] = (value[:vectors] - (wide_real * wr - wide_imag * wi)) * inverse
        result[first + vectors : first + tall, :] = (value[vectors:] - (wide_real * wi + wide_imag * wr)) * inverse


def per_device(residual, kernel, offsets, neighbor, frequency, lattice_x, lattice_y, spectral_weight):
    strips, tiles_y, _, vectors, _ = residual.shape
    modes_x, modes_y = spectral_weight.shape[1:]
    layout = Layout(strips, tiles_y, vectors, modes_x)
    tiles, rows, devices = layout.tiles, layout.rows, layout.devices
    vmem, smem = pl.BlockSpec(memory_space=pltpu.VMEM), pl.BlockSpec(memory_space=pltpu.SMEM)
    shape = jax.ShapeDtypeStruct
    params = pltpu.CompilerParams(vmem_limit_bytes=vmem_bytes)

    def call(body, name, out_shape, in_specs, scratch=()):
        return pl.pallas_call(
            body,
            out_shape=out_shape,
            in_specs=in_specs,
            out_specs=jax.tree.map(lambda _: vmem, out_shape),
            scratch_shapes=scratch,
            compiler_params=params,
            name=name,
        )

    packed = call(
        lambda *refs: pack_kernel(layout, *refs),
        "pack",
        shape((rows + layout.offset_rows, lanes), bf16),
        [vmem, vmem],
    )(residual.reshape(rows, lanes), offsets.reshape(2 * tiles, lanes))
    scale = 1.0 / math.sqrt(modes_x * modes_y * layout.panels)
    weight, guess = call(
        lambda *refs: spectral_kernel(layout, scale, *refs),
        "spectral",
        (shape((vectors, modes_y, modes_x), f32), shape((2 * vectors, lanes), f32)),
        [smem, vmem, vmem, vmem],
    )(frequency, lattice_x.reshape(1, -1), lattice_y.reshape(1, -1), spectral_weight)
    blocks = kernel.reshape(tiles, 9, 2, lanes, lanes)
    neighbor = neighbor.reshape(tiles, 9)
    tall = 2 * vectors * 2 * layout.quarter
    wide = 4 * layout.half
    scratch = [
        pltpu.VMEM((tall, layout.local), bf16),
        pltpu.VMEM((tall, wide), f32),
        pltpu.VMEM((tall, wide), bf16),
        pltpu.VMEM((tall, layout.local), f32),
    ]
    gathered = gather_blocks(packed, layout)
    basis, image, table_x, table_y = call(
        lambda *refs: first_kernel(layout, *refs),
        "first",
        (
            shape((rows, lanes), bf16),
            shape((rows, lanes), f32),
            shape((devices, wide, layout.local), bf16),
            shape((devices, 2 * layout.quarter + 8, layout.local), f32),
        ),
        [smem, vmem, vmem, vmem, vmem],
        scratch,
    )(neighbor, gathered, blocks, weight, guess)
    second = gather_blocks(basis, layout)
    result, scalars = call(
        lambda *refs: second_kernel(layout, *refs),
        "second",
        (shape((rows, lanes), f32), shape((4, vectors), f32)),
        [smem] + [vmem] * 8,
        scratch,
    )(neighbor, second, gathered, blocks, weight, guess, image, table_x, table_y)
    return result.reshape(residual.shape), scalars


def solution(mesh):
    return jax.shard_map(
        per_device,
        mesh=mesh,
        in_specs=(
            P(("grp", "tile"), "wave", None, None, None),
            P(("grp", "tile"), "wave", None, None, None, None),
            P(("grp", "tile"), "wave", None, None),
            P(("grp", "tile"), "wave", None),
            P("grp"),
            P(),
            P(),
            P(),
        ),
        out_specs=(P(("grp", "tile"), "wave", None, None, None), P("grp", None)),
        check_vma=False,
    )
```

```python
import math

import jax
import jax.numpy as jnp
from jax import lax
from jax.experimental import pallas as pl
from jax.experimental.pallas import tpu as pltpu
from jax.sharding import PartitionSpec as P

eps_norm = 1e-06
f32 = jnp.float32
bf16 = jnp.bfloat16
lanes = 128
mib = 1024 * 1024

sine_terms = (6.283185160087918, -10.3354137577709, 5.100062753380459, -1.1960903419427114, 0.1544402466966843)
cosine_terms = (0.9999999534659573, -4.93479285858416, 4.058411912342187, -1.331880149557601, 0.21969677520430975)


def horner(terms, value):
    total = jnp.full_like(value, terms[-1])
    for term in terms[-2::-1]:
        total = total * value + term
    return total


def cos_sin(turns):
    turn = turns - jnp.round(turns)
    square = turn * turn
    double = turn * horner(sine_terms, square)
    return 1.0 - 0.5 * (double * double), double * horner(cosine_terms, square)


class Layout:
    def __init__(self, strips, tiles_y, vectors, modes):
        self.strips, self.tiles_y, self.vectors = strips, tiles_y, vectors
        self.tiles = strips * tiles_y
        self.columns, self.waves = lax.axis_size("tile"), lax.axis_size("wave")
        self.devices = self.columns * self.waves
        self.count_x, self.count_y = self.columns * strips, self.waves * tiles_y
        self.panels = self.count_x * self.count_y * lanes
        self.local = self.tiles * lanes
        self.rows = self.tiles * 2 * vectors
        self.offset_rows = -(-6 * self.tiles // 16) * 16
        self.half = modes // 2
        self.quarter = modes // 4
        chip_bits = (self.columns - 1).bit_length()
        wave_bits = (self.waves - 1).bit_length()
        assert self.columns == 1 << chip_bits and self.waves == 1 << wave_bits
        other = 1 if wave_bits else 0
        self.chip_masks = [(1 << b) * self.waves + other for b in reversed(range(chip_bits))]
        self.masks = self.chip_masks + [1 << b for b in reversed(range(wave_bits))]
        self.wave_bits = wave_bits
        self.phase_row = 2 * self.quarter + 5

    def me(self):
        return lax.axis_index("tile") * self.waves + lax.axis_index("wave")

    def device_of(self, block):
        device = self.me()
        for k, mask in enumerate(self.masks):
            device = device ^ (((block >> k) & 1) * mask)
        return device

    def block_of(self, device):
        rest = device ^ self.me()
        block = 0
        for k, mask in enumerate(self.chip_masks):
            bit = (rest >> (mask.bit_length() - 1)) & 1
            block = block | (bit << k)
            rest = rest ^ (bit * mask)
        for b in range(self.wave_bits):
            bit = (rest >> (self.wave_bits - 1 - b)) & 1
            block = block | (bit << (len(self.chip_masks) + b))
        return block


def gather_blocks(array, layout):
    array = array[None]
    for mask in layout.masks:
        pairs = [(i, i ^ mask) for i in range(layout.devices)]
        array = jnp.concatenate([array, lax.ppermute(array, ("tile", "wave"), pairs)])
    return array


def pack_kernel(layout, residual, offsets, out):
    rows = layout.rows
    out[:rows, :] = residual[...].astype(bf16)
    value = offsets[...]
    first = value.astype(bf16)
    value = value - first.astype(f32)
    second = value.astype(bf16)
    third = (value - second.astype(f32)).astype(bf16)
    pieces = [first.astype(f32), second.astype(f32), third.astype(f32)]
    pad = layout.offset_rows - 6 * layout.tiles
    if pad:
        pieces.append(jnp.zeros((pad, lanes), f32))
    out[rows:, :] = jnp.concatenate(pieces, 0).astype(bf16)


def split_dot(weights, value, dims):
    total = 0.0
    for _ in range(3):
        part = value.astype(bf16)
        total = total + lax.dot_general(weights, part, dims, preferred_element_type=f32)
        value = value - part.astype(f32)
    return total


def spectral_kernel(layout, scale, frequency, lattice_x, lattice_y, weight, out, guess):
    size = 2 * layout.half
    spot = lax.broadcasted_iota(jnp.int32, (size, size), 0)
    wanted = jnp.where(spot < layout.half, spot + layout.half, size - 1 - spot)
    pick_x = jnp.where(wanted == lattice_x[...], 1.0, 0.0).astype(bf16)
    pick_y = jnp.where(wanted == lattice_y[...], 1.0, 0.0).astype(bf16)
    rows = []
    for v in range(layout.vectors):
        table = weight[frequency[v]] * scale
        moved = split_dot(pick_x, table, (((1,), (0,)), ((), ())))
        moved = split_dot(pick_y, moved, (((1,), (1,)), ((), ())))
        out[v] = moved
        mean = jnp.sum(jnp.sum(moved, 0, keepdims=True), 1, keepdims=True)
        rows.append(jnp.broadcast_to(0.5 + mean, (1, lanes)))
    guess[...] = jnp.concatenate(rows + rows, 0)


def make_tables(layout, block, offsets_of, table_x, table_y):
    tiles, half, quarter = layout.tiles, layout.half, layout.quarter
    device = layout.device_of(block)
    column, row_index = device // layout.waves, device % layout.waves
    pieces = offsets_of(block)
    offset = pieces[: 2 * tiles] + pieces[2 * tiles : 4 * tiles] + pieces[4 * tiles : 6 * tiles]
    eight = lax.broadcasted_iota(jnp.int32, (8, lanes), 0).astype(f32)
    coarse_y = jnp.where(eight < 4, quarter / 2 + 0.5 + 8 * eight, jnp.where(eight < 5, quarter / 2.0, 0.5))
    for i in range(tiles):
        g = (column * layout.strips + i // layout.tiles_y).astype(f32)
        h = (row_index * layout.tiles_y + i % layout.tiles_y).astype(f32)
        x = jnp.broadcast_to((offset[2 * i : 2 * i + 1] + g) * (1.0 / layout.count_x), (8, lanes))
        y = jnp.broadcast_to((offset[2 * i + 1 : 2 * i + 2] + h) * (1.0 / layout.count_y), (8, lanes))
        fine_xc, fine_xs = cos_sin(eight * x)
        big_xc, big_xs = cos_sin((8 * eight + 0.5) * x)
        fine_yc, fine_ys = cos_sin(eight * y)
        big_yc, big_ys = cos_sin(coarse_y * y + jnp.where(eight == 5, 0.5, 0.0) * x)
        shift_c, shift_s = big_yc[4:5], big_ys[4:5]
        span = slice(i * lanes, (i + 1) * lanes)
        for e, sign in ((0, 1.0), (1, -1.0)):
            both_c = big_xc * shift_c - sign * (big_xs * shift_s)
            both_s = big_xs * shift_c + sign * (big_xc * shift_s)
            cosines, sines = [], []
            for a in range(half // 8):
                c, s = both_c[a : a + 1], both_s[a : a + 1]
                cosines.append(c * fine_xc - s * fine_xs)
                sines.append(s * fine_xc + c * fine_xs)
            table_x[block, 2 * half * e : 2 * half * (e + 1), span] = jnp.concatenate(cosines + sines, 0).astype(bf16)
        cosines, sines = [], []
        for a in range(quarter // 8):
            c, s = big_yc[a : a + 1], big_ys[a : a + 1]
            cosines.append(c * fine_yc - s * fine_ys)
            sines.append(s * fine_yc + c * fine_ys)
        last = jnp.concatenate([big_yc[5:6], big_ys[5:6], jnp.zeros((6, lanes), f32)], 0)
        table_y[block, :, span] = jnp.concatenate(cosines + sines + [last], 0)


def twist(layout, block, density, table_y, out):
    vectors, group = layout.vectors, 2 * layout.quarter
    for i in range(layout.tiles):
        span = slice(i * lanes, (i + 1) * lanes)
        values = density[block, i * 2 * vectors : (i + 1) * 2 * vectors, :].astype(f32)
        waves = table_y[block, :group, span]
        c, s = table_y[block, group : group + 1, span], table_y[block, group + 1 : group + 2, span]
        real, imag = values[:vectors], values[vectors:]
        turned = (real * c - imag * s, imag * c + real * s)
        for part in range(2):
            for v in range(vectors):
                start = (part * vectors + v) * group
                out[start : start + group, span] = (turned[part][v : v + 1] * waves).astype(bf16)


def project(layout, density, table_x, table_y, twisted, total, before):
    def step(block, carry):
        before(block)
        twist(layout, block, density, table_y, twisted)
        product = lax.dot_general(
            twisted[...], table_x[block], (((1,), (1,)), ((), ())), preferred_element_type=f32
        )
        total[...] += product
        return carry

    total[...] = jnp.zeros_like(total)
    lax.fori_loop(0, layout.devices, step, 0)


def swap(value):
    return pltpu.roll(value, lanes // 2, 1)


def weigh(layout, total, weight, scaled):
    vectors, quarter = layout.vectors, layout.quarter
    low = lax.broadcasted_iota(jnp.int32, (quarter, lanes), 1) < layout.half
    sign = jnp.where(low, -1.0, 1.0)
    for v in range(vectors):
        table = weight[v]
        part = [table[k * quarter : (k + 1) * quarter] for k in range(4)]
        choices = ((part[1], part[3]), (part[2], part[0]), (part[0], part[2]), (part[3], part[1]))
        for e in range(2):
            span = slice(e * lanes, (e + 1) * lanes)
            real = v * 2 * quarter
            imag = (vectors + v) * 2 * quarter
            cos_r = total[real : real + quarter, span]
            sin_r = swap(total[real + quarter : real + 2 * quarter, span]) * sign
            cos_i = total[imag : imag + quarter, span]
            sin_i = swap(total[imag + quarter : imag + 2 * quarter, span]) * sign
            out = []
            for k, (mr, mi) in enumerate(((cos_r + sin_r, cos_i + sin_i), (cos_r - sin_r, cos_i - sin_i))):
                chosen = jnp.where(low, *choices[2 * e + k])
                turned = swap(chosen)
                plus, minus = chosen + turned, chosen - turned
                out.append((plus * mr + minus * swap(mi), plus * mi - minus * swap(mr)))
            for start, k in ((real, 0), (imag, 1)):
                scaled[start : start + quarter, span] = (out[0][k] + out[1][k]).astype(bf16)
                scaled[start + quarter : start + 2 * quarter, span] = swap(sign * (out[0][k] - out[1][k])).astype(bf16)


def expand(layout, scaled, table_x, table_y, summed):
    vectors, group = layout.vectors, 2 * layout.quarter
    summed[...] = jnp.dot(scaled[...], table_x[0], preferred_element_type=f32)
    result = []
    for i in range(layout.tiles):
        span = slice(i * lanes, (i + 1) * lanes)
        waves = table_y[0, :group, span]
        rows = []
        for k in range(2 * vectors):
            rows.append(jnp.sum(summed[k * group : (k + 1) * group, span] * waves, 0, keepdims=True))
        real, imag = jnp.concatenate(rows[:vectors], 0), jnp.concatenate(rows[vectors:], 0)
        c, s = table_y[0, group : group + 1, span], table_y[0, group + 1 : group + 2, span]
        result.append(jnp.concatenate([real * c + imag * s, imag * c - real * s], 0))
    return result


def near(layout, i, neighbor, density, kernel):
    vectors = layout.vectors
    g = lax.axis_index("tile") * layout.strips + i // layout.tiles_y
    h = lax.axis_index("wave") * layout.tiles_y + i % layout.tiles_y
    by_real, by_imag = 0.0, 0.0
    for j in range(9):
        slot = neighbor[i, j]
        step_x = lax.div(slot, 3)
        gx = lax.rem(g + step_x - 1 + layout.count_x, layout.count_x)
        hy = lax.rem(h + slot - 3 * step_x - 1 + layout.count_y, layout.count_y)
        block = layout.block_of(lax.div(gx, layout.strips) * layout.waves + lax.div(hy, layout.tiles_y))
        tile = lax.rem(gx, layout.strips) * layout.tiles_y + lax.rem(hy, layout.tiles_y)
        start = pl.multiple_of(tile * 2 * vectors, 2 * vectors)
        values = density[block, pl.ds(start, 2 * vectors), :]
        by_real += jnp.dot(values, kernel[i, j, 0], preferred_element_type=f32)
        by_imag += jnp.dot(values, kernel[i, j, 1], preferred_element_type=f32)
    return jnp.concatenate(
        [by_real[:vectors] - by_imag[vectors:], by_imag[:vectors] + by_real[vectors:]], 0
    )


def first_kernel(layout, neighbor, density, kernel, weight, guess, basis, image, table_x, table_y, twisted, total, scaled, summed):
    rows, tall = layout.rows, 2 * layout.vectors

    def tables(block):
        make_tables(layout, block, lambda b: density[b, rows:, :].astype(f32), table_x, table_y)

    project(layout, density, table_x, table_y, twisted, total, tables)
    weigh(layout, total, weight, scaled)
    far = expand(layout, scaled, table_x, table_y, summed)
    for i in range(layout.tiles):
        span = slice(i * tall, (i + 1) * tall)
        own = density[0, span, :].astype(f32)
        value = 0.5 * own + near(layout, i, neighbor, density, kernel) + far[i]
        image[span, :] = value
        basis[span, :] = (value - guess[...] * own).astype(bf16)


def second_kernel(layout, neighbor, density, start, kernel, weight, guess, image, table_x, table_y, result, scalars, twisted, total, scaled, summed):
    vectors, tall, tiles = layout.vectors, 2 * layout.vectors, layout.tiles
    project(layout, density, table_x, table_y, twisted, total, lambda block: None)
    weigh(layout, total, weight, scaled)
    far = expand(layout, scaled, table_x, table_y, summed)

    def pieces(device):
        block = layout.block_of(device)
        for i in range(tiles):
            r = start[block, i * tall : (i + 1) * tall, :].astype(f32)
            z = density[block, i * tall : (i + 1) * tall, :].astype(f32)
            yield r[:vectors], r[vectors:], z[:vectors], z[vectors:]

    def products(device, sums):
        squares, real, imag = sums
        for rr, ri, zr, zi in pieces(device):
            squares = squares + rr * rr + ri * ri
            real = real + rr * zr + ri * zi
            imag = imag + rr * zi - ri * zr
        return squares, real, imag

    zero = jnp.zeros((vectors, lanes), f32)
    sums = lax.fori_loop(0, layout.devices, products, (zero, zero, zero))
    squares, real, imag = [jnp.sum(s, 1, keepdims=True) * (1.0 / layout.panels) for s in sums]
    scale_sq = squares + eps_norm
    hint = guess[:vectors, :1]
    more_real = (real - hint * eps_norm) / scale_sq
    more_imag = imag / scale_sq
    wide_real = jnp.broadcast_to(more_real, (vectors, lanes))
    wide_imag = jnp.broadcast_to(more_imag, (vectors, lanes))

    def lengths(device, total_sq):
        for rr, ri, zr, zi in pieces(device):
            ur = zr - (wide_real * rr - wide_imag * ri)
            ui = zi - (wide_real * ri + wide_imag * rr)
            total_sq = total_sq + ur * ur + ui * ui
        return total_sq

    update_sq = jnp.sum(lax.fori_loop(0, layout.devices, lengths, zero), 1, keepdims=True)
    scale = jnp.sqrt(scale_sq)
    update_scale = jnp.sqrt(update_sq * (1.0 / layout.panels) / scale_sq + eps_norm)
    inverse = jnp.broadcast_to(1.0 / (scale * update_scale), (vectors, lanes))
    spot = lax.broadcasted_iota(jnp.int32, (vectors, lanes), 0)
    lane = lax.broadcasted_iota(jnp.int32, (vectors, lanes), 1)
    rows = [
        jnp.sum(jnp.where(spot == lane, jnp.broadcast_to(value, (vectors, lanes)), 0.0), 0, keepdims=True)
        for value in (scale, hint + more_real, more_imag, update_scale)
    ]
    scalars[...] = jnp.concatenate(rows, 0)[:, :vectors]
    for i in range(tiles):
        first = i * tall
        own = density[0, first : first + tall, :].astype(f32)
        value = 0.5 * own + near(layout, i, neighbor, density, kernel) + far[i]
        wr, wi = image[first : first + vectors, :], image[first + vectors : first + tall, :]
        result[first : first + vectors, :] = (value[:vectors] - (wide_real * wr - wide_imag * wi)) * inverse
        result[first + vectors : first + tall, :] = (value[vectors:] - (wide_real * wi + wide_imag * wr)) * inverse


def per_device(residual, kernel, offsets, neighbor, frequency, lattice_x, lattice_y, spectral_weight):
    strips, tiles_y, _, vectors, _ = residual.shape
    modes_x, modes_y = spectral_weight.shape[1:]
    layout = Layout(strips, tiles_y, vectors, modes_x)
    tiles, rows, devices = layout.tiles, layout.rows, layout.devices
    vmem, smem = pl.BlockSpec(memory_space=pltpu.VMEM), pl.BlockSpec(memory_space=pltpu.SMEM)
    shape = jax.ShapeDtypeStruct

    def call(body, name, out_shape, in_specs, limit, scratch=()):
        return pl.pallas_call(
            body,
            out_shape=out_shape,
            in_specs=in_specs,
            out_specs=jax.tree.map(lambda _: vmem, out_shape),
            scratch_shapes=scratch,
            compiler_params=pltpu.CompilerParams(vmem_limit_bytes=limit),
            name=name,
        )

    packed = call(
        lambda *refs: pack_kernel(layout, *refs),
        "pack",
        shape((rows + layout.offset_rows, lanes), bf16),
        [vmem, vmem],
        mib,
    )(residual.reshape(rows, lanes), offsets.reshape(2 * tiles, lanes))
    scale = 1.0 / math.sqrt(modes_x * modes_y * layout.panels)
    weight, guess = call(
        lambda *refs: spectral_kernel(layout, scale, *refs),
        "spectral",
        (shape((vectors, modes_y, modes_x), f32), shape((2 * vectors, lanes), f32)),
        [smem, vmem, vmem, vmem],
        4 * mib,
    )(frequency, lattice_x.reshape(1, -1), lattice_y.reshape(1, -1), spectral_weight)
    blocks = kernel.reshape(tiles, 9, 2, lanes, lanes)
    neighbor = neighbor.reshape(tiles, 9)
    tall = 2 * vectors * 2 * layout.quarter
    wide = 4 * layout.half
    scratch = [
        pltpu.VMEM((tall, layout.local), bf16),
        pltpu.VMEM((tall, wide), f32),
        pltpu.VMEM((tall, wide), bf16),
        pltpu.VMEM((tall, layout.local), f32),
    ]
    limit = int(24 * mib)
    gathered = gather_blocks(packed, layout)
    basis, image, table_x, table_y = call(
        lambda *refs: first_kernel(layout, *refs),
        "first",
        (
            shape((rows, lanes), bf16),
            shape((rows, lanes), f32),
            shape((devices, wide, layout.local), bf16),
            shape((devices, 2 * layout.quarter + 8, layout.local), f32),
        ),
        [smem, vmem, vmem, vmem, vmem],
        limit,
        scratch,
    )(neighbor, gathered, blocks, weight, guess)
    second = gather_blocks(basis, layout)
    result, scalars = call(
        lambda *refs: second_kernel(layout, *refs),
        "second",
        (shape((rows, lanes), f32), shape((4, vectors), f32)),
        [smem] + [vmem] * 8,
        limit,
        scratch,
    )(neighbor, second, gathered, blocks, weight, guess, image, table_x, table_y)
    return result.reshape(residual.shape), scalars


def solution(mesh):
    return jax.shard_map(
        per_device,
        mesh=mesh,
        in_specs=(
            P(("grp", "tile"), "wave", None, None, None),
            P(("grp", "tile"), "wave", None, None, None, None),
            P(("grp", "tile"), "wave", None, None),
            P(("grp", "tile"), "wave", None),
            P("grp"),
            P(),
            P(),
            P(),
        ),
        out_specs=(P(("grp", "tile"), "wave", None, None, None), P("grp", None)),
        check_vma=False,
    )
```

```python
import math

import jax
import jax.numpy as jnp
from jax import lax
from jax.experimental import pallas as pl
from jax.experimental.pallas import tpu as pltpu
from jax.sharding import PartitionSpec as P

eps_norm = 1e-06
f32 = jnp.float32
bf16 = jnp.bfloat16
lanes = 128
mib = 1024 * 1024

sine_terms = (6.283185160087918, -10.3354137577709, 5.100062753380459, -1.1960903419427114, 0.1544402466966843)
cosine_terms = (0.9999999534659573, -4.93479285858416, 4.058411912342187, -1.331880149557601, 0.21969677520430975)


def horner(terms, value):
    total = jnp.full_like(value, terms[-1])
    for term in terms[-2::-1]:
        total = total * value + term
    return total


def cos_sin(turns):
    turn = turns - jnp.round(turns)
    square = turn * turn
    double = turn * horner(sine_terms, square)
    return 1.0 - 0.5 * (double * double), double * horner(cosine_terms, square)


class Layout:
    def __init__(self, strips, tiles_y, vectors, modes):
        self.strips, self.tiles_y, self.vectors = strips, tiles_y, vectors
        self.tiles = strips * tiles_y
        self.columns, self.waves = lax.axis_size("tile"), lax.axis_size("wave")
        self.devices = self.columns * self.waves
        self.count_x, self.count_y = self.columns * strips, self.waves * tiles_y
        self.panels = self.count_x * self.count_y * lanes
        self.local = self.tiles * lanes
        self.rows = self.tiles * 2 * vectors
        self.offset_rows = -(-6 * self.tiles // 16) * 16
        self.sum_rows = 16
        self.part_v = vectors // 2
        self.half = modes // 2
        self.quarter = modes // 4
        chip_bits = (self.columns - 1).bit_length()
        assert self.columns == 1 << chip_bits and self.waves == 2
        self.chip_masks = [(1 << b) * self.waves + 1 for b in reversed(range(chip_bits))]
        self.masks = self.chip_masks + [1]

    def me(self):
        return lax.axis_index("tile") * self.waves + lax.axis_index("wave")

    def device_of(self, block):
        device = self.me()
        for k, mask in enumerate(self.masks):
            device = device ^ (((block >> k) & 1) * mask)
        return device

    def block_of(self, device):
        rest = device ^ self.me()
        block = 0
        for k, mask in enumerate(self.chip_masks):
            bit = (rest >> (mask.bit_length() - 1)) & 1
            block = block | (bit << k)
            rest = rest ^ (bit * mask)
        block = block | (rest << len(self.chip_masks))
        return block


def swap_cores(array):
    return lax.ppermute(array, "wave", [(0, 1), (1, 0)])


def gather_parts(array, layout):
    array = array[None]
    parts = []
    for mask in layout.chip_masks:
        pairs = [(i, i ^ mask) for i in range(layout.devices)]
        arrived = lax.ppermute(array, ("tile", "wave"), pairs)
        array = jnp.concatenate([array, arrived])
        parts.append(arrived if parts else array)
    return array, parts


def three_parts(value, pad):
    first = value.astype(bf16).astype(f32)
    value = value - first
    second = value.astype(bf16).astype(f32)
    pieces = [first, second, value - second]
    if pad:
        pieces.append(jnp.zeros((pad, lanes), f32))
    return jnp.concatenate(pieces, 0).astype(bf16)


def add_three(rows, count):
    return rows[:count] + rows[count : 2 * count] + rows[2 * count : 3 * count]


def pack_kernel(layout, head, out, squares):
    rows, vectors = layout.rows, layout.vectors
    out[:rows, :] = head[:rows, :].astype(bf16)
    out[rows:, :] = three_parts(head[rows:, :], layout.offset_rows - 6 * layout.tiles)
    total = 0.0
    for k in range(2 * layout.tiles):
        piece = head[k * vectors : (k + 1) * vectors, :]
        total = total + piece * piece
    squares[...] = total


def split_dot(weights, value, dims):
    total = 0.0
    for _ in range(3):
        part = value.astype(bf16)
        total = total + lax.dot_general(weights, part, dims, preferred_element_type=f32)
        value = value - part.astype(f32)
    return total


def spectral_kernel(layout, scale, table, frequency, out, guess, order, moved_all, sem):
    size = 2 * layout.half
    count = moved_all.shape[0]
    copy = pltpu.make_async_copy(frequency, order, sem)
    copy.start()
    spot = lax.broadcasted_iota(jnp.int32, (size, size), 0)
    wanted = jnp.where(spot < layout.half, spot + layout.half, size - 1 - spot).astype(f32)
    pick_x = jnp.where(wanted == table[count * size : count * size + 1], 1.0, 0.0).astype(bf16)
    pick_y = jnp.where(wanted == table[count * size + 1 : count * size + 2], 1.0, 0.0).astype(bf16)
    for f in range(count):
        moved = split_dot(pick_x, table[f * size : (f + 1) * size] * scale, (((1,), (0,)), ((), ())))
        moved_all[f] = split_dot(pick_y, moved, (((1,), (1,)), ((), ())))
    copy.wait()
    rows = []
    for v in range(layout.vectors):
        moved = moved_all[order[v]]
        out[v] = moved
        mean = jnp.sum(jnp.sum(moved, 0, keepdims=True), 1, keepdims=True)
        rows.append(jnp.broadcast_to(0.5 + mean, (1, lanes)))
    guess[...] = jnp.concatenate(rows, 0)


def make_tables(layout, base, pair, half_block, density, table_x, table_y):
    tiles, half, quarter = layout.tiles, layout.half, layout.quarter
    block = 2 * pair + half_block
    device = layout.device_of(base + block)
    column, row_index = device // layout.waves, device % layout.waves
    offset = add_three(density[block, layout.rows :, :].astype(f32), 2 * tiles)
    eight = lax.broadcasted_iota(jnp.int32, (8, lanes), 0).astype(f32)
    coarse_y = jnp.where(eight < 4, quarter / 2 + 0.5 + 8 * eight, jnp.where(eight < 5, quarter / 2.0, 0.5))
    for i in range(tiles):
        g = (column * layout.strips + i // layout.tiles_y).astype(f32)
        h = (row_index * layout.tiles_y + i % layout.tiles_y).astype(f32)
        x = jnp.broadcast_to((offset[2 * i : 2 * i + 1] + g) * (1.0 / layout.count_x), (8, lanes))
        y = jnp.broadcast_to((offset[2 * i + 1 : 2 * i + 2] + h) * (1.0 / layout.count_y), (8, lanes))
        fine_xc, fine_xs = cos_sin(eight * x)
        big_xc, big_xs = cos_sin((8 * eight + 0.5) * x)
        fine_yc, fine_ys = cos_sin(eight * y)
        big_yc, big_ys = cos_sin(coarse_y * y + jnp.where(eight == 5, 0.5, 0.0) * x)
        shift_c, shift_s = big_yc[4:5], big_ys[4:5]
        span = slice(i * lanes, (i + 1) * lanes)
        wide = slice(half_block * layout.local + i * lanes, half_block * layout.local + (i + 1) * lanes)
        for e, sign in ((0, 1.0), (1, -1.0)):
            both_c = big_xc * shift_c - sign * (big_xs * shift_s)
            both_s = big_xs * shift_c + sign * (big_xc * shift_s)
            cosines, sines = [], []
            for a in range(half // 8):
                c, s = both_c[a : a + 1], both_s[a : a + 1]
                cosines.append(c * fine_xc - s * fine_xs)
                sines.append(s * fine_xc + c * fine_xs)
            table_x[pair, 2 * half * e : 2 * half * (e + 1), wide] = jnp.concatenate(cosines + sines, 0).astype(bf16)
        cosines, sines = [], []
        for a in range(quarter // 8):
            c, s = big_yc[a : a + 1], big_ys[a : a + 1]
            cosines.append(c * fine_yc - s * fine_ys)
            sines.append(s * fine_yc + c * fine_ys)
        last = jnp.concatenate([big_yc[5:6], big_ys[5:6], jnp.zeros((6, lanes), f32)], 0)
        table_y[block, :, span] = jnp.concatenate(cosines + sines + [last], 0)


def pick_half(layout, rows, other):
    count = layout.part_v
    core = lax.axis_index("wave")
    upper = jnp.broadcast_to(1 - core if other else core, (count, lanes)) == 1
    return jnp.where(upper, rows[count:], rows[:count])


def both_halves(layout, own, other):
    upper = jnp.broadcast_to(lax.axis_index("wave"), own.shape) == 1
    return jnp.concatenate([jnp.where(upper, other, own), jnp.where(upper, own, other)], 0)


def twist(layout, pair, half_block, density, table_y, out, halves):
    vectors, group = layout.vectors, 2 * layout.quarter
    block = 2 * pair + half_block
    for i in range(layout.tiles):
        span = slice(i * lanes, (i + 1) * lanes)
        wide = slice(half_block * layout.local + i * lanes, half_block * layout.local + (i + 1) * lanes)
        values = density[block, i * 2 * vectors : (i + 1) * 2 * vectors, :].astype(f32)
        waves = table_y[block, :group, span]
        c, s = table_y[block, group : group + 1, span], table_y[block, group + 1 : group + 2, span]
        start = 0
        for other in halves:
            real, imag = pick_half(layout, values[:vectors], other), pick_half(layout, values[vectors:], other)
            turned = (real * c - imag * s, imag * c + real * s)
            for v in range(layout.part_v):
                for part in range(2):
                    out[start : start + group, wide] = (turned[part][v : v + 1] * waves).astype(bf16)
                    start += group


def project(layout, base, density, table_x, table_y, twisted, total, start, halves, with_tables):
    def step(pair, before):
        for half_block in range(2):
            if with_tables:
                make_tables(layout, base, pair, half_block, density, table_x, table_y)
            twist(layout, pair, half_block, density, table_y, twisted, halves)
        product = lax.dot_general(
            twisted[...], table_x[pair], (((1,), (1,)), ((), ())), preferred_element_type=f32
        )
        total[...] = product if before is None else before[...] + product

    step(0, start)
    pairs = density.shape[0] // 2
    if pairs > 1:
        lax.fori_loop(1, pairs, lambda pair, carry: step(pair, total) or carry, 0)


def part_kernel(layout, base, with_start, with_tables, halves, *refs):
    refs = list(refs)
    density = refs.pop(0)
    tables = None if with_tables else (refs.pop(0), refs.pop(0))
    start = refs.pop(0) if with_start else None
    total = refs.pop(0)
    table_x, table_y = tables or (refs.pop(0), refs.pop(0))
    twisted = refs.pop(0)
    if len(halves) == 1:
        size = twisted.shape[0]
        start = start.at[size * halves[0] : size * (halves[0] + 1)]
    held = refs.pop(0) if refs else total
    project(layout, base, density, table_x, table_y, twisted, held, start, halves, with_tables)
    if held is not total:
        total[...] = held[...].astype(total.dtype)


def table_kernel(layout, base, density, table_x, table_y):
    make_tables(layout, base, 0, 0, density, table_x, table_y)


def swap(value):
    return pltpu.roll(value, lanes // 2, 1)


def weigh(layout, total, weight, scaled):
    quarter = layout.quarter
    first = lax.axis_index("wave") * layout.part_v
    low = lax.broadcasted_iota(jnp.int32, (quarter, lanes), 1) < layout.half
    sign = jnp.where(low, -1.0, 1.0)
    for v in range(layout.part_v):
        table = weight[first + v]
        part = [table[k * quarter : (k + 1) * quarter] for k in range(4)]
        choices = ((part[1], part[3]), (part[2], part[0]), (part[0], part[2]), (part[3], part[1]))
        for e in range(2):
            span = slice(e * lanes, (e + 1) * lanes)
            real = v * 4 * quarter
            imag = real + 2 * quarter
            cos_r = total[real : real + quarter, span]
            sin_r = swap(total[real + quarter : real + 2 * quarter, span]) * sign
            cos_i = total[imag : imag + quarter, span]
            sin_i = swap(total[imag + quarter : imag + 2 * quarter, span]) * sign
            out = []
            for k, (mr, mi) in enumerate(((cos_r + sin_r, cos_i + sin_i), (cos_r - sin_r, cos_i - sin_i))):
                chosen = jnp.where(low, *choices[2 * e + k])
                turned = swap(chosen)
                plus, minus = chosen + turned, chosen - turned
                out.append((plus * mr + minus * swap(mi), plus * mi - minus * swap(mr)))
            for start, k in ((real, 0), (imag, 1)):
                scaled[start : start + quarter, span] = (out[0][k] + out[1][k]).astype(bf16)
                scaled[start + quarter : start + 2 * quarter, span] = swap(sign * (out[0][k] - out[1][k])).astype(bf16)


def expand(layout, scaled, table_x, table_y, summed, result):
    count, group = layout.part_v, 2 * layout.quarter
    summed[...] = jnp.dot(scaled[...], table_x[0, :, : layout.local], preferred_element_type=f32)
    for i in range(layout.tiles):
        span = slice(i * lanes, (i + 1) * lanes)
        waves = table_y[0, :group, span]
        rows = []
        for k in range(2 * count):
            rows.append(jnp.sum(summed[k * group : (k + 1) * group, span] * waves, 0, keepdims=True))
        real, imag = jnp.concatenate(rows[0::2], 0), jnp.concatenate(rows[1::2], 0)
        c, s = table_y[0, group : group + 1, span], table_y[0, group + 1 : group + 2, span]
        result[2 * count * i : 2 * count * (i + 1), :] = jnp.concatenate([real * c + imag * s, imag * c - real * s], 0)


def far_kernel(layout, own, arrived, weight, own_x, own_y, other_x, other_y, far_own, far_other, total, scaled, summed):
    total[...] = own[...] + arrived[...].astype(f32)
    weigh(layout, total, weight, scaled)
    expand(layout, scaled, other_x, other_y, summed, far_other)
    expand(layout, scaled, own_x, own_y, summed, far_own)


def far_rows(layout, i, own, other):
    count = layout.part_v
    real, imag = [
        both_halves(layout, own[start : start + count, :], other[start : start + count, :])
        for start in (2 * count * i, 2 * count * i + count)
    ]
    return real, imag


def near_tile(layout, i, neighbor, density, kernel):
    vectors = layout.vectors
    g = lax.axis_index("tile") * layout.strips + i // layout.tiles_y
    h = lax.axis_index("wave") * layout.tiles_y + i % layout.tiles_y
    by_real, by_imag = 0.0, 0.0
    for j in range(9):
        slot = neighbor[i, j]
        step_x = lax.div(slot, 3)
        gx = lax.rem(g + step_x - 1 + layout.count_x, layout.count_x)
        hy = lax.rem(h + slot - 3 * step_x - 1 + layout.count_y, layout.count_y)
        block = layout.block_of(lax.div(gx, layout.strips) * layout.waves + lax.div(hy, layout.tiles_y))
        tile = lax.rem(gx, layout.strips) * layout.tiles_y + lax.rem(hy, layout.tiles_y)
        start = pl.multiple_of(tile * 2 * vectors, 2 * vectors)
        values = density[block, pl.ds(start, 2 * vectors), :]
        by_real += jnp.dot(values, kernel[i, j, 0], preferred_element_type=f32)
        by_imag += jnp.dot(values, kernel[i, j, 1], preferred_element_type=f32)
    return jnp.concatenate(
        [by_real[:vectors] - by_imag[vectors:], by_imag[:vectors] + by_real[vectors:]], 0
    )


def near_kernel(layout, density, blocks, neighbor, out, places, sem):
    copy = pltpu.make_async_copy(neighbor, places, sem)
    copy.start()
    copy.wait()
    tall = 2 * layout.vectors
    for i in range(layout.tiles):
        out[i * tall : (i + 1) * tall, :] = near_tile(layout, i, places, density, blocks)


def spread(layout, row_of):
    spot = lax.broadcasted_iota(jnp.int32, (layout.vectors, lanes), 0)
    lane = lax.broadcasted_iota(jnp.int32, (layout.vectors, lanes), 1)
    return [lane == spot + k * layout.vectors for k in row_of]


def first_kernel(layout, density, near, far_own, far_other, guess, squares, basis, image):
    vectors, tall, rows = layout.vectors, 2 * layout.vectors, layout.rows
    hint = guess[...]
    sums = [squares[...]] + [0.0] * 4
    for i in range(layout.tiles):
        first = i * tall
        far_real, far_imag = far_rows(layout, i, far_own, far_other)
        own = density[first : first + tall, :].astype(f32)
        rr, ri = own[:vectors], own[vectors:]
        wr = 0.5 * rr + near[first : first + vectors, :] + far_real
        wi = 0.5 * ri + near[first + vectors : first + tall, :] + far_imag
        zr, zi = wr - hint * rr, wi - hint * ri
        image[first : first + tall, :] = jnp.concatenate([wr, wi], 0)
        basis[first : first + tall, :] = jnp.concatenate([zr, zi], 0).astype(bf16)
        terms = (rr * rr + ri * ri, rr * zr + ri * zi, rr * zi - ri * zr, zr * zr + zi * zi)
        sums = sums[:1] + [a + b for a, b in zip(sums[1:], terms)]
    line = jnp.zeros((vectors, lanes), f32)
    for value, place in zip(sums, spread(layout, range(5))):
        line = line + jnp.where(place, jnp.sum(value, 1, keepdims=True), 0.0)
    basis[rows:, :] = three_parts(jnp.sum(line, 0, keepdims=True), layout.sum_rows - 3)


def scalar_kernel(layout, density, guess, scalars, factors):
    vectors, rows = layout.vectors, layout.rows
    line = jnp.zeros((1, lanes), f32)
    for device in range(layout.devices):
        line = line + add_three(density[layout.block_of(device), rows:, :].astype(f32), 1)
    line = jnp.broadcast_to(line * (1.0 / layout.panels), (vectors, lanes))
    exact, squares, real, imag, rest = [
        jnp.broadcast_to(jnp.sum(jnp.where(place, line, 0.0), 1, keepdims=True), (vectors, lanes))
        for place in spread(layout, range(5))
    ]
    hint = guess[...]
    scale_sq = exact + eps_norm
    coef_real = (real + hint * squares) / scale_sq
    coef_imag = imag / scale_sq
    more_real, more_imag = coef_real - hint, coef_imag
    update_sq = rest - 2.0 * (more_real * real + more_imag * imag) + (more_real * more_real + more_imag * more_imag) * squares
    scale = jnp.sqrt(scale_sq)
    update_scale = jnp.sqrt(jnp.maximum(update_sq, 0.0) / scale_sq + eps_norm)
    here = spread(layout, [0])[0]
    lines = [
        jnp.sum(jnp.where(here, value, 0.0), 0, keepdims=True)
        for value in (scale, coef_real, coef_imag, update_scale)
    ]
    scalars[...] = jnp.concatenate(lines, 0)[:, :vectors]
    factors[...] = jnp.concatenate([more_real, more_imag, 1.0 / (scale * update_scale)], 0)


def second_kernel(layout, density, near, far_own, far_other, image, factors, result):
    vectors, tall = layout.vectors, 2 * layout.vectors
    more_real, more_imag = factors[:vectors, :], factors[vectors : 2 * vectors, :]
    inverse = factors[2 * vectors :, :]
    for i in range(layout.tiles):
        first = i * tall
        far_real, far_imag = far_rows(layout, i, far_own, far_other)
        own = density[first : first + tall, :].astype(f32)
        wr, wi = image[first : first + vectors, :], image[first + vectors : first + tall, :]
        real = 0.5 * own[:vectors] + near[first : first + vectors, :] + far_real
        imag = 0.5 * own[vectors:] + near[first + vectors : first + tall, :] + far_imag
        result[first : first + vectors, :] = (real - (more_real * wr - more_imag * wi)) * inverse
        result[first + vectors : first + tall, :] = (imag - (more_real * wi + more_imag * wr)) * inverse


def per_device(residual, kernel, offsets, neighbor, frequency, lattice_x, lattice_y, spectral_weight):
    strips, tiles_y, _, vectors, _ = residual.shape
    modes_x, modes_y = spectral_weight.shape[1:]
    layout = Layout(strips, tiles_y, vectors, modes_x)
    tiles, rows, devices = layout.tiles, layout.rows, layout.devices
    vmem, hbm = pl.BlockSpec(memory_space=pltpu.VMEM), pl.BlockSpec(memory_space=pltpu.HBM)
    shape = jax.ShapeDtypeStruct
    tall = 2 * vectors * 2 * layout.quarter
    wide = 4 * layout.half
    count = spectral_weight.shape[0]

    def call(body, name, out_shape, in_specs, limit, scratch=(), flops=0, aliases=None):
        return pl.pallas_call(
            body,
            out_shape=out_shape,
            in_specs=in_specs,
            out_specs=jax.tree.map(lambda _: vmem, out_shape),
            scratch_shapes=scratch,
            input_output_aliases=aliases or {},
            compiler_params=pltpu.CompilerParams(vmem_limit_bytes=int(limit * mib)),
            cost_estimate=pl.CostEstimate(flops=flops, bytes_accessed=0, transcendentals=0),
            name=name,
        )

    head = jnp.concatenate([residual.reshape(rows, lanes), offsets.reshape(2 * tiles, lanes)], 0)
    packed, squares = call(
        lambda *refs: pack_kernel(layout, *refs),
        "pack",
        (shape((rows + layout.offset_rows, lanes), bf16), shape((vectors, lanes), f32)),
        [vmem],
        1,
    )(head)
    scale = 1.0 / math.sqrt(modes_x * modes_y * layout.panels)
    table = jnp.concatenate(
        [spectral_weight.reshape(-1, lanes), lattice_x.astype(f32)[None], lattice_y.astype(f32)[None]], 0
    )
    weight, guess = call(
        lambda *refs: spectral_kernel(layout, scale, *refs),
        "spectral",
        (shape((vectors, modes_y, modes_x), f32), shape((vectors, lanes), f32)),
        [vmem, hbm],
        4,
        [
            pltpu.SMEM(frequency.shape, jnp.int32),
            pltpu.VMEM(spectral_weight.shape, f32),
            pltpu.SemaphoreType.DMA,
        ],
        flops=12 * count * modes_x**3,
    )(table, frequency)
    blocks = kernel.reshape(tiles, 9, 2, lanes, lanes)
    neighbor = neighbor.reshape(tiles, 9)

    def table_shapes(size):
        return (
            shape((-(-size // 2), wide, min(size, 2) * layout.local), bf16),
            shape((size, 2 * layout.quarter + 8, layout.local), f32),
        )

    def part_call(name, base, part, tables, total, halves, dtype):
        size = part.shape[0]
        high = len(halves) * tall // 2
        given = [part] + list(tables or ()) + ([] if total is None else [total])
        scratch = [pltpu.VMEM((high, 2 * layout.local), bf16)]
        if dtype != f32:
            scratch.append(pltpu.VMEM((high, wide), f32))
        with_start = total is not None
        return call(
            lambda *refs: part_kernel(layout, base, with_start, not tables, halves, *refs),
            name,
            (shape((high, wide), dtype), *(() if tables else table_shapes(size))),
            [vmem] * len(given),
            24,
            scratch,
            flops=size * 2 * layout.local * high * wide,
            aliases={len(given) - 1: 0} if with_start and len(halves) == 2 else None,
        )(*given)

    def far_field(parts, tables, arrive):
        total, base, made = None, 0, []
        for k, part in enumerate(parts[:-1]):
            total, *new = part_call("part", base, part, tables and tables[k], total, (0, 1), f32)
            base += part.shape[0]
            made.append(new or tables[k])
        leaving, *new = part_call("leaving", base, parts[-1], tables and tables[-1], total, (1,), bf16)
        made.append(new or tables[-1])
        arrived = swap_cores(leaving)
        (staying,) = part_call("staying", base, parts[-1], made[-1], total, (0,), f32)
        far_own, far_other = call(
            lambda *refs: far_kernel(layout, *refs),
            "far",
            tuple([shape((rows // 2, lanes), f32)] * 2),
            [vmem] * 7,
            24,
            [
                pltpu.VMEM((tall // 2, wide), f32),
                pltpu.VMEM((tall // 2, wide), bf16),
                pltpu.VMEM((tall // 2, layout.local), f32),
            ],
            flops=2 * tall * wide * layout.local,
        )(staying, arrived, weight, *made[0], *arrive)
        return far_own, swap_cores(far_other), made

    def near_field(density):
        return call(
            lambda *refs: near_kernel(layout, *refs),
            "near",
            shape((rows, lanes), f32),
            [vmem, vmem, hbm],
            12,
            [pltpu.SMEM(neighbor.shape, jnp.int32), pltpu.SemaphoreType.DMA],
            flops=2 * tiles * 9 * 2 * lanes * lanes * 2 * vectors,
        )(density, blocks, neighbor)

    def with_other_core(array):
        return jnp.concatenate([array, swap_cores(array)])

    other_tables = call(
        lambda *refs: table_kernel(layout, devices // 2, *refs),
        "other_tables",
        table_shapes(1),
        [vmem],
        8,
        flops=layout.local * wide * 100,
    )(swap_cores(packed)[None])
    gathered, parts = gather_parts(packed, layout)
    near_one = near_field(with_other_core(gathered))
    far_own, far_other, tables = far_field(parts, None, other_tables)
    basis, image = call(
        lambda *refs: first_kernel(layout, *refs),
        "first",
        (shape((rows + layout.sum_rows, lanes), bf16), shape((rows, lanes), f32)),
        [vmem] * 6,
        2,
    )(packed, near_one, far_own, far_other, guess, squares)
    gathered, parts = gather_parts(basis, layout)
    everything = with_other_core(gathered)
    scalars, factors = call(
        lambda *refs: scalar_kernel(layout, *refs),
        "scalars",
        (shape((4, vectors), f32), shape((3 * vectors, lanes), f32)),
        [vmem] * 2,
        2,
    )(everything, guess)
    near_two = near_field(everything)
    far_own, far_other, _ = far_field(parts, tables, other_tables)
    result = call(
        lambda *refs: second_kernel(layout, *refs),
        "second",
        shape((rows, lanes), f32),
        [vmem] * 6,
        2,
    )(basis, near_two, far_own, far_other, image, factors)
    return result.reshape(residual.shape), scalars


def solution(mesh):
    return jax.shard_map(
        per_device,
        mesh=mesh,
        in_specs=(
            P(("grp", "tile"), "wave", None, None, None),
            P(("grp", "tile"), "wave", None, None, None, None),
            P(("grp", "tile"), "wave", None, None),
            P(("grp", "tile"), "wave", None),
            P("grp"),
            P(),
            P(),
            P(),
        ),
        out_specs=(P(("grp", "tile"), "wave", None, None, None), P("grp", None)),
        check_vma=False,
    )
```

```python
import math

import jax
import jax.numpy as jnp
from jax import lax
from jax.experimental import pallas as pl
from jax.experimental.pallas import tpu as pltpu
from jax.sharding import PartitionSpec as P

eps_norm = 1e-06
lengths = {"part": 1, "leaving": 1, "staying": 2, "spectral": 2, "other_tables": 0.5, "far": 1, "near": 2}
f32 = jnp.float32
bf16 = jnp.bfloat16
lanes = 128
mib = 1024 * 1024

sine_terms = (6.283185160087918, -10.3354137577709, 5.100062753380459, -1.1960903419427114, 0.1544402466966843)
cosine_terms = (0.9999999534659573, -4.93479285858416, 4.058411912342187, -1.331880149557601, 0.21969677520430975)


def horner(terms, value):
    total = jnp.full_like(value, terms[-1])
    for term in terms[-2::-1]:
        total = total * value + term
    return total


def cos_sin(turns):
    turn = turns - jnp.round(turns)
    square = turn * turn
    double = turn * horner(sine_terms, square)
    return 1.0 - 0.5 * (double * double), double * horner(cosine_terms, square)


class Layout:
    def __init__(self, strips, tiles_y, vectors, modes):
        self.strips, self.tiles_y, self.vectors = strips, tiles_y, vectors
        self.tiles = strips * tiles_y
        self.columns, self.waves = lax.axis_size("tile"), lax.axis_size("wave")
        self.devices = self.columns * self.waves
        self.count_x, self.count_y = self.columns * strips, self.waves * tiles_y
        self.panels = self.count_x * self.count_y * lanes
        self.local = self.tiles * lanes
        self.rows = self.tiles * 2 * vectors
        self.offset_rows = -(-6 * self.tiles // 16) * 16
        self.sum_rows = 16
        self.part_v = vectors // 2
        self.half = modes // 2
        self.quarter = modes // 4
        chip_bits = (self.columns - 1).bit_length()
        assert self.columns == 1 << chip_bits and self.waves == 2
        self.chip_masks = [(1 << b) * self.waves + 1 for b in reversed(range(chip_bits))]
        self.masks = self.chip_masks + [1]

    def me(self):
        return lax.axis_index("tile") * self.waves + lax.axis_index("wave")

    def device_of(self, block):
        device = self.me()
        for k, mask in enumerate(self.masks):
            device = device ^ (((block >> k) & 1) * mask)
        return device

    def group_of(self, density):
        return min(density.shape[0], 4)

    def block_of(self, device):
        rest = device ^ self.me()
        block = 0
        for k, mask in enumerate(self.chip_masks):
            bit = (rest >> (mask.bit_length() - 1)) & 1
            block = block | (bit << k)
            rest = rest ^ (bit * mask)
        block = block | (rest << len(self.chip_masks))
        return block


def swap_cores(array):
    return lax.ppermute(array, "wave", [(0, 1), (1, 0)])


def after(value, *others):
    return lax.optimization_barrier((value, *others))[0]


def three_parts(value, pad):
    first = value.astype(bf16).astype(f32)
    value = value - first
    second = value.astype(bf16).astype(f32)
    pieces = [first, second, value - second]
    if pad:
        pieces.append(jnp.zeros((pad, lanes), f32))
    return jnp.concatenate(pieces, 0).astype(bf16)


def add_three(rows, count):
    return rows[:count] + rows[count : 2 * count] + rows[2 * count : 3 * count]


def pack_kernel(layout, head, out, squares):
    rows, vectors = layout.rows, layout.vectors
    out[:rows, :] = head[:rows, :].astype(bf16)
    out[rows:, :] = three_parts(head[rows:, :], layout.offset_rows - 6 * layout.tiles)
    total = 0.0
    for k in range(2 * layout.tiles):
        piece = head[k * vectors : (k + 1) * vectors, :]
        total = total + piece * piece
    squares[...] = total


def split_dot(weights, value, dims):
    total = 0.0
    for _ in range(3):
        part = value.astype(bf16)
        total = total + lax.dot_general(weights, part, dims, preferred_element_type=f32)
        value = value - part.astype(f32)
    return total


def spectral_kernel(layout, scale, integers, table, out, guess, order, moved_all, sem):
    size = 2 * layout.half
    count = moved_all.shape[0]
    copy = pltpu.make_async_copy(integers.at[2:3], order, sem)
    copy.start()
    spot = lax.broadcasted_iota(jnp.int32, (size, size), 0)
    wanted = jnp.where(spot < layout.half, spot + layout.half, size - 1 - spot)
    pick_x = jnp.where(wanted == integers[0:1], 1.0, 0.0).astype(bf16)
    pick_y = jnp.where(wanted == integers[1:2], 1.0, 0.0).astype(bf16)
    for f in range(count):
        moved = split_dot(pick_x, table[f] * scale, (((1,), (0,)), ((), ())))
        moved_all[f] = split_dot(pick_y, moved, (((1,), (1,)), ((), ())))
    copy.wait()
    rows = []
    for v in range(layout.vectors):
        moved = moved_all[order[0, v]]
        out[v] = moved
        mean = jnp.sum(jnp.sum(moved, 0, keepdims=True), 1, keepdims=True)
        rows.append(jnp.broadcast_to(0.5 + mean, (1, lanes)))
    guess[...] = jnp.concatenate(rows, 0)


def make_tables(layout, base, group, k, density, table_x, table_y):
    tiles, half, quarter = layout.tiles, layout.half, layout.quarter
    block = layout.group_of(density) * group + k
    device = layout.device_of(base + block)
    column, row_index = device // layout.waves, device % layout.waves
    offset = add_three(density[block, layout.rows :, :].astype(f32), 2 * tiles)
    eight = lax.broadcasted_iota(jnp.int32, (8, lanes), 0).astype(f32)
    coarse_y = jnp.where(eight < 4, quarter / 2 + 0.5 + 8 * eight, jnp.where(eight < 5, quarter / 2.0, 0.5))
    for i in range(tiles):
        g = (column * layout.strips + i // layout.tiles_y).astype(f32)
        h = (row_index * layout.tiles_y + i % layout.tiles_y).astype(f32)
        x = jnp.broadcast_to((offset[2 * i : 2 * i + 1] + g) * (1.0 / layout.count_x), (8, lanes))
        y = jnp.broadcast_to((offset[2 * i + 1 : 2 * i + 2] + h) * (1.0 / layout.count_y), (8, lanes))
        fine_xc, fine_xs = cos_sin(eight * x)
        big_xc, big_xs = cos_sin((8 * eight + 0.5) * x)
        fine_yc, fine_ys = cos_sin(eight * y)
        big_yc, big_ys = cos_sin(coarse_y * y + jnp.where(eight == 5, 0.5, 0.0) * x)
        shift_c, shift_s = big_yc[4:5], big_ys[4:5]
        span = slice(i * lanes, (i + 1) * lanes)
        wide = slice(k * layout.local + i * lanes, k * layout.local + (i + 1) * lanes)
        for e, sign in ((0, 1.0), (1, -1.0)):
            both_c = big_xc * shift_c - sign * (big_xs * shift_s)
            both_s = big_xs * shift_c + sign * (big_xc * shift_s)
            cosines, sines = [], []
            for a in range(half // 8):
                c, s = both_c[a : a + 1], both_s[a : a + 1]
                cosines.append(c * fine_xc - s * fine_xs)
                sines.append(s * fine_xc + c * fine_xs)
            table_x[group, 2 * half * e : 2 * half * (e + 1), wide] = jnp.concatenate(cosines + sines, 0).astype(bf16)
        cosines, sines = [], []
        for a in range(quarter // 8):
            c, s = big_yc[a : a + 1], big_ys[a : a + 1]
            cosines.append(c * fine_yc - s * fine_ys)
            sines.append(s * fine_yc + c * fine_ys)
        last = jnp.concatenate([big_yc[5:6], big_ys[5:6], jnp.zeros((6, lanes), f32)], 0)
        table_y[block, :, span] = jnp.concatenate(cosines + sines + [last], 0)


def pick_half(layout, rows, other):
    count = layout.part_v
    core = lax.axis_index("wave")
    upper = jnp.broadcast_to(1 - core if other else core, (count, lanes)) == 1
    return jnp.where(upper, rows[count:], rows[:count])


def both_halves(layout, own, other):
    upper = jnp.broadcast_to(lax.axis_index("wave"), own.shape) == 1
    return jnp.concatenate([jnp.where(upper, other, own), jnp.where(upper, own, other)], 0)


def twist(layout, block, k, density, table_y, out, halves):
    vectors, group = layout.vectors, 2 * layout.quarter
    for i in range(layout.tiles):
        span = slice(i * lanes, (i + 1) * lanes)
        wide = slice(k * layout.local + i * lanes, k * layout.local + (i + 1) * lanes)
        values = density[block, i * 2 * vectors : (i + 1) * 2 * vectors, :].astype(f32)
        waves = table_y[block, :group, span]
        c, s = table_y[block, group : group + 1, span], table_y[block, group + 1 : group + 2, span]
        start = 0
        for other in halves:
            real, imag = pick_half(layout, values[:vectors], other), pick_half(layout, values[vectors:], other)
            turned = (real * c - imag * s, imag * c + real * s)
            for v in range(layout.part_v):
                for part in range(2):
                    out[start : start + group, wide] = (turned[part][v : v + 1] * waves).astype(bf16)
                    start += group


def project(layout, base, density, table_x, table_y, twisted, total, start, halves, with_tables):
    size = layout.group_of(density)

    def step(group, before):
        for k in range(size):
            if with_tables:
                make_tables(layout, base, group, k, density, table_x, table_y)
            twist(layout, size * group + k, k, density, table_y, twisted, halves)
        product = lax.dot_general(
            twisted[...], table_x[group], (((1,), (1,)), ((), ())), preferred_element_type=f32
        )
        total[...] = product if before is None else before[...] + product

    step(0, start)
    groups = density.shape[0] // size
    if groups > 1:
        lax.fori_loop(1, groups, lambda group, carry: step(group, total) or carry, 0)


def part_kernel(layout, base, with_start, with_tables, halves, *refs):
    refs = list(refs)
    density = refs.pop(0)
    tables = None if with_tables else (refs.pop(0), refs.pop(0))
    start = refs.pop(0) if with_start else None
    total = refs.pop(0)
    table_x, table_y = tables or (refs.pop(0), refs.pop(0))
    twisted = refs.pop(0)
    if len(halves) == 1:
        size = twisted.shape[0]
        start = start.at[size * halves[0] : size * (halves[0] + 1)]
    held = refs.pop(0) if refs else total
    project(layout, base, density, table_x, table_y, twisted, held, start, halves, with_tables)
    if held is not total:
        total[...] = held[...].astype(total.dtype)


def table_kernel(layout, base, density, table_x, table_y):
    make_tables(layout, base, 0, 0, density, table_x, table_y)


def swap(value):
    return pltpu.roll(value, lanes // 2, 1)


def weigh(layout, total, weight, scaled):
    quarter = layout.quarter
    first = lax.axis_index("wave") * layout.part_v
    low = lax.broadcasted_iota(jnp.int32, (quarter, lanes), 1) < layout.half
    sign = jnp.where(low, -1.0, 1.0)
    for v in range(layout.part_v):
        table = weight[first + v]
        part = [table[k * quarter : (k + 1) * quarter] for k in range(4)]
        choices = ((part[1], part[3]), (part[2], part[0]), (part[0], part[2]), (part[3], part[1]))
        for e in range(2):
            span = slice(e * lanes, (e + 1) * lanes)
            real = v * 4 * quarter
            imag = real + 2 * quarter
            cos_r = total[real : real + quarter, span]
            sin_r = swap(total[real + quarter : real + 2 * quarter, span]) * sign
            cos_i = total[imag : imag + quarter, span]
            sin_i = swap(total[imag + quarter : imag + 2 * quarter, span]) * sign
            out = []
            for k, (mr, mi) in enumerate(((cos_r + sin_r, cos_i + sin_i), (cos_r - sin_r, cos_i - sin_i))):
                chosen = jnp.where(low, *choices[2 * e + k])
                turned = swap(chosen)
                plus, minus = chosen + turned, chosen - turned
                out.append((plus * mr + minus * swap(mi), plus * mi - minus * swap(mr)))
            for start, k in ((real, 0), (imag, 1)):
                scaled[start : start + quarter, span] = (out[0][k] + out[1][k]).astype(bf16)
                scaled[start + quarter : start + 2 * quarter, span] = swap(sign * (out[0][k] - out[1][k])).astype(bf16)


def expand(layout, scaled, table_x, table_y, summed, result):
    count, group = layout.part_v, 2 * layout.quarter
    summed[...] = jnp.dot(scaled[...], table_x[0, :, : layout.local], preferred_element_type=f32)
    for i in range(layout.tiles):
        span = slice(i * lanes, (i + 1) * lanes)
        waves = table_y[0, :group, span]
        rows = []
        for k in range(2 * count):
            rows.append(jnp.sum(summed[k * group : (k + 1) * group, span] * waves, 0, keepdims=True))
        real, imag = jnp.concatenate(rows[0::2], 0), jnp.concatenate(rows[1::2], 0)
        c, s = table_y[0, group : group + 1, span], table_y[0, group + 1 : group + 2, span]
        result[2 * count * i : 2 * count * (i + 1), :] = jnp.concatenate([real * c + imag * s, imag * c - real * s], 0)


def far_kernel(layout, own, arrived, weight, own_x, own_y, other_x, other_y, far_own, far_other, total, scaled, summed, summed_other):
    total[...] = own[...] + arrived[...].astype(f32)
    weigh(layout, total, weight, scaled)
    expand(layout, scaled, other_x, other_y, summed_other, far_other)
    expand(layout, scaled, own_x, own_y, summed, far_own)


def far_rows(layout, i, own, other):
    count = layout.part_v
    real, imag = [
        both_halves(layout, own[start : start + count, :], other[start : start + count, :])
        for start in (2 * count * i, 2 * count * i + count)
    ]
    return real, imag


def near_tile(layout, i, neighbor, density, kernel):
    vectors = layout.vectors
    g = lax.axis_index("tile") * layout.strips + i // layout.tiles_y
    h = lax.axis_index("wave") * layout.tiles_y + i % layout.tiles_y
    values = []
    for j in range(9):
        slot = neighbor[i, j]
        step_x = lax.div(slot, 3)
        gx = lax.rem(g + step_x - 1 + layout.count_x, layout.count_x)
        hy = lax.rem(h + slot - 3 * step_x - 1 + layout.count_y, layout.count_y)
        block = layout.block_of(lax.div(gx, layout.strips) * layout.waves + lax.div(hy, layout.tiles_y))
        tile = lax.rem(gx, layout.strips) * layout.tiles_y + lax.rem(hy, layout.tiles_y)
        start = pl.multiple_of(tile * 2 * vectors, 2 * vectors)
        values.append(density[block, pl.ds(start, 2 * vectors), :])
    total = 0.0
    for j in range(0, 9, 2):
        span = range(j, min(j + 2, 9))
        left = jnp.concatenate([values[k] for k in span], 1)
        right = jnp.concatenate([jnp.concatenate([kernel[i, k, 0], kernel[i, k, 1]], 1) for k in span], 0)
        total += jnp.dot(left, right, preferred_element_type=f32)
    upper, lower = total[:vectors], total[vectors:]
    return jnp.concatenate([upper[:, :lanes] - lower[:, lanes:], upper[:, lanes:] + lower[:, :lanes]], 0)


def near_kernel(layout, density, blocks, neighbor, out):
    places = neighbor[...]
    tall = 2 * layout.vectors
    for i in range(layout.tiles):
        out[i * tall : (i + 1) * tall, :] = near_tile(layout, i, places, density, blocks)


def spread(layout, row_of):
    spot = lax.broadcasted_iota(jnp.int32, (layout.vectors, lanes), 0)
    lane = lax.broadcasted_iota(jnp.int32, (layout.vectors, lanes), 1)
    return [lane == spot + k * layout.vectors for k in row_of]


def first_kernel(layout, density, near, far_own, far_other, guess, squares, basis, image):
    vectors, tall, rows = layout.vectors, 2 * layout.vectors, layout.rows
    hint = guess[...]
    sums = [squares[...]] + [0.0] * 4
    for i in range(layout.tiles):
        first = i * tall
        far_real, far_imag = far_rows(layout, i, far_own, far_other)
        own = density[first : first + tall, :].astype(f32)
        rr, ri = own[:vectors], own[vectors:]
        wr = 0.5 * rr + near[first : first + vectors, :] + far_real
        wi = 0.5 * ri + near[first + vectors : first + tall, :] + far_imag
        zr, zi = wr - hint * rr, wi - hint * ri
        image[first : first + tall, :] = jnp.concatenate([wr, wi], 0)
        basis[first : first + tall, :] = jnp.concatenate([zr, zi], 0).astype(bf16)
        terms = (rr * rr + ri * ri, rr * zr + ri * zi, rr * zi - ri * zr, zr * zr + zi * zi)
        sums = sums[:1] + [a + b for a, b in zip(sums[1:], terms)]
    line = jnp.zeros((vectors, lanes), f32)
    for value, place in zip(sums, spread(layout, range(5))):
        line = line + jnp.where(place, jnp.sum(value, 1, keepdims=True), 0.0)
    basis[rows:, :] = three_parts(jnp.sum(line, 0, keepdims=True), layout.sum_rows - 3)


def scalar_kernel(layout, density, guess, factors):
    vectors, rows = layout.vectors, layout.rows
    line = jnp.zeros((1, lanes), f32)
    for device in range(layout.devices):
        line = line + add_three(density[layout.block_of(device), rows:, :].astype(f32), 1)
    line = jnp.broadcast_to(line * (1.0 / layout.panels), (vectors, lanes))
    exact, squares, real, imag, rest = [
        jnp.broadcast_to(jnp.sum(jnp.where(place, line, 0.0), 1, keepdims=True), (vectors, lanes))
        for place in spread(layout, range(5))
    ]
    hint = guess[...]
    scale_sq = exact + eps_norm
    coef_real = (real + hint * squares) / scale_sq
    coef_imag = imag / scale_sq
    more_real, more_imag = coef_real - hint, coef_imag
    update_sq = rest - 2.0 * (more_real * real + more_imag * imag) + (more_real * more_real + more_imag * more_imag) * squares
    scale = jnp.sqrt(scale_sq)
    update_scale = jnp.sqrt(jnp.maximum(update_sq, 0.0) / scale_sq + eps_norm)
    here = spread(layout, [0])[0]
    lines = [
        jnp.sum(jnp.where(here, value, 0.0), 0, keepdims=True)
        for value in (scale, coef_real, coef_imag, update_scale)
    ]
    lines.append(jnp.zeros((vectors - 4, lanes), f32))
    factors[...] = jnp.concatenate([more_real, more_imag, 1.0 / (scale * update_scale)] + lines, 0)


def second_kernel(layout, density, near, far_own, far_other, image, factors, result, scalars):
    vectors, tall = layout.vectors, 2 * layout.vectors
    more_real, more_imag = factors[:vectors, :], factors[vectors : 2 * vectors, :]
    inverse = factors[2 * vectors : 3 * vectors, :]
    scalars[...] = factors[3 * vectors : 3 * vectors + 4, :vectors]
    for i in range(layout.tiles):
        first = i * tall
        far_real, far_imag = far_rows(layout, i, far_own, far_other)
        own = density[first : first + tall, :].astype(f32)
        wr, wi = image[first : first + vectors, :], image[first + vectors : first + tall, :]
        real = 0.5 * own[:vectors] + near[first : first + vectors, :] + far_real
        imag = 0.5 * own[vectors:] + near[first + vectors : first + tall, :] + far_imag
        result[first : first + vectors, :] = (real - (more_real * wr - more_imag * wi)) * inverse
        result[first + vectors : first + tall, :] = (imag - (more_real * wi + more_imag * wr)) * inverse


def per_device(residual, kernel, offsets, neighbor, frequency, lattice_x, lattice_y, spectral_weight):
    strips, tiles_y, _, vectors, _ = residual.shape
    modes_x, modes_y = spectral_weight.shape[1:]
    layout = Layout(strips, tiles_y, vectors, modes_x)
    tiles, rows, devices = layout.tiles, layout.rows, layout.devices
    vmem = pl.BlockSpec(memory_space=pltpu.VMEM)
    shape = jax.ShapeDtypeStruct
    tall = 2 * vectors * 2 * layout.quarter
    wide = 4 * layout.half
    count = spectral_weight.shape[0]

    def call(body, name, out_shape, in_specs, limit, scratch=(), aliases=None):
        return pl.pallas_call(
            body,
            out_shape=out_shape,
            in_specs=in_specs,
            out_specs=jax.tree.map(lambda _: vmem, out_shape),
            scratch_shapes=scratch,
            input_output_aliases=aliases or {},
            compiler_params=pltpu.CompilerParams(vmem_limit_bytes=int(limit * mib)),
            cost_estimate=pl.CostEstimate(
                flops=int(lengths.get(name, 0) * 1e9), bytes_accessed=0, transcendentals=0
            ),
            name=name,
        )

    head = jnp.concatenate([residual.reshape(rows, lanes), offsets.reshape(2 * tiles, lanes)], 0)
    packed, squares = call(
        lambda *refs: pack_kernel(layout, *refs),
        "pack",
        (shape((rows + layout.offset_rows, lanes), bf16), shape((vectors, lanes), f32)),
        [vmem],
        1,
    )(head)
    scale = 1.0 / math.sqrt(modes_x * modes_y * layout.panels)
    integers = jnp.stack([lattice_x, lattice_y, jnp.pad(frequency, (0, lanes - frequency.shape[0]))])

    def spectral(integers):
        return call(
            lambda *refs: spectral_kernel(layout, scale, *refs),
            "spectral",
            (shape((vectors, modes_y, modes_x), f32), shape((vectors, lanes), f32)),
            [vmem, vmem],
            4,
            [
                pltpu.SMEM((1, lanes), jnp.int32),
                pltpu.VMEM(spectral_weight.shape, f32),
                pltpu.SemaphoreType.DMA,
            ],
        )(integers, spectral_weight)

    blocks = kernel.reshape(tiles, 9, 2, lanes, lanes)
    neighbor = neighbor.reshape(tiles, 9)

    def table_shapes(size):
        return (
            shape((size // min(size, 4), wide, min(size, 4) * layout.local), bf16),
            shape((size, 2 * layout.quarter + 8, layout.local), f32),
        )

    def part_call(name, base, part, tables, total, halves, dtype):
        size = part.shape[0]
        high = len(halves) * tall // 2
        given = [part] + list(tables or ()) + ([] if total is None else [total])
        scratch = [pltpu.VMEM((high, min(size, 4) * layout.local), bf16)]
        if dtype != f32:
            scratch.append(pltpu.VMEM((high, wide), f32))
        with_start = total is not None
        return call(
            lambda *refs: part_kernel(layout, base, with_start, not tables, halves, *refs),
            name,
            (shape((high, wide), dtype), *(() if tables else table_shapes(size))),
            [vmem] * len(given),
            24,
            scratch,
            aliases={len(given) - 1: 0} if with_start and len(halves) == 2 else None,
        )(*given)

    def gather_and_project(array, tables):
        array = array[None]
        total, base, made, seen = None, 0, [], []
        for k, mask in enumerate(layout.chip_masks):
            pairs = [(i, i ^ mask) for i in range(devices)]
            arrived = lax.ppermute(array, ("tile", "wave"), pairs)
            array = jnp.concatenate([array, arrived])
            seen.append(array)
            part = arrived if k else array
            if k < len(layout.chip_masks) - 1:
                total, *new = part_call("part", base, part, tables and tables[k], total, (0, 1), f32)
                base += part.shape[0]
                made.append(new or tables[k])
        leaving, *new = part_call("leaving", base, part, tables and tables[-1], total, (1,), bf16)
        made.append(new or tables[-1])
        (staying,) = part_call("staying", base, part, made[-1], total, (0,), f32)
        return seen, leaving, staying, made

    def far_field(leaving, staying, weight, own_tables, other_tables):
        far_own, far_other = call(
            lambda *refs: far_kernel(layout, *refs),
            "far",
            tuple([shape((rows // 2, lanes), f32)] * 2),
            [vmem] * 7,
            24,
            [
                pltpu.VMEM((tall // 2, wide), f32),
                pltpu.VMEM((tall // 2, wide), bf16),
                pltpu.VMEM((tall // 2, layout.local), f32),
                pltpu.VMEM((tall // 2, layout.local), f32),
            ],
        )(staying, swap_cores(leaving), weight, *own_tables, *other_tables)
        return far_own, swap_cores(far_other)

    def near_field(density):
        return call(
            lambda *refs: near_kernel(layout, *refs),
            "near",
            shape((rows, lanes), f32),
            [vmem] * 3,
            12,
        )(density, blocks, neighbor)

    def with_other_core(array):
        return jnp.concatenate([array, swap_cores(array)])

    seen, leaving, staying, tables = gather_and_project(packed, None)
    other_tables = call(
        lambda *refs: table_kernel(layout, devices // 2, *refs),
        "other_tables",
        table_shapes(1),
        [vmem],
        8,
    )(swap_cores(after(packed, seen[0]))[None])
    weight, guess = spectral(after(integers, seen[1]))
    near_one = near_field(with_other_core(seen[-1]))
    far_own, far_other = far_field(leaving, staying, weight, tables[0], other_tables)
    basis, image = call(
        lambda *refs: first_kernel(layout, *refs),
        "first",
        (shape((rows + layout.sum_rows, lanes), bf16), shape((rows, lanes), f32)),
        [vmem] * 6,
        2,
    )(packed, near_one, far_own, far_other, guess, squares)
    seen, leaving, staying, _ = gather_and_project(basis, tables)
    everything = with_other_core(seen[-1])
    factors = call(
        lambda *refs: scalar_kernel(layout, *refs),
        "scalars",
        shape((4 * vectors, lanes), f32),
        [vmem] * 2,
        2,
    )(everything, guess)
    near_two = near_field(everything)
    far_own, far_other = far_field(leaving, staying, weight, tables[0], other_tables)
    result, scalars = call(
        lambda *refs: second_kernel(layout, *refs),
        "second",
        (shape((rows, lanes), f32), shape((4, vectors), f32)),
        [vmem] * 6,
        2,
    )(basis, near_two, far_own, far_other, image, factors)
    return result.reshape(residual.shape), scalars


def solution(mesh):
    return jax.shard_map(
        per_device,
        mesh=mesh,
        in_specs=(
            P(("grp", "tile"), "wave", None, None, None),
            P(("grp", "tile"), "wave", None, None, None, None),
            P(("grp", "tile"), "wave", None, None),
            P(("grp", "tile"), "wave", None),
            P("grp"),
            P(),
            P(),
            P(),
        ),
        out_specs=(P(("grp", "tile"), "wave", None, None, None), P("grp", None)),
        check_vma=False,
    )
```

```python
import math

import jax
import jax.numpy as jnp
from jax import lax
from jax.experimental import pallas as pl
from jax.experimental.pallas import tpu as pltpu
from jax.sharding import PartitionSpec as P

eps_norm = 1e-06
lengths = {"part": 1, "leaving": 1, "staying": 2, "spectral": 2, "other_tables": 0.5, "far": 1, "near": 2}
f32 = jnp.float32
bf16 = jnp.bfloat16
lanes = 128
mib = 1024 * 1024

sine_terms = (6.283185160087918, -10.3354137577709, 5.100062753380459, -1.1960903419427114, 0.1544402466966843)
cosine_terms = (0.9999999534659573, -4.93479285858416, 4.058411912342187, -1.331880149557601, 0.21969677520430975)


def horner(terms, value):
    total = jnp.full_like(value, terms[-1])
    for term in terms[-2::-1]:
        total = total * value + term
    return total


def cos_sin(turns):
    turn = turns - jnp.round(turns)
    square = turn * turn
    double = turn * horner(sine_terms, square)
    return 1.0 - 0.5 * (double * double), double * horner(cosine_terms, square)


class Layout:
    def __init__(self, strips, tiles_y, vectors, modes):
        self.strips, self.tiles_y, self.vectors = strips, tiles_y, vectors
        self.tiles = strips * tiles_y
        self.columns, self.waves = lax.axis_size("tile"), lax.axis_size("wave")
        self.devices = self.columns * self.waves
        self.count_x, self.count_y = self.columns * strips, self.waves * tiles_y
        self.panels = self.count_x * self.count_y * lanes
        self.local = self.tiles * lanes
        self.rows = self.tiles * 2 * vectors
        self.offset_rows = -(-4 * self.tiles // 16) * 16
        self.part_v = vectors // 2
        self.half = modes // 2
        self.quarter = modes // 4
        chip_bits = (self.columns - 1).bit_length()
        assert self.columns == 1 << chip_bits and self.waves == 2
        self.chip_masks = [(1 << b) * self.waves + 1 for b in reversed(range(chip_bits))]
        self.masks = self.chip_masks + [1]

    def me(self):
        return lax.axis_index("tile") * self.waves + lax.axis_index("wave")

    def device_of(self, block):
        device = self.me()
        for k, mask in enumerate(self.masks):
            device = device ^ (((block >> k) & 1) * mask)
        return device

    def group_of(self, density):
        return min(density.shape[0], 4)

    def block_of(self, device):
        rest = device ^ self.me()
        block = 0
        for k, mask in enumerate(self.chip_masks):
            bit = (rest >> (mask.bit_length() - 1)) & 1
            block = block | (bit << k)
            rest = rest ^ (bit * mask)
        block = block | (rest << len(self.chip_masks))
        return block


def swap_cores(array):
    return lax.ppermute(array, "wave", [(0, 1), (1, 0)])


def after(value, *others):
    return lax.optimization_barrier((value, *others))[0]


def two_parts(value):
    first = value.astype(bf16)
    return first, (value - first.astype(f32)).astype(bf16)


def pack_kernel(layout, head, out):
    rows, count = layout.rows, 2 * layout.tiles
    out[:rows, :] = head[:rows, :].astype(bf16)
    first, second = two_parts(head[rows:, :])
    pieces = [first.astype(f32), second.astype(f32)]
    if layout.offset_rows > 2 * count:
        pieces.append(jnp.zeros((layout.offset_rows - 2 * count, lanes), f32))
    out[rows:, :] = jnp.concatenate(pieces, 0).astype(bf16)


def swap(value):
    return pltpu.roll(value, lanes // 2, 1)


def spectral_kernel(layout, scale, integers, table, out, guess, order, moved_all, sem):
    half, quarter = layout.half, layout.quarter
    size = 2 * half
    count = moved_all.shape[0]
    copy = pltpu.make_async_copy(integers.at[2:3], order, sem)
    copy.start()
    spot = lax.broadcasted_iota(jnp.int32, (size, size), 0)
    wanted = jnp.where(spot < half, spot + half, size - 1 - spot)
    pick_x, pick_y = [jnp.where(wanted == integers[k : k + 1], 1.0, 0.0).astype(bf16) for k in range(2)]
    pick_x, pick_y = [jnp.concatenate([pick, pick], 1) for pick in (pick_x, pick_y)]
    for f in range(0, count, 2):
        pair = range(f, min(f + 2, count))
        columns = [jnp.concatenate(two_parts(table[k] * scale), 0) for k in pair]
        moved = jnp.dot(pick_x, jnp.concatenate(columns, 1), preferred_element_type=f32)
        rows = [jnp.concatenate(two_parts(moved[:, n * size : (n + 1) * size]), 1) for n in range(len(pair))]
        moved = lax.dot_general(
            pick_y, jnp.concatenate(rows, 0), (((1,), (1,)), ((), ())), preferred_element_type=f32
        )
        for n, k in enumerate(pair):
            moved_all[k] = moved[:, n * size : (n + 1) * size]
    copy.wait()
    low = lax.broadcasted_iota(jnp.int32, (quarter, lanes), 1) < half
    rows = []
    for v in range(layout.vectors):
        moved = moved_all[order[0, v]]
        mean = jnp.sum(jnp.sum(moved, 0, keepdims=True), 1, keepdims=True)
        rows.append(jnp.broadcast_to(0.5 + mean, (1, lanes)))
        part = [moved[k * quarter : (k + 1) * quarter] for k in range(4)]
        for k, (one, other) in enumerate(((part[1], part[3]), (part[2], part[0]), (part[0], part[2]), (part[3], part[1]))):
            chosen = jnp.where(low, one, other)
            turned = swap(chosen)
            out[v, 2 * k * quarter : (2 * k + 1) * quarter, :] = chosen + turned
            out[v, (2 * k + 1) * quarter : (2 * k + 2) * quarter, :] = chosen - turned
    guess[...] = jnp.concatenate(rows, 0)


def make_tables(layout, base, group, k, density, table_x, table_y):
    tiles, half, quarter = layout.tiles, layout.half, layout.quarter
    block = layout.group_of(density) * group + k
    device = layout.device_of(base + block)
    column, row_index = device // layout.waves, device % layout.waves
    pieces = density[block, layout.rows :, :].astype(f32)
    offset = pieces[: 2 * tiles] + pieces[2 * tiles : 4 * tiles]
    eight = lax.broadcasted_iota(jnp.int32, (8, lanes), 0).astype(f32)
    coarse_y = jnp.where(eight < 4, quarter / 2 + 0.5 + 8 * eight, jnp.where(eight < 5, quarter / 2.0, 0.5))
    for i in range(tiles):
        g = (column * layout.strips + i // layout.tiles_y).astype(f32)
        h = (row_index * layout.tiles_y + i % layout.tiles_y).astype(f32)
        x = jnp.broadcast_to((offset[2 * i : 2 * i + 1] + g) * (1.0 / layout.count_x), (8, lanes))
        y = jnp.broadcast_to((offset[2 * i + 1 : 2 * i + 2] + h) * (1.0 / layout.count_y), (8, lanes))
        fine_xc, fine_xs = cos_sin(eight * x)
        big_xc, big_xs = cos_sin((8 * eight + 0.5) * x)
        fine_yc, fine_ys = cos_sin(eight * y)
        big_yc, big_ys = cos_sin(coarse_y * y + jnp.where(eight == 5, 0.5, 0.0) * x)
        shift_c, shift_s = big_yc[4:5], big_ys[4:5]
        span = slice(i * lanes, (i + 1) * lanes)
        wide = slice(k * layout.local + i * lanes, k * layout.local + (i + 1) * lanes)
        for e, sign in ((0, 1.0), (1, -1.0)):
            both_c = big_xc * shift_c - sign * (big_xs * shift_s)
            both_s = big_xs * shift_c + sign * (big_xc * shift_s)
            cosines, sines = [], []
            for a in range(half // 8):
                c, s = both_c[a : a + 1], both_s[a : a + 1]
                cosines.append(c * fine_xc - s * fine_xs)
                sines.append(s * fine_xc + c * fine_xs)
            table_x[group, 2 * half * e : 2 * half * (e + 1), wide] = jnp.concatenate(cosines + sines, 0).astype(bf16)
        cosines, sines = [], []
        for a in range(quarter // 8):
            c, s = big_yc[a : a + 1], big_ys[a : a + 1]
            cosines.append(c * fine_yc - s * fine_ys)
            sines.append(s * fine_yc + c * fine_ys)
        last = jnp.concatenate([big_yc[5:6], big_ys[5:6], jnp.zeros((6, lanes), f32)], 0)
        table_y[block, :, span] = jnp.concatenate(cosines + sines + [last], 0)


def pick_half(layout, rows, other):
    count = layout.part_v
    core = lax.axis_index("wave")
    upper = jnp.broadcast_to(1 - core if other else core, (count, lanes)) == 1
    return jnp.where(upper, rows[count:], rows[:count])


def both_halves(layout, own, other):
    upper = jnp.broadcast_to(lax.axis_index("wave"), own.shape) == 1
    return jnp.concatenate([jnp.where(upper, other, own), jnp.where(upper, own, other)], 0)


def twist(layout, block, k, density, table_y, out, halves):
    vectors, group = layout.vectors, 2 * layout.quarter
    for i in range(layout.tiles):
        span = slice(i * lanes, (i + 1) * lanes)
        wide = slice(k * layout.local + i * lanes, k * layout.local + (i + 1) * lanes)
        values = density[block, i * 2 * vectors : (i + 1) * 2 * vectors, :].astype(f32)
        waves = table_y[block, :group, span]
        c, s = table_y[block, group : group + 1, span], table_y[block, group + 1 : group + 2, span]
        start = 0
        for other in halves:
            real, imag = pick_half(layout, values[:vectors], other), pick_half(layout, values[vectors:], other)
            turned = (real * c - imag * s, imag * c + real * s)
            for v in range(layout.part_v):
                for part in range(2):
                    out[start : start + group, wide] = (turned[part][v : v + 1] * waves).astype(bf16)
                    start += group


def project(layout, base, density, table_x, table_y, twisted, total, start, halves, with_tables):
    size = layout.group_of(density)

    def step(group, before):
        for k in range(size):
            if with_tables:
                make_tables(layout, base, group, k, density, table_x, table_y)
            twist(layout, size * group + k, k, density, table_y, twisted, halves)
        product = lax.dot_general(
            twisted[...], table_x[group], (((1,), (1,)), ((), ())), preferred_element_type=f32
        )
        total[...] = product if before is None else before[...] + product

    step(0, start)
    groups = density.shape[0] // size
    if groups > 1:
        lax.fori_loop(1, groups, lambda group, carry: step(group, total) or carry, 0)


def part_kernel(layout, base, with_start, with_tables, halves, *refs):
    refs = list(refs)
    density = refs.pop(0)
    tables = None if with_tables else (refs.pop(0), refs.pop(0))
    start = refs.pop(0) if with_start else None
    total = refs.pop(0)
    table_x, table_y = tables or (refs.pop(0), refs.pop(0))
    twisted = refs.pop(0)
    if len(halves) == 1:
        size = twisted.shape[0]
        start = start.at[size * halves[0] : size * (halves[0] + 1)]
    held = refs.pop(0) if refs else total
    project(layout, base, density, table_x, table_y, twisted, held, start, halves, with_tables)
    if held is not total:
        total[...] = held[...].astype(total.dtype)


def table_kernel(layout, base, density, table_x, table_y):
    make_tables(layout, base, 0, 0, density, table_x, table_y)


def weigh(layout, total, weight, scaled):
    quarter = layout.quarter
    first = lax.axis_index("wave") * layout.part_v
    low = lax.broadcasted_iota(jnp.int32, (quarter, lanes), 1) < layout.half
    sign = jnp.where(low, -1.0, 1.0)
    for v in range(layout.part_v):
        for e in range(2):
            span = slice(e * lanes, (e + 1) * lanes)
            real = v * 4 * quarter
            imag = real + 2 * quarter
            cos_r = total[real : real + quarter, span]
            sin_r = swap(total[real + quarter : real + 2 * quarter, span]) * sign
            cos_i = total[imag : imag + quarter, span]
            sin_i = swap(total[imag + quarter : imag + 2 * quarter, span]) * sign
            out = []
            for k, (mr, mi) in enumerate(((cos_r + sin_r, cos_i + sin_i), (cos_r - sin_r, cos_i - sin_i))):
                start = 2 * (2 * e + k) * quarter
                plus = weight[first + v, start : start + quarter, :]
                minus = weight[first + v, start + quarter : start + 2 * quarter, :]
                out.append((plus * mr + minus * swap(mi), plus * mi - minus * swap(mr)))
            for start, k in ((real, 0), (imag, 1)):
                scaled[start : start + quarter, span] = (out[0][k] + out[1][k]).astype(bf16)
                scaled[start + quarter : start + 2 * quarter, span] = swap(sign * (out[0][k] - out[1][k])).astype(bf16)


def expand(layout, scaled, table_x, table_y, summed, result):
    count, group = layout.part_v, 2 * layout.quarter
    summed[...] = jnp.dot(scaled[...], table_x[0, :, : layout.local], preferred_element_type=f32)
    for i in range(layout.tiles):
        span = slice(i * lanes, (i + 1) * lanes)
        waves = table_y[0, :group, span]
        rows = []
        for k in range(2 * count):
            rows.append(jnp.sum(summed[k * group : (k + 1) * group, span] * waves, 0, keepdims=True))
        real, imag = jnp.concatenate(rows[0::2], 0), jnp.concatenate(rows[1::2], 0)
        c, s = table_y[0, group : group + 1, span], table_y[0, group + 1 : group + 2, span]
        result[2 * count * i : 2 * count * (i + 1), :] = jnp.concatenate([real * c + imag * s, imag * c - real * s], 0)


def far_kernel(layout, own, arrived, weight, own_x, own_y, other_x, other_y, far_own, far_other, total, scaled, summed, summed_other):
    total[...] = own[...] + arrived[...].astype(f32)
    weigh(layout, total, weight, scaled)
    expand(layout, scaled, other_x, other_y, summed_other, far_other)
    expand(layout, scaled, own_x, own_y, summed, far_own)


def far_rows(layout, i, own, other):
    count = layout.part_v
    real, imag = [
        both_halves(layout, own[start : start + count, :], other[start : start + count, :])
        for start in (2 * count * i, 2 * count * i + count)
    ]
    return real, imag


def near_tile(layout, i, neighbor, density, kernel):
    vectors = layout.vectors
    g = lax.axis_index("tile") * layout.strips + i // layout.tiles_y
    h = lax.axis_index("wave") * layout.tiles_y + i % layout.tiles_y
    values = []
    for j in range(9):
        slot = neighbor[i, j]
        step_x = lax.div(slot, 3)
        gx = lax.rem(g + step_x - 1 + layout.count_x, layout.count_x)
        hy = lax.rem(h + slot - 3 * step_x - 1 + layout.count_y, layout.count_y)
        block = layout.block_of(lax.div(gx, layout.strips) * layout.waves + lax.div(hy, layout.tiles_y))
        tile = lax.rem(gx, layout.strips) * layout.tiles_y + lax.rem(hy, layout.tiles_y)
        start = pl.multiple_of(tile * 2 * vectors, 2 * vectors)
        values.append(density[block, pl.ds(start, 2 * vectors), :])
    total = 0.0
    for j in range(0, 9, 2):
        span = range(j, min(j + 2, 9))
        left = jnp.concatenate([values[k] for k in span], 1)
        right = jnp.concatenate([jnp.concatenate([kernel[i, k, 0], kernel[i, k, 1]], 1) for k in span], 0)
        total += jnp.dot(left, right, preferred_element_type=f32)
    upper, lower = total[:vectors], total[vectors:]
    return jnp.concatenate([upper[:, :lanes] - lower[:, lanes:], upper[:, lanes:] + lower[:, :lanes]], 0)


def near_kernel(layout, density, blocks, neighbor, out):
    places = neighbor[...]
    tall = 2 * layout.vectors
    for i in range(layout.tiles):
        out[i * tall : (i + 1) * tall, :] = near_tile(layout, i, places, density, blocks)


def first_kernel(layout, density, near, far_own, far_other, guess, basis, image):
    vectors, tall = layout.vectors, 2 * layout.vectors
    hint = guess[...]
    for i in range(layout.tiles):
        first = i * tall
        far_real, far_imag = far_rows(layout, i, far_own, far_other)
        own = density[first : first + tall, :].astype(f32)
        rr, ri = own[:vectors], own[vectors:]
        wr = 0.5 * rr + near[first : first + vectors, :] + far_real
        wi = 0.5 * ri + near[first + vectors : first + tall, :] + far_imag
        image[first : first + tall, :] = jnp.concatenate([wr, wi], 0)
        basis[first : first + tall, :] = jnp.concatenate([wr - hint * rr, wi - hint * ri], 0).astype(bf16)


def block_sums(layout, start, density, block):
    vectors, tall = layout.vectors, 2 * layout.vectors
    total = None
    for i in range(layout.tiles):
        r = start[block, i * tall : (i + 1) * tall, :].astype(f32)
        z = density[block, i * tall : (i + 1) * tall, :].astype(f32)
        rr, ri, zr, zi = r[:vectors], r[vectors:], z[:vectors], z[vectors:]
        terms = (rr * rr + ri * ri, rr * zr + ri * zi, rr * zi - ri * zr, zr * zr + zi * zi)
        total = terms if total is None else [a + b for a, b in zip(total, terms)]
    return total


def tree_sums(layout, start, density, block, count):
    if count == 1:
        return block_sums(layout, start, density, block)
    lower = tree_sums(layout, start, density, block, count // 2)
    upper = tree_sums(layout, start, density, block + count // 2, count // 2)
    return [a + b for a, b in zip(lower, upper)]


def scalar_kernel(layout, start, density, guess, factors):
    vectors = layout.vectors
    sums = tree_sums(layout, start, density, 0, layout.devices)
    squares, real, imag, rest = [
        jnp.broadcast_to(jnp.sum(value, 1, keepdims=True) * (1.0 / layout.panels), (vectors, lanes)) for value in sums
    ]
    hint = guess[...]
    scale_sq = squares + eps_norm
    coef_real = (real + hint * squares) / scale_sq
    coef_imag = imag / scale_sq
    more_real, more_imag = coef_real - hint, coef_imag
    update_sq = rest - 2.0 * (more_real * real + more_imag * imag) + (more_real * more_real + more_imag * more_imag) * squares
    scale = jnp.sqrt(scale_sq)
    update_scale = jnp.sqrt(jnp.maximum(update_sq, 0.0) / scale_sq + eps_norm)
    spot = lax.broadcasted_iota(jnp.int32, (vectors, lanes), 0)
    lane = lax.broadcasted_iota(jnp.int32, (vectors, lanes), 1)
    lines = [
        jnp.sum(jnp.where(spot == lane, value, 0.0), 0, keepdims=True)
        for value in (scale, coef_real, coef_imag, update_scale)
    ]
    lines.append(jnp.zeros((vectors - 4, lanes), f32))
    factors[...] = jnp.concatenate([more_real, more_imag, 1.0 / (scale * update_scale)] + lines, 0)


def second_kernel(layout, density, near, far_own, far_other, image, factors, result, scalars):
    vectors, tall = layout.vectors, 2 * layout.vectors
    more_real, more_imag = factors[:vectors, :], factors[vectors : 2 * vectors, :]
    inverse = factors[2 * vectors : 3 * vectors, :]
    scalars[...] = factors[3 * vectors : 3 * vectors + 4, :vectors]
    for i in range(layout.tiles):
        first = i * tall
        far_real, far_imag = far_rows(layout, i, far_own, far_other)
        own = density[first : first + tall, :].astype(f32)
        wr, wi = image[first : first + vectors, :], image[first + vectors : first + tall, :]
        real = 0.5 * own[:vectors] + near[first : first + vectors, :] + far_real
        imag = 0.5 * own[vectors:] + near[first + vectors : first + tall, :] + far_imag
        result[first : first + vectors, :] = (real - (more_real * wr - more_imag * wi)) * inverse
        result[first + vectors : first + tall, :] = (imag - (more_real * wi + more_imag * wr)) * inverse


def per_device(residual, kernel, offsets, neighbor, frequency, lattice_x, lattice_y, spectral_weight):
    strips, tiles_y, _, vectors, _ = residual.shape
    modes_x, modes_y = spectral_weight.shape[1:]
    layout = Layout(strips, tiles_y, vectors, modes_x)
    tiles, rows, devices = layout.tiles, layout.rows, layout.devices
    vmem = pl.BlockSpec(memory_space=pltpu.VMEM)
    shape = jax.ShapeDtypeStruct
    tall = 2 * vectors * 2 * layout.quarter
    wide = 4 * layout.half
    count = spectral_weight.shape[0]

    def call(body, name, out_shape, in_specs, limit, scratch=(), aliases=None):
        return pl.pallas_call(
            body,
            out_shape=out_shape,
            in_specs=in_specs,
            out_specs=jax.tree.map(lambda _: vmem, out_shape),
            scratch_shapes=scratch,
            input_output_aliases=aliases or {},
            compiler_params=pltpu.CompilerParams(vmem_limit_bytes=int(limit * mib)),
            cost_estimate=pl.CostEstimate(
                flops=int(lengths.get(name, 0) * 1e9), bytes_accessed=0, transcendentals=0
            ),
            name=name,
        )

    head = jnp.concatenate([residual.reshape(rows, lanes), offsets.reshape(2 * tiles, lanes)], 0)
    packed = call(
        lambda *refs: pack_kernel(layout, *refs),
        "pack",
        shape((rows + layout.offset_rows, lanes), bf16),
        [vmem],
        1,
    )(head)
    scale = 1.0 / math.sqrt(modes_x * modes_y * layout.panels)
    integers = jnp.stack([lattice_x, lattice_y, jnp.pad(frequency, (0, lanes - frequency.shape[0]))])

    def spectral(integers):
        return call(
            lambda *refs: spectral_kernel(layout, scale, *refs),
            "spectral",
            (shape((vectors, 2 * modes_y, modes_x), f32), shape((vectors, lanes), f32)),
            [vmem, vmem],
            4,
            [
                pltpu.SMEM((1, lanes), jnp.int32),
                pltpu.VMEM(spectral_weight.shape, f32),
                pltpu.SemaphoreType.DMA,
            ],
        )(integers, spectral_weight)

    blocks = kernel.reshape(tiles, 9, 2, lanes, lanes)
    neighbor = neighbor.reshape(tiles, 9)

    def table_shapes(size):
        return (
            shape((size // min(size, 4), wide, min(size, 4) * layout.local), bf16),
            shape((size, 2 * layout.quarter + 8, layout.local), f32),
        )

    def part_call(name, base, part, tables, total, halves, dtype):
        size = part.shape[0]
        high = len(halves) * tall // 2
        given = [part] + list(tables or ()) + ([] if total is None else [total])
        scratch = [pltpu.VMEM((high, min(size, 4) * layout.local), bf16)]
        if dtype != f32:
            scratch.append(pltpu.VMEM((high, wide), f32))
        with_start = total is not None
        return call(
            lambda *refs: part_kernel(layout, base, with_start, not tables, halves, *refs),
            name,
            (shape((high, wide), dtype), *(() if tables else table_shapes(size))),
            [vmem] * len(given),
            24,
            scratch,
            aliases={len(given) - 1: 0} if with_start and len(halves) == 2 else None,
        )(*given)

    def gather_and_project(array, tables):
        array = array[None]
        total, base, made, seen = None, 0, [], []
        for k, mask in enumerate(layout.chip_masks):
            pairs = [(i, i ^ mask) for i in range(devices)]
            arrived = lax.ppermute(array, ("tile", "wave"), pairs)
            array = jnp.concatenate([array, arrived])
            seen.append(array)
            part = arrived if k else array
            if k < len(layout.chip_masks) - 1:
                total, *new = part_call("part", base, part, tables and tables[k], total, (0, 1), f32)
                base += part.shape[0]
                made.append(new or tables[k])
        leaving, *new = part_call("leaving", base, part, tables and tables[-1], total, (1,), bf16)
        made.append(new or tables[-1])
        (staying,) = part_call("staying", base, part, made[-1], total, (0,), f32)
        return seen, leaving, staying, made

    def far_field(leaving, staying, weight, own_tables, other_tables):
        far_own, far_other = call(
            lambda *refs: far_kernel(layout, *refs),
            "far",
            tuple([shape((rows // 2, lanes), f32)] * 2),
            [vmem] * 7,
            24,
            [
                pltpu.VMEM((tall // 2, wide), f32),
                pltpu.VMEM((tall // 2, wide), bf16),
                pltpu.VMEM((tall // 2, layout.local), f32),
                pltpu.VMEM((tall // 2, layout.local), f32),
            ],
        )(staying, swap_cores(leaving), weight, *own_tables, *other_tables)
        return far_own, swap_cores(far_other)

    def near_field(density):
        return call(
            lambda *refs: near_kernel(layout, *refs),
            "near",
            shape((rows, lanes), f32),
            [vmem] * 3,
            12,
        )(density, blocks, neighbor)

    def with_other_core(array):
        return jnp.concatenate([array, swap_cores(array)])

    seen, leaving, staying, tables = gather_and_project(packed, None)
    other_tables = call(
        lambda *refs: table_kernel(layout, devices // 2, *refs),
        "other_tables",
        table_shapes(1),
        [vmem],
        8,
    )(swap_cores(after(packed, seen[0]))[None])
    weight, guess = spectral(after(integers, seen[1]))
    start = with_other_core(seen[-1])
    near_one = near_field(start)
    far_own, far_other = far_field(leaving, staying, weight, tables[0], other_tables)
    basis, image = call(
        lambda *refs: first_kernel(layout, *refs),
        "first",
        (shape((rows, lanes), bf16), shape((rows, lanes), f32)),
        [vmem] * 5,
        2,
    )(packed, near_one, far_own, far_other, guess)
    seen, leaving, staying, _ = gather_and_project(basis, tables)
    everything = with_other_core(seen[-1])
    factors = call(
        lambda *refs: scalar_kernel(layout, *refs),
        "scalars",
        shape((4 * vectors, lanes), f32),
        [vmem] * 3,
        1 + devices / 8,
    )(start, everything, guess)
    near_two = near_field(everything)
    far_own, far_other = far_field(leaving, after(staying, factors), weight, tables[0], other_tables)
    result, scalars = call(
        lambda *refs: second_kernel(layout, *refs),
        "second",
        (shape((rows, lanes), f32), shape((4, vectors), f32)),
        [vmem] * 6,
        2,
    )(basis, near_two, far_own, far_other, image, factors)
    return result.reshape(residual.shape), scalars


def solution(mesh):
    return jax.shard_map(
        per_device,
        mesh=mesh,
        in_specs=(
            P(("grp", "tile"), "wave", None, None, None),
            P(("grp", "tile"), "wave", None, None, None, None),
            P(("grp", "tile"), "wave", None, None),
            P(("grp", "tile"), "wave", None),
            P("grp"),
            P(),
            P(),
            P(),
        ),
        out_specs=(P(("grp", "tile"), "wave", None, None, None), P("grp", None)),
        check_vma=False,
    )
```

```python
import math

import jax
import jax.numpy as jnp
from jax import lax
from jax.experimental import pallas as pl
from jax.experimental.pallas import tpu as pltpu
from jax.sharding import PartitionSpec as P

eps_norm = 1e-06
lengths = {"part": 1, "leaving": 0.5, "staying": 0.8, "spectral": 2, "other_tables": 0.5, "far": 0.3, "near": 2}
f32 = jnp.float32
bf16 = jnp.bfloat16
lanes = 128
mib = 1024 * 1024

sine_terms = (6.283185160087918, -10.3354137577709, 5.100062753380459, -1.1960903419427114, 0.1544402466966843)
cosine_terms = (0.9999999534659573, -4.93479285858416, 4.058411912342187, -1.331880149557601, 0.21969677520430975)


def horner(terms, value):
    total = jnp.full_like(value, terms[-1])
    for term in terms[-2::-1]:
        total = total * value + term
    return total


def cos_sin(turns):
    turn = turns - jnp.round(turns)
    square = turn * turn
    double = turn * horner(sine_terms, square)
    return 1.0 - 0.5 * (double * double), double * horner(cosine_terms, square)


class Layout:
    def __init__(self, strips, tiles_y, vectors, modes):
        self.strips, self.tiles_y, self.vectors = strips, tiles_y, vectors
        self.tiles = strips * tiles_y
        self.columns, self.waves = lax.axis_size("tile"), lax.axis_size("wave")
        self.devices = self.columns * self.waves
        self.count_x, self.count_y = self.columns * strips, self.waves * tiles_y
        self.panels = self.count_x * self.count_y * lanes
        self.local = self.tiles * lanes
        self.rows = self.tiles * 2 * vectors
        self.offset_rows = -(-4 * self.tiles // 16) * 16
        self.part_v = vectors // 2
        self.half = modes // 2
        self.quarter = modes // 4
        chip_bits = (self.columns - 1).bit_length()
        assert self.columns == 1 << chip_bits and self.waves == 2
        self.chip_masks = [(1 << b) * self.waves + 1 for b in reversed(range(chip_bits))]
        self.masks = self.chip_masks + [1]

    def me(self):
        return lax.axis_index("tile") * self.waves + lax.axis_index("wave")

    def device_of(self, block):
        device = self.me()
        for k, mask in enumerate(self.masks):
            device = device ^ (((block >> k) & 1) * mask)
        return device

    def group_of(self, density):
        return min(density.shape[0], 4)

    def block_of(self, device):
        rest = device ^ self.me()
        block = 0
        for k, mask in enumerate(self.chip_masks):
            bit = (rest >> (mask.bit_length() - 1)) & 1
            block = block | (bit << k)
            rest = rest ^ (bit * mask)
        block = block | (rest << len(self.chip_masks))
        return block


def swap_cores(array):
    return lax.ppermute(array, "wave", [(0, 1), (1, 0)])


def after(value, *others):
    return lax.optimization_barrier((value, *others))[0]


def two_parts(value):
    first = value.astype(bf16)
    return first, (value - first.astype(f32)).astype(bf16)


def pack_kernel(layout, head, out):
    rows, count = layout.rows, 2 * layout.tiles
    out[:rows, :] = head[:rows, :].astype(bf16)
    first, second = two_parts(head[rows:, :])
    pieces = [first.astype(f32), second.astype(f32)]
    if layout.offset_rows > 2 * count:
        pieces.append(jnp.zeros((layout.offset_rows - 2 * count, lanes), f32))
    out[rows:, :] = jnp.concatenate(pieces, 0).astype(bf16)


def swap(value):
    return pltpu.roll(value, lanes // 2, 1)


def spectral_kernel(layout, scale, integers, table, out, guess, order, moved_all, sem):
    half, quarter = layout.half, layout.quarter
    size = 2 * half
    count = moved_all.shape[0]
    copy = pltpu.make_async_copy(integers.at[2:3], order, sem)
    copy.start()
    spot = lax.broadcasted_iota(jnp.int32, (size, size), 0)
    wanted = jnp.where(spot < half, spot + half, size - 1 - spot)
    pick_x, pick_y = [jnp.where(wanted == integers[k : k + 1], 1.0, 0.0).astype(bf16) for k in range(2)]
    pick_x, pick_y = [jnp.concatenate([pick, pick], 1) for pick in (pick_x, pick_y)]
    for f in range(0, count, 2):
        pair = range(f, min(f + 2, count))
        columns = [jnp.concatenate(two_parts(table[k] * scale), 0) for k in pair]
        moved = jnp.dot(pick_x, jnp.concatenate(columns, 1), preferred_element_type=f32)
        rows = [jnp.concatenate(two_parts(moved[:, n * size : (n + 1) * size]), 1) for n in range(len(pair))]
        moved = lax.dot_general(
            pick_y, jnp.concatenate(rows, 0), (((1,), (1,)), ((), ())), preferred_element_type=f32
        )
        for n, k in enumerate(pair):
            moved_all[k] = moved[:, n * size : (n + 1) * size]
    copy.wait()
    low = lax.broadcasted_iota(jnp.int32, (quarter, lanes), 1) < half
    rows = []
    for v in range(layout.vectors):
        moved = moved_all[order[0, v]]
        mean = jnp.sum(jnp.sum(moved, 0, keepdims=True), 1, keepdims=True)
        rows.append(jnp.broadcast_to(0.5 + mean, (1, lanes)))
        part = [moved[k * quarter : (k + 1) * quarter] for k in range(4)]
        for k, choices in enumerate((((1, 3), (0, 2)), ((2, 0), (3, 1)))):
            chosen = [jnp.where(low, part[one], part[other]) for one, other in choices]
            turned = [swap(value) for value in chosen]
            plus = jnp.where(low, chosen[0] + turned[0], chosen[1] + turned[1])
            minus = jnp.where(low, chosen[0] - turned[0], turned[1] - chosen[1])
            out[v, 2 * k * quarter : 2 * (k + 1) * quarter, :] = jnp.concatenate([plus, minus], 0)
    guess[...] = jnp.concatenate(rows, 0)


def make_tables(layout, base, group, k, density, table_x, table_y):
    tiles, half, quarter = layout.tiles, layout.half, layout.quarter
    block = layout.group_of(density) * group + k
    device = layout.device_of(base + block)
    column, row_index = device // layout.waves, device % layout.waves
    pieces = density[block, layout.rows :, :].astype(f32)
    offset = pieces[: 2 * tiles] + pieces[2 * tiles : 4 * tiles]
    eight = lax.broadcasted_iota(jnp.int32, (8, lanes), 0).astype(f32)
    coarse_y = jnp.where(eight < 4, quarter / 2 + 0.5 + 8 * eight, jnp.where(eight < 5, quarter / 2.0, 0.5))
    for i in range(tiles):
        g = (column * layout.strips + i // layout.tiles_y).astype(f32)
        h = (row_index * layout.tiles_y + i % layout.tiles_y).astype(f32)
        x = jnp.broadcast_to((offset[2 * i : 2 * i + 1] + g) * (1.0 / layout.count_x), (8, lanes))
        y = jnp.broadcast_to((offset[2 * i + 1 : 2 * i + 2] + h) * (1.0 / layout.count_y), (8, lanes))
        fine_xc, fine_xs = cos_sin(eight * x)
        big_xc, big_xs = cos_sin((8 * eight + 0.5) * x)
        fine_yc, fine_ys = cos_sin(eight * y)
        big_yc, big_ys = cos_sin(coarse_y * y + jnp.where(eight == 5, 0.5, 0.0) * x)
        shift_c, shift_s = big_yc[4:5], big_ys[4:5]
        span = slice(i * lanes, (i + 1) * lanes)
        wide = slice(k * layout.local + i * lanes, k * layout.local + (i + 1) * lanes)
        for e, sign in ((0, 1.0), (1, -1.0)):
            both_c = big_xc * shift_c - sign * (big_xs * shift_s)
            both_s = big_xs * shift_c + sign * (big_xc * shift_s)
            cosines, sines = [], []
            for a in range(half // 8):
                c, s = both_c[a : a + 1], both_s[a : a + 1]
                cosines.append(c * fine_xc - s * fine_xs)
                sines.append(s * fine_xc + c * fine_xs)
            table_x[group, half * e : half * (e + 1), wide] = jnp.concatenate(cosines, 0).astype(bf16)
            table_x[group, half * (e + 2) : half * (e + 3), wide] = jnp.concatenate(sines, 0).astype(bf16)
        cosines, sines = [], []
        for a in range(quarter // 8):
            c, s = big_yc[a : a + 1], big_ys[a : a + 1]
            cosines.append(c * fine_yc - s * fine_ys)
            sines.append(s * fine_yc + c * fine_ys)
        last = jnp.concatenate([big_yc[5:6], big_ys[5:6], jnp.zeros((6, lanes), f32)], 0)
        table_y[block, :, span] = jnp.concatenate(cosines + sines + [last], 0)


def pick_half(layout, rows, other):
    count = layout.part_v
    core = lax.axis_index("wave")
    upper = jnp.broadcast_to(1 - core if other else core, (count, lanes)) == 1
    return jnp.where(upper, rows[count:], rows[:count])


def both_halves(layout, own, other):
    upper = jnp.broadcast_to(lax.axis_index("wave"), own.shape) == 1
    return jnp.concatenate([jnp.where(upper, other, own), jnp.where(upper, own, other)], 0)


def twist(layout, block, k, density, table_y, out, halves):
    vectors, group = layout.vectors, 2 * layout.quarter
    for i in range(layout.tiles):
        span = slice(i * lanes, (i + 1) * lanes)
        wide = slice(k * layout.local + i * lanes, k * layout.local + (i + 1) * lanes)
        values = density[block, i * 2 * vectors : (i + 1) * 2 * vectors, :].astype(f32)
        waves = table_y[block, :group, span]
        c, s = table_y[block, group : group + 1, span], table_y[block, group + 1 : group + 2, span]
        start = 0
        for other in halves:
            real, imag = pick_half(layout, values[:vectors], other), pick_half(layout, values[vectors:], other)
            turned = (real * c - imag * s, imag * c + real * s)
            for v in range(layout.part_v):
                for part in range(2):
                    out[start : start + group, wide] = (turned[part][v : v + 1] * waves).astype(bf16)
                    start += group


def project(layout, base, density, table_x, table_y, twisted, total, start, halves, with_tables):
    size = layout.group_of(density)

    def step(group, before):
        for k in range(size):
            if with_tables:
                make_tables(layout, base, group, k, density, table_x, table_y)
            twist(layout, size * group + k, k, density, table_y, twisted, halves)
        product = lax.dot_general(
            twisted[...], table_x[group], (((1,), (1,)), ((), ())), preferred_element_type=f32
        )
        total[...] = product if before is None else before[...] + product

    step(0, start)
    groups = density.shape[0] // size
    if groups > 1:
        lax.fori_loop(1, groups, lambda group, carry: step(group, total) or carry, 0)


def part_kernel(layout, base, with_start, with_tables, halves, *refs):
    refs = list(refs)
    density = refs.pop(0)
    tables = None if with_tables else (refs.pop(0), refs.pop(0))
    start = refs.pop(0) if with_start else None
    total = refs.pop(0)
    table_x, table_y = tables or (refs.pop(0), refs.pop(0))
    twisted = refs.pop(0)
    if len(halves) == 1:
        size = twisted.shape[0]
        start = start.at[size * halves[0] : size * (halves[0] + 1)]
    held = refs.pop(0) if refs else total
    project(layout, base, density, table_x, table_y, twisted, held, start, halves, with_tables)
    if held is not total:
        total[...] = held[...].astype(total.dtype)


def table_kernel(layout, base, density, table_x, table_y):
    make_tables(layout, base, 0, 0, density, table_x, table_y)


def weigh(layout, total, weight, scaled):
    quarter = layout.quarter
    first = lax.axis_index("wave") * layout.part_v
    for v in range(layout.part_v):
        plus_sum, plus_rest, minus_sum, minus_rest = [
            weight[first + v, k * quarter : (k + 1) * quarter, :] for k in range(4)
        ]
        starts = [(4 * v + k) * quarter for k in range(4)]
        cc, cs = [[total[starts[2 * part + k] : starts[2 * part + k] + quarter, :lanes] for part in range(2)] for k in range(2)]
        sc, ss = [[total[starts[2 * part + k] : starts[2 * part + k] + quarter, lanes:] for part in range(2)] for k in range(2)]
        ur, ui = [cc[part] - ss[part] for part in range(2)]
        vr, vi = [sc[part] + cs[part] for part in range(2)]
        one = plus_sum * ur + plus_rest * vi, plus_sum * ui - plus_rest * vr
        one_sine = plus_sum * vr - plus_rest * ui, plus_sum * vi + plus_rest * ur
        ur, ui = [cc[part] + ss[part] for part in range(2)]
        vr, vi = [sc[part] - cs[part] for part in range(2)]
        two = minus_sum * ur + minus_rest * vi, minus_sum * ui - minus_rest * vr
        two_sine = minus_sum * vr - minus_rest * ui, minus_sum * vi + minus_rest * ur
        for part in range(2):
            cosine, sine = [slice(start, start + quarter) for start in starts[2 * part : 2 * part + 2]]
            scaled[cosine, :lanes] = (one[part] + two[part]).astype(bf16)
            scaled[cosine, lanes:] = (one_sine[part] + two_sine[part]).astype(bf16)
            scaled[sine, :lanes] = (one_sine[part] - two_sine[part]).astype(bf16)
            scaled[sine, lanes:] = (two[part] - one[part]).astype(bf16)


def expand(layout, scaled, table_x, table_y, summed, result):
    count, group = layout.part_v, 2 * layout.quarter
    summed[...] = jnp.dot(scaled[...], table_x[0, :, : layout.local], preferred_element_type=f32)
    for i in range(layout.tiles):
        span = slice(i * lanes, (i + 1) * lanes)
        waves = table_y[0, :group, span]
        rows = []
        for k in range(2 * count):
            rows.append(jnp.sum(summed[k * group : (k + 1) * group, span] * waves, 0, keepdims=True))
        real, imag = jnp.concatenate(rows[0::2], 0), jnp.concatenate(rows[1::2], 0)
        c, s = table_y[0, group : group + 1, span], table_y[0, group + 1 : group + 2, span]
        result[2 * count * i : 2 * count * (i + 1), :] = jnp.concatenate([real * c + imag * s, imag * c - real * s], 0)


def far_kernel(layout, own, arrived, weight, own_x, own_y, other_x, other_y, far_own, far_other, total, scaled, summed, summed_other):
    total[...] = own[...] + arrived[...].astype(f32)
    weigh(layout, total, weight, scaled)
    expand(layout, scaled, other_x, other_y, summed_other, far_other)
    expand(layout, scaled, own_x, own_y, summed, far_own)


def far_rows(layout, i, own, other):
    count = layout.part_v
    real, imag = [
        both_halves(layout, own[start : start + count, :], other[start : start + count, :])
        for start in (2 * count * i, 2 * count * i + count)
    ]
    return real, imag


def near_tile(layout, i, neighbor, density, kernel):
    vectors = layout.vectors
    g = lax.axis_index("tile") * layout.strips + i // layout.tiles_y
    h = lax.axis_index("wave") * layout.tiles_y + i % layout.tiles_y
    values = []
    for j in range(9):
        slot = neighbor[i, j]
        step_x = lax.div(slot, 3)
        gx = lax.rem(g + step_x - 1 + layout.count_x, layout.count_x)
        hy = lax.rem(h + slot - 3 * step_x - 1 + layout.count_y, layout.count_y)
        block = layout.block_of(lax.div(gx, layout.strips) * layout.waves + lax.div(hy, layout.tiles_y))
        tile = lax.rem(gx, layout.strips) * layout.tiles_y + lax.rem(hy, layout.tiles_y)
        start = pl.multiple_of(tile * 2 * vectors, 2 * vectors)
        values.append(density[block, pl.ds(start, 2 * vectors), :])
    total = 0.0
    for j in range(0, 9, 2):
        span = range(j, min(j + 2, 9))
        left = jnp.concatenate([values[k] for k in span], 1)
        right = jnp.concatenate([jnp.concatenate([kernel[i, k, 0], kernel[i, k, 1]], 1) for k in span], 0)
        total += jnp.dot(left, right, preferred_element_type=f32)
    upper, lower = total[:vectors], total[vectors:]
    return jnp.concatenate([upper[:, :lanes] - lower[:, lanes:], upper[:, lanes:] + lower[:, :lanes]], 0)


def near_kernel(layout, density, blocks, neighbor, out):
    places = neighbor[...]
    tall = 2 * layout.vectors
    for i in range(layout.tiles):
        out[i * tall : (i + 1) * tall, :] = near_tile(layout, i, places, density, blocks)


def first_kernel(layout, density, near, far_own, far_other, guess, basis, image):
    vectors, tall = layout.vectors, 2 * layout.vectors
    hint = guess[...]
    for i in range(layout.tiles):
        first = i * tall
        far_real, far_imag = far_rows(layout, i, far_own, far_other)
        own = density[first : first + tall, :].astype(f32)
        rr, ri = own[:vectors], own[vectors:]
        wr = 0.5 * rr + near[first : first + vectors, :] + far_real
        wi = 0.5 * ri + near[first + vectors : first + tall, :] + far_imag
        image[first : first + tall, :] = jnp.concatenate([wr, wi], 0)
        basis[first : first + tall, :] = jnp.concatenate([wr - hint * rr, wi - hint * ri], 0).astype(bf16)


def block_sums(layout, start, density, block):
    vectors, tall = layout.vectors, 2 * layout.vectors
    total = None
    for i in range(layout.tiles):
        r = start[block, i * tall : (i + 1) * tall, :].astype(f32)
        z = density[block, i * tall : (i + 1) * tall, :].astype(f32)
        rr, ri, zr, zi = r[:vectors], r[vectors:], z[:vectors], z[vectors:]
        terms = (rr * rr + ri * ri, rr * zr + ri * zi, rr * zi - ri * zr, zr * zr + zi * zi)
        total = terms if total is None else [a + b for a, b in zip(total, terms)]
    return total


def tree_sums(layout, start, density, block, count):
    if count == 1:
        return block_sums(layout, start, density, block)
    lower = tree_sums(layout, start, density, block, count // 2)
    upper = tree_sums(layout, start, density, block + count // 2, count // 2)
    return [a + b for a, b in zip(lower, upper)]


def scalar_kernel(layout, start, density, guess, factors):
    vectors = layout.vectors
    sums = tree_sums(layout, start, density, 0, layout.devices)
    squares, real, imag, rest = [
        jnp.broadcast_to(jnp.sum(value, 1, keepdims=True) * (1.0 / layout.panels), (vectors, lanes)) for value in sums
    ]
    hint = guess[...]
    scale_sq = squares + eps_norm
    coef_real = (real + hint * squares) / scale_sq
    coef_imag = imag / scale_sq
    more_real, more_imag = coef_real - hint, coef_imag
    update_sq = rest - 2.0 * (more_real * real + more_imag * imag) + (more_real * more_real + more_imag * more_imag) * squares
    scale = jnp.sqrt(scale_sq)
    update_scale = jnp.sqrt(jnp.maximum(update_sq, 0.0) / scale_sq + eps_norm)
    spot = lax.broadcasted_iota(jnp.int32, (vectors, lanes), 0)
    lane = lax.broadcasted_iota(jnp.int32, (vectors, lanes), 1)
    lines = [
        jnp.sum(jnp.where(spot == lane, value, 0.0), 0, keepdims=True)
        for value in (scale, coef_real, coef_imag, update_scale)
    ]
    lines.append(jnp.zeros((vectors - 4, lanes), f32))
    factors[...] = jnp.concatenate([more_real, more_imag, 1.0 / (scale * update_scale)] + lines, 0)


def second_kernel(layout, density, near, far_own, far_other, image, factors, result, scalars):
    vectors, tall = layout.vectors, 2 * layout.vectors
    more_real, more_imag = factors[:vectors, :], factors[vectors : 2 * vectors, :]
    inverse = factors[2 * vectors : 3 * vectors, :]
    scalars[...] = factors[3 * vectors : 3 * vectors + 4, :vectors]
    for i in range(layout.tiles):
        first = i * tall
        far_real, far_imag = far_rows(layout, i, far_own, far_other)
        own = density[first : first + tall, :].astype(f32)
        wr, wi = image[first : first + vectors, :], image[first + vectors : first + tall, :]
        real = 0.5 * own[:vectors] + near[first : first + vectors, :] + far_real
        imag = 0.5 * own[vectors:] + near[first + vectors : first + tall, :] + far_imag
        result[first : first + vectors, :] = (real - (more_real * wr - more_imag * wi)) * inverse
        result[first + vectors : first + tall, :] = (imag - (more_real * wi + more_imag * wr)) * inverse


def per_device(residual, kernel, offsets, neighbor, frequency, lattice_x, lattice_y, spectral_weight):
    strips, tiles_y, _, vectors, _ = residual.shape
    modes_x, modes_y = spectral_weight.shape[1:]
    layout = Layout(strips, tiles_y, vectors, modes_x)
    tiles, rows, devices = layout.tiles, layout.rows, layout.devices
    vmem = pl.BlockSpec(memory_space=pltpu.VMEM)
    shape = jax.ShapeDtypeStruct
    tall = 2 * vectors * 2 * layout.quarter
    wide = 4 * layout.half
    count = spectral_weight.shape[0]

    def call(body, name, out_shape, in_specs, limit, scratch=(), aliases=None):
        return pl.pallas_call(
            body,
            out_shape=out_shape,
            in_specs=in_specs,
            out_specs=jax.tree.map(lambda _: vmem, out_shape),
            scratch_shapes=scratch,
            input_output_aliases=aliases or {},
            compiler_params=pltpu.CompilerParams(vmem_limit_bytes=int(limit * mib)),
            cost_estimate=pl.CostEstimate(
                flops=int(lengths.get(name, 0) * 1e9), bytes_accessed=0, transcendentals=0
            ),
            name=name,
        )

    head = jnp.concatenate([residual.reshape(rows, lanes), offsets.reshape(2 * tiles, lanes)], 0)
    packed = call(
        lambda *refs: pack_kernel(layout, *refs),
        "pack",
        shape((rows + layout.offset_rows, lanes), bf16),
        [vmem],
        1,
    )(head)
    scale = 1.0 / math.sqrt(modes_x * modes_y * layout.panels)
    integers = jnp.stack([lattice_x, lattice_y, jnp.pad(frequency, (0, lanes - frequency.shape[0]))])

    def spectral(integers):
        return call(
            lambda *refs: spectral_kernel(layout, scale, *refs),
            "spectral",
            (shape((vectors, modes_y, modes_x), f32), shape((vectors, lanes), f32)),
            [vmem, vmem],
            4,
            [
                pltpu.SMEM((1, lanes), jnp.int32),
                pltpu.VMEM(spectral_weight.shape, f32),
                pltpu.SemaphoreType.DMA,
            ],
        )(integers, spectral_weight)

    blocks = kernel.reshape(tiles, 9, 2, lanes, lanes)
    neighbor = neighbor.reshape(tiles, 9)

    def table_shapes(size):
        return (
            shape((size // min(size, 4), wide, min(size, 4) * layout.local), bf16),
            shape((size, 2 * layout.quarter + 8, layout.local), f32),
        )

    def part_call(name, base, part, tables, total, halves, dtype):
        size = part.shape[0]
        high = len(halves) * tall // 2
        given = [part] + list(tables or ()) + ([] if total is None else [total])
        scratch = [pltpu.VMEM((high, min(size, 4) * layout.local), bf16)]
        if dtype != f32:
            scratch.append(pltpu.VMEM((high, wide), f32))
        with_start = total is not None
        return call(
            lambda *refs: part_kernel(layout, base, with_start, not tables, halves, *refs),
            name,
            (shape((high, wide), dtype), *(() if tables else table_shapes(size))),
            [vmem] * len(given),
            24,
            scratch,
            aliases={len(given) - 1: 0} if with_start and len(halves) == 2 else None,
        )(*given)

    def gather_and_project(array, tables):
        array = array[None]
        total, base, made, seen = None, 0, [], []
        for k, mask in enumerate(layout.chip_masks):
            pairs = [(i, i ^ mask) for i in range(devices)]
            arrived = lax.ppermute(array, ("tile", "wave"), pairs)
            array = jnp.concatenate([array, arrived])
            seen.append(array)
            part = arrived if k else array
            if k < len(layout.chip_masks) - 1:
                total, *new = part_call("part", base, part, tables and tables[k], total, (0, 1), f32)
                base += part.shape[0]
                made.append(new or tables[k])
        leaving, *new = part_call("leaving", base, part, tables and tables[-1], total, (1,), bf16)
        made.append(new or tables[-1])
        (staying,) = part_call("staying", base, part, made[-1], total, (0,), f32)
        return seen, leaving, staying, made

    def far_field(leaving, staying, weight, own_tables, other_tables):
        far_own, far_other = call(
            lambda *refs: far_kernel(layout, *refs),
            "far",
            tuple([shape((rows // 2, lanes), f32)] * 2),
            [vmem] * 7,
            24,
            [
                pltpu.VMEM((tall // 2, wide), f32),
                pltpu.VMEM((tall // 2, wide), bf16),
                pltpu.VMEM((tall // 2, layout.local), f32),
                pltpu.VMEM((tall // 2, layout.local), f32),
            ],
        )(staying, swap_cores(leaving), weight, *own_tables, *other_tables)
        return far_own, swap_cores(far_other)

    def near_field(density):
        return call(
            lambda *refs: near_kernel(layout, *refs),
            "near",
            shape((rows, lanes), f32),
            [vmem] * 3,
            12,
        )(density, blocks, neighbor)

    def with_other_core(array):
        return jnp.concatenate([array, swap_cores(array)])

    seen, leaving, staying, tables = gather_and_project(packed, None)
    other_tables = call(
        lambda *refs: table_kernel(layout, devices // 2, *refs),
        "other_tables",
        table_shapes(1),
        [vmem],
        8,
    )(swap_cores(after(packed, seen[0]))[None])
    weight, guess = spectral(after(integers, seen[1]))
    start = with_other_core(seen[-1])
    near_one = near_field(start)
    far_own, far_other = far_field(leaving, staying, weight, tables[0], other_tables)
    basis, image = call(
        lambda *refs: first_kernel(layout, *refs),
        "first",
        (shape((rows, lanes), bf16), shape((rows, lanes), f32)),
        [vmem] * 5,
        2,
    )(packed, near_one, far_own, far_other, guess)
    seen, leaving, staying, _ = gather_and_project(basis, tables)
    everything = with_other_core(seen[-1])
    factors = call(
        lambda *refs: scalar_kernel(layout, *refs),
        "scalars",
        shape((4 * vectors, lanes), f32),
        [vmem] * 3,
        1 + devices / 8,
    )(start, everything, guess)
    near_two = near_field(everything)
    far_own, far_other = far_field(leaving, after(staying, factors), weight, tables[0], other_tables)
    result, scalars = call(
        lambda *refs: second_kernel(layout, *refs),
        "second",
        (shape((rows, lanes), f32), shape((4, vectors), f32)),
        [vmem] * 6,
        2,
    )(basis, near_two, far_own, far_other, image, factors)
    return result.reshape(residual.shape), scalars


def solution(mesh):
    return jax.shard_map(
        per_device,
        mesh=mesh,
        in_specs=(
            P(("grp", "tile"), "wave", None, None, None),
            P(("grp", "tile"), "wave", None, None, None, None),
            P(("grp", "tile"), "wave", None, None),
            P(("grp", "tile"), "wave", None),
            P("grp"),
            P(),
            P(),
            P(),
        ),
        out_specs=(P(("grp", "tile"), "wave", None, None, None), P("grp", None)),
        check_vma=False,
    )
```

```python
import math

import jax
import jax.numpy as jnp
from jax import lax
from jax.experimental import pallas as pl
from jax.experimental.pallas import tpu as pltpu
from jax.sharding import PartitionSpec as P

eps_norm = 1e-06
lengths = {"part": 1, "leaving": 2, "staying": 0.8, "spectral": 2, "other_tables": 0.5, "far": 0.3, "near": 2, "tables": 0.5, "whole": 0.8}
f32 = jnp.float32
bf16 = jnp.bfloat16
lanes = 128
mib = 1024 * 1024

sine_terms = (6.283185160087918, -10.3354137577709, 5.100062753380459, -1.1960903419427114, 0.1544402466966843)
cosine_terms = (0.9999999534659573, -4.93479285858416, 4.058411912342187, -1.331880149557601, 0.21969677520430975)


def horner(terms, value):
    total = jnp.full_like(value, terms[-1])
    for term in terms[-2::-1]:
        total = total * value + term
    return total


def cos_sin(turns):
    turn = turns - jnp.round(turns)
    square = turn * turn
    double = turn * horner(sine_terms, square)
    return 1.0 - 0.5 * (double * double), double * horner(cosine_terms, square)


class Layout:
    def __init__(self, strips, tiles_y, vectors, modes):
        self.strips, self.tiles_y, self.vectors = strips, tiles_y, vectors
        self.tiles = strips * tiles_y
        self.columns, self.waves = lax.axis_size("tile"), lax.axis_size("wave")
        self.devices = self.columns * self.waves
        self.count_x, self.count_y = self.columns * strips, self.waves * tiles_y
        self.panels = self.count_x * self.count_y * lanes
        self.local = self.tiles * lanes
        self.rows = self.tiles * 2 * vectors
        self.offset_rows = -(-4 * self.tiles // 16) * 16
        self.part_v = vectors // 2
        self.half = modes // 2
        self.quarter = modes // 4
        chip_bits = (self.columns - 1).bit_length()
        assert self.columns == 1 << chip_bits and self.waves == 2
        self.chip_masks = [(1 << b) * self.waves + 1 for b in reversed(range(chip_bits))]
        self.masks = self.chip_masks + [1]

    def me(self):
        return lax.axis_index("tile") * self.waves + lax.axis_index("wave")

    def half_index(self):
        column, half = lax.axis_index("tile"), lax.axis_index("wave")
        for b in range(len(self.chip_masks)):
            half = half ^ ((column >> b) & 1)
        return half

    def device_of(self, block):
        device = self.me()
        for k, mask in enumerate(self.masks):
            device = device ^ (((block >> k) & 1) * mask)
        return device

    def group_of(self, density):
        return min(density.shape[0], 4)

    def block_of(self, device):
        rest = device ^ self.me()
        block = 0
        for k, mask in enumerate(self.chip_masks):
            bit = (rest >> (mask.bit_length() - 1)) & 1
            block = block | (bit << k)
            rest = rest ^ (bit * mask)
        block = block | (rest << len(self.chip_masks))
        return block


def swap_cores(array):
    return lax.ppermute(array, "wave", [(0, 1), (1, 0)])


def after(value, *others):
    return lax.optimization_barrier((value, *others))[0]


def two_parts(value):
    first = value.astype(bf16)
    return first, (value - first.astype(f32)).astype(bf16)


def pack_kernel(layout, head, out):
    rows, count = layout.rows, 2 * layout.tiles
    out[:rows, :] = head[:rows, :].astype(bf16)
    first, second = two_parts(head[rows:, :])
    pieces = [first.astype(f32), second.astype(f32)]
    if layout.offset_rows > 2 * count:
        pieces.append(jnp.zeros((layout.offset_rows - 2 * count, lanes), f32))
    out[rows:, :] = jnp.concatenate(pieces, 0).astype(bf16)


def swap(value):
    return pltpu.roll(value, lanes // 2, 1)


def spectral_kernel(layout, scale, integers, table, out, guess, order, moved_all, sem):
    half, quarter = layout.half, layout.quarter
    size = 2 * half
    count = moved_all.shape[0]
    copy = pltpu.make_async_copy(integers.at[2:3], order, sem)
    copy.start()
    spot = lax.broadcasted_iota(jnp.int32, (size, size), 0)
    wanted = jnp.where(spot < half, spot + half, size - 1 - spot)
    pick_x, pick_y = [jnp.where(wanted == integers[k : k + 1], 1.0, 0.0).astype(bf16) for k in range(2)]
    pick_x, pick_y = [jnp.concatenate([pick, pick], 1) for pick in (pick_x, pick_y)]
    for f in range(0, count, 2):
        pair = range(f, min(f + 2, count))
        columns = [jnp.concatenate(two_parts(table[k] * scale), 0) for k in pair]
        moved = jnp.dot(pick_x, jnp.concatenate(columns, 1), preferred_element_type=f32)
        rows = [jnp.concatenate(two_parts(moved[:, n * size : (n + 1) * size]), 1) for n in range(len(pair))]
        moved = lax.dot_general(
            pick_y, jnp.concatenate(rows, 0), (((1,), (1,)), ((), ())), preferred_element_type=f32
        )
        for n, k in enumerate(pair):
            moved_all[k] = moved[:, n * size : (n + 1) * size]
    copy.wait()
    low = lax.broadcasted_iota(jnp.int32, (quarter, lanes), 1) < half
    rows = []
    for v in range(layout.vectors):
        moved = moved_all[order[0, v]]
        mean = jnp.sum(jnp.sum(moved, 0, keepdims=True), 1, keepdims=True)
        rows.append(jnp.broadcast_to(0.5 + mean, (1, lanes)))
        part = [moved[k * quarter : (k + 1) * quarter] for k in range(4)]
        for k, choices in enumerate((((1, 3), (0, 2)), ((2, 0), (3, 1)))):
            chosen = [jnp.where(low, part[one], part[other]) for one, other in choices]
            turned = [swap(value) for value in chosen]
            plus = jnp.where(low, chosen[0] + turned[0], chosen[1] + turned[1])
            minus = jnp.where(low, chosen[0] - turned[0], turned[1] - chosen[1])
            out[v, 2 * k * quarter : 2 * (k + 1) * quarter, :] = jnp.concatenate([plus, minus], 0)
    guess[...] = jnp.concatenate(rows, 0)


def make_tables(layout, base, group, k, density, table_x, table_y):
    tiles, half, quarter = layout.tiles, layout.half, layout.quarter
    block = layout.group_of(density) * group + k
    device = layout.device_of(base + block)
    column, row_index = device // layout.waves, device % layout.waves
    pieces = density[block, layout.rows :, :].astype(f32)
    offset = pieces[: 2 * tiles] + pieces[2 * tiles : 4 * tiles]
    eight = lax.broadcasted_iota(jnp.int32, (8, lanes), 0).astype(f32)
    coarse_y = jnp.where(eight < 4, quarter / 2 + 0.5 + 8 * eight, jnp.where(eight < 5, quarter / 2.0, 0.5))
    for i in range(tiles):
        g = (column * layout.strips + i // layout.tiles_y).astype(f32)
        h = (row_index * layout.tiles_y + i % layout.tiles_y).astype(f32)
        x = jnp.broadcast_to((offset[2 * i : 2 * i + 1] + g) * (1.0 / layout.count_x), (8, lanes))
        y = jnp.broadcast_to((offset[2 * i + 1 : 2 * i + 2] + h) * (1.0 / layout.count_y), (8, lanes))
        fine_xc, fine_xs = cos_sin(eight * x)
        big_xc, big_xs = cos_sin((8 * eight + 0.5) * x)
        fine_yc, fine_ys = cos_sin(eight * y)
        big_yc, big_ys = cos_sin(coarse_y * y + jnp.where(eight == 5, 0.5, 0.0) * x)
        shift_c, shift_s = big_yc[4:5], big_ys[4:5]
        span = slice(i * lanes, (i + 1) * lanes)
        wide = slice(k * layout.local + i * lanes, k * layout.local + (i + 1) * lanes)
        for e, sign in ((0, 1.0), (1, -1.0)):
            both_c = big_xc * shift_c - sign * (big_xs * shift_s)
            both_s = big_xs * shift_c + sign * (big_xc * shift_s)
            cosines, sines = [], []
            for a in range(half // 8):
                c, s = both_c[a : a + 1], both_s[a : a + 1]
                cosines.append(c * fine_xc - s * fine_xs)
                sines.append(s * fine_xc + c * fine_xs)
            table_x[group, half * e : half * (e + 1), wide] = jnp.concatenate(cosines, 0).astype(bf16)
            table_x[group, half * (e + 2) : half * (e + 3), wide] = jnp.concatenate(sines, 0).astype(bf16)
        cosines, sines = [], []
        for a in range(quarter // 8):
            c, s = big_yc[a : a + 1], big_ys[a : a + 1]
            cosines.append(c * fine_yc - s * fine_ys)
            sines.append(s * fine_yc + c * fine_ys)
        last = jnp.concatenate([big_yc[5:6], big_ys[5:6], jnp.zeros((6, lanes), f32)], 0)
        table_y[block, :, span] = jnp.concatenate(cosines + sines + [last], 0)


def pick_half(layout, rows, other):
    count = layout.part_v
    core = layout.half_index()
    upper = jnp.broadcast_to(1 - core if other else core, (count, lanes)) == 1
    return jnp.where(upper, rows[count:], rows[:count])


def both_halves(layout, own, other):
    upper = jnp.broadcast_to(layout.half_index(), own.shape) == 1
    return jnp.concatenate([jnp.where(upper, other, own), jnp.where(upper, own, other)], 0)


def twist(layout, block, k, density, table_y, out, halves):
    vectors, group = layout.vectors, 2 * layout.quarter
    for i in range(layout.tiles):
        span = slice(i * lanes, (i + 1) * lanes)
        wide = slice(k * layout.local + i * lanes, k * layout.local + (i + 1) * lanes)
        values = density[block, i * 2 * vectors : (i + 1) * 2 * vectors, :].astype(f32)
        waves = table_y[block, :group, span]
        c, s = table_y[block, group : group + 1, span], table_y[block, group + 1 : group + 2, span]
        start = 0
        for other in halves:
            real, imag = pick_half(layout, values[:vectors], other), pick_half(layout, values[vectors:], other)
            turned = (real * c - imag * s, imag * c + real * s)
            for v in range(layout.part_v):
                for part in range(2):
                    out[start : start + group, wide] = (turned[part][v : v + 1] * waves).astype(bf16)
                    start += group


def project(layout, base, density, table_x, table_y, twisted, total, start, halves, with_tables):
    size = layout.group_of(density)

    def step(group, before):
        for k in range(size):
            if with_tables:
                make_tables(layout, base, group, k, density, table_x, table_y)
            twist(layout, size * group + k, k, density, table_y, twisted, halves)
        product = lax.dot_general(
            twisted[...], table_x[group], (((1,), (1,)), ((), ())), preferred_element_type=f32
        )
        total[...] = product if before is None else before[...] + product

    step(0, start)
    groups = density.shape[0] // size
    if groups > 1:
        lax.fori_loop(1, groups, lambda group, carry: step(group, total) or carry, 0)


def of_core(core, rows):
    return jnp.where(jnp.broadcast_to(core, (rows.shape[0] // 2, lanes)) == 1, rows[rows.shape[0] // 2 :], rows[: rows.shape[0] // 2])


def twist_chip(layout, block, core, k, density, table_y, out):
    count, group = layout.part_v, 2 * layout.quarter
    for i in range(layout.tiles):
        span = slice(i * lanes, (i + 1) * lanes)
        wide = slice(k * layout.local + i * lanes, k * layout.local + (i + 1) * lanes)
        values = of_core(core, density[block, i * 4 * count : (i + 1) * 4 * count, :].astype(f32))
        waves = table_y[block, :group, span]
        c, s = table_y[block, group : group + 1, span], table_y[block, group + 1 : group + 2, span]
        real, imag = values[:count], values[count:]
        turned = (real * c - imag * s, imag * c + real * s)
        for v in range(count):
            for part in range(2):
                start = (2 * v + part) * group
                out[start : start + group, wide] = (turned[part][v : v + 1] * waves).astype(bf16)


def chips_kernel(layout, base, with_start, density, own_x, own_y, other_x, other_y, *refs):
    start = refs[0] if with_start else None
    total, own_twisted, other_twisted = refs[-3:]
    size = layout.group_of(density)

    def step(group, before):
        for k in range(size):
            block = size * group + k
            core = layout.device_of(base + block) & 1
            twist_chip(layout, block, core, k, density, own_y, own_twisted)
            twist_chip(layout, block, 1 - core, k, density, other_y, other_twisted)
        product = 0.0
        for twisted, table in ((own_twisted, own_x), (other_twisted, other_x)):
            product = product + lax.dot_general(
                twisted[...], table[group], (((1,), (1,)), ((), ())), preferred_element_type=f32
            )
        total[...] = product if before is None else before[...] + product

    step(0, start)
    groups = density.shape[0] // size
    if groups > 1:
        lax.fori_loop(1, groups, lambda group, carry: step(group, total) or carry, 0)


def part_kernel(layout, base, with_start, with_tables, halves, *refs):
    refs = list(refs)
    density = refs.pop(0)
    tables = None if with_tables else (refs.pop(0), refs.pop(0))
    start = refs.pop(0) if with_start else None
    total = refs.pop(0)
    table_x, table_y = tables or (refs.pop(0), refs.pop(0))
    twisted = refs.pop(0)
    if len(halves) == 1:
        size = twisted.shape[0]
        start = start.at[size * halves[0] : size * (halves[0] + 1)]
    held = refs.pop(0) if refs else total
    project(layout, base, density, table_x, table_y, twisted, held, start, halves, with_tables)
    if held is not total:
        total[...] = held[...].astype(total.dtype)


def table_kernel(layout, base, density, table_x, table_y):
    size = layout.group_of(density)

    def step(group, carry):
        for k in range(size):
            make_tables(layout, base, group, k, density, table_x, table_y)
        return carry

    step(0, 0)
    groups = density.shape[0] // size
    if groups > 1:
        lax.fori_loop(1, groups, step, 0)


def weigh(layout, total, weight, scaled):
    quarter = layout.quarter
    first = layout.half_index() * layout.part_v
    for v in range(layout.part_v):
        plus_sum, plus_rest, minus_sum, minus_rest = [
            weight[first + v, k * quarter : (k + 1) * quarter, :] for k in range(4)
        ]
        starts = [(4 * v + k) * quarter for k in range(4)]
        cc, cs = [[total[starts[2 * part + k] : starts[2 * part + k] + quarter, :lanes] for part in range(2)] for k in range(2)]
        sc, ss = [[total[starts[2 * part + k] : starts[2 * part + k] + quarter, lanes:] for part in range(2)] for k in range(2)]
        ur, ui = [cc[part] - ss[part] for part in range(2)]
        vr, vi = [sc[part] + cs[part] for part in range(2)]
        one = plus_sum * ur + plus_rest * vi, plus_sum * ui - plus_rest * vr
        one_sine = plus_sum * vr - plus_rest * ui, plus_sum * vi + plus_rest * ur
        ur, ui = [cc[part] + ss[part] for part in range(2)]
        vr, vi = [sc[part] - cs[part] for part in range(2)]
        two = minus_sum * ur + minus_rest * vi, minus_sum * ui - minus_rest * vr
        two_sine = minus_sum * vr - minus_rest * ui, minus_sum * vi + minus_rest * ur
        for part in range(2):
            cosine, sine = [slice(start, start + quarter) for start in starts[2 * part : 2 * part + 2]]
            scaled[cosine, :lanes] = (one[part] + two[part]).astype(bf16)
            scaled[cosine, lanes:] = (one_sine[part] + two_sine[part]).astype(bf16)
            scaled[sine, :lanes] = (one_sine[part] - two_sine[part]).astype(bf16)
            scaled[sine, lanes:] = (two[part] - one[part]).astype(bf16)


def expand(layout, scaled, table_x, table_y, summed, result):
    count, group = layout.part_v, 2 * layout.quarter
    summed[...] = jnp.dot(scaled[...], table_x[0, :, : layout.local], preferred_element_type=f32)
    for i in range(layout.tiles):
        span = slice(i * lanes, (i + 1) * lanes)
        waves = table_y[0, :group, span]
        rows = []
        for k in range(2 * count):
            rows.append(jnp.sum(summed[k * group : (k + 1) * group, span] * waves, 0, keepdims=True))
        real, imag = jnp.concatenate(rows[0::2], 0), jnp.concatenate(rows[1::2], 0)
        c, s = table_y[0, group : group + 1, span], table_y[0, group + 1 : group + 2, span]
        result[2 * count * i : 2 * count * (i + 1), :] = jnp.concatenate([real * c + imag * s, imag * c - real * s], 0)


def far_kernel(layout, *refs):
    own, weight, own_x, own_y, other_x, other_y, far_own, far_other, total, scaled, summed, summed_other = refs[-12:]
    if len(refs) > 12:
        total[...] = own[...] + refs[0][...].astype(f32)
        own = total
    weigh(layout, own, weight, scaled)
    expand(layout, scaled, other_x, other_y, summed_other, far_other)
    expand(layout, scaled, own_x, own_y, summed, far_own)


def all_rows(layout, i, own, other):
    count = layout.part_v
    real, imag = [
        both_halves(layout, own[start : start + count, :], other[start : start + count, :])
        for start in (2 * count * i, 2 * count * i + count)
    ]
    return real, imag


def near_tile(layout, i, neighbor, values_of, kernel):
    g = lax.axis_index("tile") * layout.strips + i // layout.tiles_y
    h = lax.axis_index("wave") * layout.tiles_y + i % layout.tiles_y
    values = []
    for j in range(9):
        slot = neighbor[i, j]
        step_x = lax.div(slot, 3)
        gx = lax.rem(g + step_x - 1 + layout.count_x, layout.count_x)
        hy = lax.rem(h + slot - 3 * step_x - 1 + layout.count_y, layout.count_y)
        core = lax.div(hy, layout.tiles_y)
        block = layout.block_of(lax.div(gx, layout.strips) * layout.waves + core)
        tile = lax.rem(gx, layout.strips) * layout.tiles_y + lax.rem(hy, layout.tiles_y)
        values.append(values_of(block, core, pl.multiple_of(tile * 2 * layout.vectors, 2 * layout.vectors)))
    total = 0.0
    for j in range(0, 9, 2):
        span = range(j, min(j + 2, 9))
        left = jnp.concatenate([values[k] for k in span], 1)
        right = jnp.concatenate([jnp.concatenate([kernel[i, k, 0], kernel[i, k, 1]], 1) for k in span], 0)
        total += jnp.dot(left, right, preferred_element_type=f32)
    return total


def turn(upper, lower):
    return upper[:, :lanes] - lower[:, lanes:], upper[:, lanes:] + lower[:, :lanes]


def near_kernel(layout, whole, density, blocks, neighbor, near_own, near_other):
    places = neighbor[...]
    count, vectors, tall = layout.part_v, layout.vectors, 2 * layout.vectors
    chips = layout.devices // 2

    def of_device(block, core, start):
        return density[block, pl.ds(start, tall), :]

    def of_chip(block, core, start):
        chip = block & (chips - 1)
        parts = [density[chip + first, pl.ds(start, tall), :].astype(f32) for first in (0, chips)]
        return jnp.concatenate([of_core(core, part) for part in parts], 0).astype(bf16)

    for i in range(layout.tiles):
        total = near_tile(layout, i, places, of_device if whole else of_chip, blocks)
        span = slice(i * 2 * count, (i + 1) * 2 * count)
        if whole:
            parts = turn(total[:vectors], total[vectors:])
            near_own[span, :] = jnp.concatenate([pick_half(layout, part, False) for part in parts], 0)
            near_other[span, :] = jnp.concatenate([pick_half(layout, part, True) for part in parts], 0)
        else:
            near_own[span, :] = jnp.concatenate(turn(total[:count], total[count : 2 * count]), 0)
            near_other[span, :] = jnp.concatenate(turn(total[2 * count : 3 * count], total[3 * count :]), 0)


def first_kernel(layout, own, other, near_own, near_other, far_own, far_other, guess, basis, image_own, image_other):
    count, vectors, tall = layout.part_v, layout.vectors, 2 * layout.vectors
    hint = pick_half(layout, guess[...], False)
    core = lax.axis_index("wave")
    for i in range(layout.tiles):
        span = slice(i * 2 * count, (i + 1) * 2 * count)
        rests = []
        for density, near, far, image in ((own, near_own, far_own, image_own), (other, near_other, far_other, image_other)):
            values = density[i * tall : (i + 1) * tall, :].astype(f32)
            rr, ri = pick_half(layout, values[:vectors], False), pick_half(layout, values[vectors:], False)
            value = 0.5 * jnp.concatenate([rr, ri], 0) + near[span, :] + far[span, :]
            image[span, :] = value
            rests.append(value - jnp.concatenate([hint * rr, hint * ri], 0))
        upper = jnp.broadcast_to(core, rests[0].shape) == 1
        lines = [jnp.where(upper, rests[1], rests[0]), jnp.where(upper, rests[0], rests[1])]
        basis[i * tall : (i + 1) * tall, :] = jnp.concatenate(lines, 0).astype(bf16)


def chip_rows(layout, i, density, block, core):
    count, tall = layout.part_v, 2 * layout.vectors
    chips = layout.devices // 2
    halves = [
        of_core(core, density[block + first, i * tall : (i + 1) * tall, :].astype(f32)) for first in (0, chips)
    ]
    return [both_halves(layout, *[half[start : start + count] for half in halves]) for start in (0, count)]


def block_sums(layout, start, density, block):
    vectors, tall = layout.vectors, 2 * layout.vectors
    core = layout.device_of(block) & 1
    total = None
    for i in range(layout.tiles):
        r = start[block, i * tall : (i + 1) * tall, :].astype(f32)
        rr, ri = r[:vectors], r[vectors:]
        zr, zi = chip_rows(layout, i, density, block % (layout.devices // 2), core)
        terms = (rr * rr + ri * ri, rr * zr + ri * zi, rr * zi - ri * zr, zr * zr + zi * zi)
        total = terms if total is None else [a + b for a, b in zip(total, terms)]
    return total


def tree_sums(layout, start, density, block, count):
    if count == 1:
        return block_sums(layout, start, density, block)
    lower = tree_sums(layout, start, density, block, count // 2)
    upper = tree_sums(layout, start, density, block + count // 2, count // 2)
    return [a + b for a, b in zip(lower, upper)]


def scalar_kernel(layout, start, density, guess, factors):
    vectors = layout.vectors
    sums = tree_sums(layout, start, density, 0, layout.devices)
    squares, real, imag, rest = [
        jnp.broadcast_to(jnp.sum(value, 1, keepdims=True) * (1.0 / layout.panels), (vectors, lanes)) for value in sums
    ]
    hint = guess[...]
    scale_sq = squares + eps_norm
    coef_real = (real + hint * squares) / scale_sq
    coef_imag = imag / scale_sq
    more_real, more_imag = coef_real - hint, coef_imag
    update_sq = rest - 2.0 * (more_real * real + more_imag * imag) + (more_real * more_real + more_imag * more_imag) * squares
    scale = jnp.sqrt(scale_sq)
    update_scale = jnp.sqrt(jnp.maximum(update_sq, 0.0) / scale_sq + eps_norm)
    spot = lax.broadcasted_iota(jnp.int32, (vectors, lanes), 0)
    lane = lax.broadcasted_iota(jnp.int32, (vectors, lanes), 1)
    lines = [
        jnp.sum(jnp.where(spot == lane, value, 0.0), 0, keepdims=True)
        for value in (scale, coef_real, coef_imag, update_scale)
    ]
    lines.append(jnp.zeros((vectors - 4, lanes), f32))
    factors[...] = jnp.concatenate([more_real, more_imag, 1.0 / (scale * update_scale)] + lines, 0)


def second_kernel(layout, density, near_own, near_other, far_own, far_other, image_own, image_other, factors, result, scalars):
    vectors, tall = layout.vectors, 2 * layout.vectors
    more_real, more_imag = factors[:vectors, :], factors[vectors : 2 * vectors, :]
    inverse = factors[2 * vectors : 3 * vectors, :]
    scalars[...] = factors[3 * vectors : 3 * vectors + 4, :vectors]
    core = lax.axis_index("wave")
    for i in range(layout.tiles):
        first = i * tall
        far_real, far_imag = all_rows(layout, i, far_own, far_other)
        near_real, near_imag = all_rows(layout, i, near_own, near_other)
        wr, wi = all_rows(layout, i, image_own, image_other)
        zr, zi = chip_rows(layout, i, density, 0, core)
        real = 0.5 * zr + near_real + far_real
        imag = 0.5 * zi + near_imag + far_imag
        result[first : first + vectors, :] = (real - (more_real * wr - more_imag * wi)) * inverse
        result[first + vectors : first + tall, :] = (imag - (more_real * wi + more_imag * wr)) * inverse


def per_device(residual, kernel, offsets, neighbor, frequency, lattice_x, lattice_y, spectral_weight):
    strips, tiles_y, _, vectors, _ = residual.shape
    modes_x, modes_y = spectral_weight.shape[1:]
    layout = Layout(strips, tiles_y, vectors, modes_x)
    tiles, rows, devices = layout.tiles, layout.rows, layout.devices
    vmem = pl.BlockSpec(memory_space=pltpu.VMEM)
    shape = jax.ShapeDtypeStruct
    tall = 2 * vectors * 2 * layout.quarter
    wide = 4 * layout.half
    count = spectral_weight.shape[0]

    def call(body, name, out_shape, in_specs, limit, scratch=(), aliases=None):
        return pl.pallas_call(
            body,
            out_shape=out_shape,
            in_specs=in_specs,
            out_specs=jax.tree.map(lambda _: vmem, out_shape),
            scratch_shapes=scratch,
            input_output_aliases=aliases or {},
            compiler_params=pltpu.CompilerParams(vmem_limit_bytes=int(limit * mib)),
            cost_estimate=pl.CostEstimate(
                flops=int(lengths.get(name, 0) * 1e9), bytes_accessed=0, transcendentals=0
            ),
            name=name,
        )

    head = jnp.concatenate([residual.reshape(rows, lanes), offsets.reshape(2 * tiles, lanes)], 0)
    packed = call(
        lambda *refs: pack_kernel(layout, *refs),
        "pack",
        shape((rows + layout.offset_rows, lanes), bf16),
        [vmem],
        1,
    )(head)
    scale = 1.0 / math.sqrt(modes_x * modes_y * layout.panels)
    integers = jnp.stack([lattice_x, lattice_y, jnp.pad(frequency, (0, lanes - frequency.shape[0]))])

    def spectral(integers):
        return call(
            lambda *refs: spectral_kernel(layout, scale, *refs),
            "spectral",
            (shape((vectors, modes_y, modes_x), f32), shape((vectors, lanes), f32)),
            [vmem, vmem],
            4,
            [
                pltpu.SMEM((1, lanes), jnp.int32),
                pltpu.VMEM(spectral_weight.shape, f32),
                pltpu.SemaphoreType.DMA,
            ],
        )(integers, spectral_weight)

    blocks = kernel.reshape(tiles, 9, 2, lanes, lanes)
    neighbor = neighbor.reshape(tiles, 9)

    def table_shapes(size):
        return (
            shape((size // min(size, 4), wide, min(size, 4) * layout.local), bf16),
            shape((size, 2 * layout.quarter + 8, layout.local), f32),
        )

    def part_call(name, base, part, tables, total, halves, dtype):
        size = part.shape[0]
        high = len(halves) * tall // 2
        given = [part] + list(tables or ()) + ([] if total is None else [total])
        scratch = [pltpu.VMEM((high, min(size, 4) * layout.local), bf16)]
        if dtype != f32:
            scratch.append(pltpu.VMEM((high, wide), f32))
        with_start = total is not None
        return call(
            lambda *refs: part_kernel(layout, base, with_start, not tables, halves, *refs),
            name,
            (shape((high, wide), dtype), *(() if tables else table_shapes(size))),
            [vmem] * len(given),
            24,
            scratch,
            aliases={len(given) - 1: 0} if with_start and len(halves) == 2 else None,
        )(*given)

    def gather_and_project(array, tables):
        array = array[None]
        total, base, made, seen = None, 0, [], []
        for k, mask in enumerate(layout.chip_masks):
            pairs = [(i, i ^ mask) for i in range(devices)]
            arrived = lax.ppermute(array, ("tile", "wave"), pairs)
            array = jnp.concatenate([array, arrived])
            seen.append(array)
            part = arrived if k else array
            if k < len(layout.chip_masks) - 1:
                total, *new = part_call("part", base, part, tables and tables[k], total, (0, 1), f32)
                base += part.shape[0]
                made.append(new or tables[k])
        leaving, *new = part_call("leaving", base, part, tables and tables[-1], total, (1,), bf16)
        made.append(new or tables[-1])

        def stay(first):
            return part_call("staying", base, after(part, first), made[-1], total, (0,), f32)[0]

        return seen, leaving, stay, made

    def make(name, base, density):
        return call(
            lambda *refs: table_kernel(layout, base, *refs),
            name,
            table_shapes(density.shape[0]),
            [vmem],
            8,
        )(density)

    def gather_chips(array, tables, other):
        array = array[None]
        total, base, seen = None, 0, []
        for k, mask in enumerate(layout.chip_masks):
            pairs = [(i, i ^ mask) for i in range(devices)]
            arrived = lax.ppermute(array, ("tile", "wave"), pairs)
            array = jnp.concatenate([array, arrived])
            seen.append(array)
            part = arrived if k else array
            wait = seen[min(k, 1)]
            more = make("tables", devices // 2 + base, after(other, wait)[base : base + part.shape[0]])
            given = [part, *tables[k], *more] + ([] if total is None else [total])
            width = layout.group_of(part) * layout.local
            total = call(
                lambda *refs, base=base, start=total is not None: chips_kernel(layout, base, start, *refs),
                "part" if k < len(layout.chip_masks) - 1 else "whole",
                shape((tall // 2, wide), f32),
                [vmem] * len(given),
                24,
                [pltpu.VMEM((tall // 2, width), bf16)] * 2,
                aliases={} if total is None else {len(given) - 1: 0},
            )(*given)
            base += part.shape[0]
        return seen, total

    def far_field(sums, weight, own_tables, other_tables):
        return call(
            lambda *refs: far_kernel(layout, *refs),
            "far",
            tuple([shape((rows // 2, lanes), f32)] * 2),
            [vmem] * (5 + len(sums)),
            24,
            [
                pltpu.VMEM((tall // 2, wide), f32),
                pltpu.VMEM((tall // 2, wide), bf16),
                pltpu.VMEM((tall // 2, layout.local), f32),
                pltpu.VMEM((tall // 2, layout.local), f32),
            ],
        )(*sums, weight, *own_tables, *other_tables)

    def near_field(density, whole):
        return call(
            lambda *refs: near_kernel(layout, whole, *refs),
            "near",
            tuple([shape((rows // 2, lanes), f32)] * 2),
            [vmem] * 3,
            12,
        )(density, blocks, neighbor)

    def with_other_core(array):
        return jnp.concatenate([array, swap_cores(array)])

    seen, leaving, stay, tables = gather_and_project(packed, None)
    other_packed = swap_cores(after(packed, seen[0]))
    beside = make("other_tables", devices // 2, other_packed[None])
    weight, guess = spectral(after(integers, seen[1]))
    start = with_other_core(seen[-1])
    near_own, near_other = near_field(start, True)
    far_own, far_other = far_field((swap_cores(leaving), stay(near_own)), weight, tables[0], beside)
    basis, image_own, image_other = call(
        lambda *refs: first_kernel(layout, *refs),
        "first",
        (shape((rows, lanes), bf16), shape((rows // 2, lanes), f32), shape((rows // 2, lanes), f32)),
        [vmem] * 7,
        2,
    )(packed, other_packed, near_own, swap_cores(near_other), far_own, far_other, guess)
    seen, total = gather_chips(basis, tables, start[devices // 2 :])
    everything = with_other_core(seen[-1])
    factors = call(
        lambda *refs: scalar_kernel(layout, *refs),
        "scalars",
        shape((4 * vectors, lanes), f32),
        [vmem] * 3,
        1 + devices / 8,
    )(start, everything, guess)
    near_own, near_other = near_field(everything, False)
    far_own, far_other = far_field((total,), weight, tables[0], beside)
    result, scalars = call(
        lambda *refs: second_kernel(layout, *refs),
        "second",
        (shape((rows, lanes), f32), shape((4, vectors), f32)),
        [vmem] * 8,
        2,
    )(
        everything,
        near_own,
        near_other,
        far_own,
        swap_cores(far_other),
        image_own,
        swap_cores(image_other),
        factors,
    )
    return result.reshape(residual.shape), scalars


def solution(mesh):
    return jax.shard_map(
        per_device,
        mesh=mesh,
        in_specs=(
            P(("grp", "tile"), "wave", None, None, None),
            P(("grp", "tile"), "wave", None, None, None, None),
            P(("grp", "tile"), "wave", None, None),
            P(("grp", "tile"), "wave", None),
            P("grp"),
            P(),
            P(),
            P(),
        ),
        out_specs=(P(("grp", "tile"), "wave", None, None, None), P("grp", None)),
        check_vma=False,
    )
```

```python
import math

import jax
import jax.numpy as jnp
from jax import lax
from jax.experimental import pallas as pl
from jax.experimental.pallas import tpu as pltpu
from jax.sharding import PartitionSpec as P

eps_norm = 1e-06
lengths = {"part": 1, "leaving": 2, "staying": 0.8, "spectral": 2, "other_tables": 0.5, "far": 0.3, "near": 2, "tables": 0.5, "whole": 0.8}
f32 = jnp.float32
bf16 = jnp.bfloat16
lanes = 128
mib = 1024 * 1024

sine_terms = (6.283185160087918, -10.3354137577709, 5.100062753380459, -1.1960903419427114, 0.1544402466966843)
cosine_terms = (0.9999999534659573, -4.93479285858416, 4.058411912342187, -1.331880149557601, 0.21969677520430975)


def horner(terms, value):
    total = jnp.full_like(value, terms[-1])
    for term in terms[-2::-1]:
        total = total * value + term
    return total


def cos_sin(turns):
    turn = turns - jnp.round(turns)
    square = turn * turn
    double = turn * horner(sine_terms, square)
    return 1.0 - 0.5 * (double * double), double * horner(cosine_terms, square)


class Layout:
    def __init__(self, strips, tiles_y, vectors, modes):
        self.strips, self.tiles_y, self.vectors = strips, tiles_y, vectors
        self.tiles = strips * tiles_y
        self.columns, self.waves = lax.axis_size("tile"), lax.axis_size("wave")
        self.devices = self.columns * self.waves
        self.count_x, self.count_y = self.columns * strips, self.waves * tiles_y
        self.panels = self.count_x * self.count_y * lanes
        self.local = self.tiles * lanes
        self.rows = self.tiles * 2 * vectors
        self.offset_rows = -(-4 * self.tiles // 16) * 16
        self.part_v = vectors // 2
        self.x_bits, self.y_bits = (strips - 1).bit_length(), (tiles_y - 1).bit_length()
        assert strips == 1 << self.x_bits and tiles_y == 1 << self.y_bits
        self.half = modes // 2
        self.quarter = modes // 4
        chip_bits = (self.columns - 1).bit_length()
        assert self.columns == 1 << chip_bits and self.waves == 2
        self.chip_masks = [(1 << b) * self.waves + 1 for b in reversed(range(chip_bits))]
        self.masks = self.chip_masks + [1]

    def me(self):
        return lax.axis_index("tile") * self.waves + lax.axis_index("wave")

    def half_index(self):
        column, half = lax.axis_index("tile"), lax.axis_index("wave")
        for b in range(len(self.chip_masks)):
            half = half ^ ((column >> b) & 1)
        return half

    def device_of(self, block):
        device = self.me()
        for k, mask in enumerate(self.masks):
            device = device ^ (((block >> k) & 1) * mask)
        return device

    def group_of(self, density):
        return min(density.shape[0], 4)

    def block_of(self, device):
        rest = device ^ self.me()
        block = 0
        for k, mask in enumerate(self.chip_masks):
            bit = (rest >> (mask.bit_length() - 1)) & 1
            block = block | (bit << k)
            rest = rest ^ (bit * mask)
        block = block | (rest << len(self.chip_masks))
        return block


def swap_cores(array):
    return lax.ppermute(array, "wave", [(0, 1), (1, 0)])


def after(value, *others):
    return lax.optimization_barrier((value, *others))[0]


def two_parts(value):
    first = value.astype(bf16)
    return first, (value - first.astype(f32)).astype(bf16)


def pack_kernel(layout, head, out):
    rows, count = layout.rows, 2 * layout.tiles
    out[:rows, :] = head[:rows, :].astype(bf16)
    first, second = two_parts(head[rows:, :])
    pieces = [first.astype(f32), second.astype(f32)]
    if layout.offset_rows > 2 * count:
        pieces.append(jnp.zeros((layout.offset_rows - 2 * count, lanes), f32))
    out[rows:, :] = jnp.concatenate(pieces, 0).astype(bf16)


def swap(value):
    return pltpu.roll(value, lanes // 2, 1)


def spectral_kernel(layout, scale, integers, table, out, guess, order, moved_all, sem):
    half, quarter = layout.half, layout.quarter
    size = 2 * half
    count = moved_all.shape[0]
    copy = pltpu.make_async_copy(integers.at[2:3], order, sem)
    copy.start()
    spot = lax.broadcasted_iota(jnp.int32, (size, size), 0)
    wanted = jnp.where(spot < half, spot + half, size - 1 - spot)
    pick_x, pick_y = [jnp.where(wanted == integers[k : k + 1], 1.0, 0.0).astype(bf16) for k in range(2)]
    pick_x, pick_y = [jnp.concatenate([pick, pick], 1) for pick in (pick_x, pick_y)]
    for f in range(0, count, 2):
        pair = range(f, min(f + 2, count))
        columns = [jnp.concatenate(two_parts(table[k] * scale), 0) for k in pair]
        moved = jnp.dot(pick_x, jnp.concatenate(columns, 1), preferred_element_type=f32)
        rows = [jnp.concatenate(two_parts(moved[:, n * size : (n + 1) * size]), 1) for n in range(len(pair))]
        moved = lax.dot_general(
            pick_y, jnp.concatenate(rows, 0), (((1,), (1,)), ((), ())), preferred_element_type=f32
        )
        for n, k in enumerate(pair):
            moved_all[k] = moved[:, n * size : (n + 1) * size]
    copy.wait()
    low = lax.broadcasted_iota(jnp.int32, (quarter, lanes), 1) < half
    rows = []
    for v in range(layout.vectors):
        moved = moved_all[order[0, v]]
        mean = jnp.sum(jnp.sum(moved, 0, keepdims=True), 1, keepdims=True)
        rows.append(jnp.broadcast_to(0.5 + mean, (1, lanes)))
        part = [moved[k * quarter : (k + 1) * quarter] for k in range(4)]
        for k, choices in enumerate((((1, 3), (0, 2)), ((2, 0), (3, 1)))):
            chosen = [jnp.where(low, part[one], part[other]) for one, other in choices]
            turned = [swap(value) for value in chosen]
            plus = jnp.where(low, chosen[0] + turned[0], chosen[1] + turned[1])
            minus = jnp.where(low, chosen[0] - turned[0], turned[1] - chosen[1])
            out[v, 2 * k * quarter : 2 * (k + 1) * quarter, :] = jnp.concatenate([plus, minus], 0)
    guess[...] = jnp.concatenate(rows, 0)


def climb(start, step, count):
    (c, s), (step_c, step_s) = start, step
    cosines, sines = [c], [s]
    for _ in range(count - 1):
        c, s = c * step_c - s * step_s, s * step_c + c * step_s
        cosines.append(c)
        sines.append(s)
    return jnp.concatenate(cosines, 0), jnp.concatenate(sines, 0)


def make_tables(layout, base, group, k, density, table_x, table_y):
    tiles, half, quarter = layout.tiles, layout.half, layout.quarter
    block = layout.group_of(density) * group + k
    device = layout.device_of(base + block)
    column, row_index = device // layout.waves, device % layout.waves
    pieces = density[block, layout.rows :, :].astype(f32)
    spot = lax.broadcasted_iota(jnp.int32, (2 * tiles, lanes), 0)
    along_x = (spot & 1) == 0
    tile = spot >> 1
    corner = jnp.where(
        along_x,
        column * layout.strips + (tile >> layout.y_bits),
        row_index * layout.tiles_y + (tile & (layout.tiles_y - 1)),
    )
    size = jnp.where(along_x, 1.0 / layout.count_x, 1.0 / layout.count_y)
    position = (pieces[: 2 * tiles] + pieces[2 * tiles : 4 * tiles] + corner.astype(f32)) * size
    steps = cos_sin(8.0 * position)
    phases = cos_sin(0.5 * (position + pltpu.roll(position, 2 * tiles - 1, 0)))
    eight = lax.broadcasted_iota(jnp.int32, (8, lanes), 0).astype(f32) + 0.5

    def row(array, index):
        return jnp.broadcast_to(array[index : index + 1], (8, lanes))

    for i in range(tiles):
        x, y = row(position, 2 * i), row(position, 2 * i + 1)
        step_x, step_y = [[row(step, 2 * i + n) for step in steps] for n in range(2)]
        span = slice(i * lanes, (i + 1) * lanes)
        wide = slice(k * layout.local + i * lanes, k * layout.local + (i + 1) * lanes)
        for e, shift in ((0, quarter / 2), (1, -quarter / 2)):
            cosines, sines = climb(cos_sin(eight * x + shift * y), step_x, half // 8)
            table_x[group, half * e : half * (e + 1), wide] = cosines.astype(bf16)
            table_x[group, half * (e + 2) : half * (e + 3), wide] = sines.astype(bf16)
        cosines, sines = climb(cos_sin((eight + quarter / 2) * y), step_y, quarter // 8)
        last = [phase[2 * i : 2 * i + 1] for phase in phases]
        table_y[block, :, span] = jnp.concatenate([cosines, sines] + last + [jnp.zeros((6, lanes), f32)], 0)


def pick_half(layout, rows, other):
    count = layout.part_v
    core = layout.half_index()
    upper = jnp.broadcast_to(1 - core if other else core, (count, lanes)) == 1
    return jnp.where(upper, rows[count:], rows[:count])


def both_halves(layout, own, other):
    upper = jnp.broadcast_to(layout.half_index(), own.shape) == 1
    return jnp.concatenate([jnp.where(upper, other, own), jnp.where(upper, own, other)], 0)


def twist(layout, block, k, density, table_y, out, halves):
    vectors, group = layout.vectors, 2 * layout.quarter
    for i in range(layout.tiles):
        span = slice(i * lanes, (i + 1) * lanes)
        wide = slice(k * layout.local + i * lanes, k * layout.local + (i + 1) * lanes)
        values = density[block, i * 2 * vectors : (i + 1) * 2 * vectors, :].astype(f32)
        waves = table_y[block, :group, span]
        c, s = table_y[block, group : group + 1, span], table_y[block, group + 1 : group + 2, span]
        start = 0
        for other in halves:
            real, imag = pick_half(layout, values[:vectors], other), pick_half(layout, values[vectors:], other)
            turned = (real * c - imag * s, imag * c + real * s)
            for v in range(layout.part_v):
                for part in range(2):
                    out[start : start + group, wide] = (turned[part][v : v + 1] * waves).astype(bf16)
                    start += group


def project(layout, base, density, table_x, table_y, twisted, total, start, halves, with_tables):
    size = layout.group_of(density)

    def step(group, before):
        for k in range(size):
            if with_tables:
                make_tables(layout, base, group, k, density, table_x, table_y)
            twist(layout, size * group + k, k, density, table_y, twisted, halves)
        product = lax.dot_general(
            twisted[...], table_x[group], (((1,), (1,)), ((), ())), preferred_element_type=f32
        )
        total[...] = product if before is None else before[...] + product

    step(0, start)
    groups = density.shape[0] // size
    if groups > 1:
        lax.fori_loop(1, groups, lambda group, carry: step(group, total) or carry, 0)


def of_core(core, rows):
    return jnp.where(jnp.broadcast_to(core, (rows.shape[0] // 2, lanes)) == 1, rows[rows.shape[0] // 2 :], rows[: rows.shape[0] // 2])


def twist_chip(layout, block, core, k, density, table_y, out):
    count, group = layout.part_v, 2 * layout.quarter
    for i in range(layout.tiles):
        span = slice(i * lanes, (i + 1) * lanes)
        wide = slice(k * layout.local + i * lanes, k * layout.local + (i + 1) * lanes)
        values = of_core(core, density[block, i * 4 * count : (i + 1) * 4 * count, :].astype(f32))
        waves = table_y[block, :group, span]
        c, s = table_y[block, group : group + 1, span], table_y[block, group + 1 : group + 2, span]
        real, imag = values[:count], values[count:]
        turned = (real * c - imag * s, imag * c + real * s)
        for v in range(count):
            for part in range(2):
                start = (2 * v + part) * group
                out[start : start + group, wide] = (turned[part][v : v + 1] * waves).astype(bf16)


def chips_kernel(layout, base, with_start, density, own_x, own_y, other_x, other_y, *refs):
    start = refs[0] if with_start else None
    total, own_twisted, other_twisted = refs[-3:]
    size = layout.group_of(density)

    def step(group, before):
        for k in range(size):
            block = size * group + k
            core = layout.device_of(base + block) & 1
            twist_chip(layout, block, core, k, density, own_y, own_twisted)
            twist_chip(layout, block, 1 - core, k, density, other_y, other_twisted)
        product = 0.0
        for twisted, table in ((own_twisted, own_x), (other_twisted, other_x)):
            product = product + lax.dot_general(
                twisted[...], table[group], (((1,), (1,)), ((), ())), preferred_element_type=f32
            )
        total[...] = product if before is None else before[...] + product

    step(0, start)
    groups = density.shape[0] // size
    if groups > 1:
        lax.fori_loop(1, groups, lambda group, carry: step(group, total) or carry, 0)


def part_kernel(layout, base, with_start, with_tables, halves, *refs):
    refs = list(refs)
    density = refs.pop(0)
    tables = None if with_tables else (refs.pop(0), refs.pop(0))
    start = refs.pop(0) if with_start else None
    total = refs.pop(0)
    table_x, table_y = tables or (refs.pop(0), refs.pop(0))
    twisted = refs.pop(0)
    if len(halves) == 1:
        size = twisted.shape[0]
        start = start.at[size * halves[0] : size * (halves[0] + 1)]
    held = refs.pop(0) if refs else total
    project(layout, base, density, table_x, table_y, twisted, held, start, halves, with_tables)
    if held is not total:
        total[...] = held[...].astype(total.dtype)


def table_kernel(layout, base, density, table_x, table_y):
    size = layout.group_of(density)

    def step(group, carry):
        for k in range(size):
            make_tables(layout, base, group, k, density, table_x, table_y)
        return carry

    step(0, 0)
    groups = density.shape[0] // size
    if groups > 1:
        lax.fori_loop(1, groups, step, 0)


def weigh(layout, total, weight, scaled):
    quarter = layout.quarter
    first = layout.half_index() * layout.part_v
    for v in range(layout.part_v):
        plus_sum, plus_rest, minus_sum, minus_rest = [
            weight[first + v, k * quarter : (k + 1) * quarter, :] for k in range(4)
        ]
        starts = [(4 * v + k) * quarter for k in range(4)]
        cc, cs = [[total[starts[2 * part + k] : starts[2 * part + k] + quarter, :lanes] for part in range(2)] for k in range(2)]
        sc, ss = [[total[starts[2 * part + k] : starts[2 * part + k] + quarter, lanes:] for part in range(2)] for k in range(2)]
        ur, ui = [cc[part] - ss[part] for part in range(2)]
        vr, vi = [sc[part] + cs[part] for part in range(2)]
        one = plus_sum * ur + plus_rest * vi, plus_sum * ui - plus_rest * vr
        one_sine = plus_sum * vr - plus_rest * ui, plus_sum * vi + plus_rest * ur
        ur, ui = [cc[part] + ss[part] for part in range(2)]
        vr, vi = [sc[part] - cs[part] for part in range(2)]
        two = minus_sum * ur + minus_rest * vi, minus_sum * ui - minus_rest * vr
        two_sine = minus_sum * vr - minus_rest * ui, minus_sum * vi + minus_rest * ur
        for part in range(2):
            cosine, sine = [slice(start, start + quarter) for start in starts[2 * part : 2 * part + 2]]
            scaled[cosine, :lanes] = (one[part] + two[part]).astype(bf16)
            scaled[cosine, lanes:] = (one_sine[part] + two_sine[part]).astype(bf16)
            scaled[sine, :lanes] = (one_sine[part] - two_sine[part]).astype(bf16)
            scaled[sine, lanes:] = (two[part] - one[part]).astype(bf16)


def expand(layout, scaled, table_x, table_y, summed, result):
    count, group = layout.part_v, 2 * layout.quarter
    summed[...] = jnp.dot(scaled[...], table_x[0, :, : layout.local], preferred_element_type=f32)
    for i in range(layout.tiles):
        span = slice(i * lanes, (i + 1) * lanes)
        waves = table_y[0, :group, span]
        rows = []
        for k in range(2 * count):
            rows.append(jnp.sum(summed[k * group : (k + 1) * group, span] * waves, 0, keepdims=True))
        real, imag = jnp.concatenate(rows[0::2], 0), jnp.concatenate(rows[1::2], 0)
        c, s = table_y[0, group : group + 1, span], table_y[0, group + 1 : group + 2, span]
        result[2 * count * i : 2 * count * (i + 1), :] = jnp.concatenate([real * c + imag * s, imag * c - real * s], 0)


def far_kernel(layout, *refs):
    own, weight, own_x, own_y, other_x, other_y, far_own, far_other, total, scaled, summed, summed_other = refs[-12:]
    if len(refs) > 12:
        total[...] = own[...] + refs[0][...].astype(f32)
        own = total
    weigh(layout, own, weight, scaled)
    expand(layout, scaled, other_x, other_y, summed_other, far_other)
    expand(layout, scaled, own_x, own_y, summed, far_own)


def all_rows(layout, i, own, other):
    count = layout.part_v
    real, imag = [
        both_halves(layout, own[start : start + count, :], other[start : start + count, :])
        for start in (2 * count * i, 2 * count * i + count)
    ]
    return real, imag


def near_places(layout, neighbor, block_rows, mask):
    tile = lax.broadcasted_iota(jnp.int32, neighbor.shape, 0)
    step_x = (neighbor * 11) >> 5
    gx = lax.axis_index("tile") * layout.strips + (tile >> layout.y_bits) + step_x - 1
    hy = lax.axis_index("wave") * layout.tiles_y + (tile & (layout.tiles_y - 1)) + neighbor - 3 * step_x - 1
    gx, hy = gx & (layout.count_x - 1), hy & (layout.count_y - 1)
    core = hy >> layout.y_bits
    block = layout.block_of((gx >> layout.x_bits) * layout.waves + core) & mask
    source = ((gx & (layout.strips - 1)) << layout.y_bits) + (hy & (layout.tiles_y - 1))
    return 2 * (block * block_rows + source * 2 * layout.vectors) + core


def near_tile(layout, i, places, values_of, kernel):
    values = [values_of(places[i, j]) for j in range(9)]
    total = 0.0
    for j in range(0, 9, 2):
        span = range(j, min(j + 2, 9))
        left = jnp.concatenate([values[k] for k in span], 1)
        right = jnp.concatenate([jnp.concatenate([kernel[i, k, 0], kernel[i, k, 1]], 1) for k in span], 0)
        total += jnp.dot(left, right, preferred_element_type=f32)
    return total


def turn(upper, lower):
    return upper[:, :lanes] - lower[:, lanes:], upper[:, lanes:] + lower[:, :lanes]


def near_kernel(layout, whole, density, blocks, neighbor, near_own, near_other):
    count, vectors, tall = layout.part_v, layout.vectors, 2 * layout.vectors
    chips = layout.devices // 2
    block_rows = density.shape[0] // layout.devices
    places = near_places(layout, neighbor[...], block_rows, layout.devices - 1 if whole else chips - 1)

    def of_device(place):
        return density[pl.ds(pl.multiple_of(place >> 1, tall), tall), :]

    def of_chip(place):
        start = place >> 1
        parts = [
            density[pl.ds(pl.multiple_of(start + first, tall), tall), :].astype(f32) for first in (0, chips * block_rows)
        ]
        return jnp.concatenate([of_core(place & 1, part) for part in parts], 0).astype(bf16)

    for i in range(layout.tiles):
        total = near_tile(layout, i, places, of_device if whole else of_chip, blocks)
        span = slice(i * 2 * count, (i + 1) * 2 * count)
        if whole:
            parts = turn(total[:vectors], total[vectors:])
            near_own[span, :] = jnp.concatenate([pick_half(layout, part, False) for part in parts], 0)
            near_other[span, :] = jnp.concatenate([pick_half(layout, part, True) for part in parts], 0)
        else:
            near_own[span, :] = jnp.concatenate(turn(total[:count], total[count : 2 * count]), 0)
            near_other[span, :] = jnp.concatenate(turn(total[2 * count : 3 * count], total[3 * count :]), 0)


def first_kernel(layout, own, other, near_own, near_other, far_own, far_other, guess, basis, image_own, image_other):
    count, vectors, tall = layout.part_v, layout.vectors, 2 * layout.vectors
    hint = pick_half(layout, guess[...], False)
    core = lax.axis_index("wave")
    for i in range(layout.tiles):
        span = slice(i * 2 * count, (i + 1) * 2 * count)
        rests = []
        for density, near, far, image in ((own, near_own, far_own, image_own), (other, near_other, far_other, image_other)):
            values = density[i * tall : (i + 1) * tall, :].astype(f32)
            rr, ri = pick_half(layout, values[:vectors], False), pick_half(layout, values[vectors:], False)
            value = 0.5 * jnp.concatenate([rr, ri], 0) + near[span, :] + far[span, :]
            image[span, :] = value
            rests.append(value - jnp.concatenate([hint * rr, hint * ri], 0))
        upper = jnp.broadcast_to(core, rests[0].shape) == 1
        lines = [jnp.where(upper, rests[1], rests[0]), jnp.where(upper, rests[0], rests[1])]
        basis[i * tall : (i + 1) * tall, :] = jnp.concatenate(lines, 0).astype(bf16)


def chip_rows(layout, i, density, block, core):
    count, tall = layout.part_v, 2 * layout.vectors
    chips = layout.devices // 2
    halves = [
        of_core(core, density[block + first, i * tall : (i + 1) * tall, :].astype(f32)) for first in (0, chips)
    ]
    return [both_halves(layout, *[half[start : start + count] for half in halves]) for start in (0, count)]


def chip_sums(layout, start, density, chip):
    vectors, tall, count = layout.vectors, 2 * layout.vectors, layout.part_v
    chips = layout.devices // 2
    swapped = layout.device_of(chip) & 1
    half = layout.half_index()
    upper = lax.broadcasted_iota(jnp.int32, (vectors, lanes), 0) >= count
    total = None
    for i in range(layout.tiles):
        span = slice(i * tall, (i + 1) * tall)
        low, high = [density[chip + chips * which, span, :].astype(f32) for which in (half, 1 - half)]
        for core in range(2):
            r = start[chip + chips * (core ^ swapped), span, :].astype(f32)
            rr, ri = r[:vectors], r[vectors:]
            one, two = [z[core * vectors : (core + 1) * vectors] for z in (low, high)]
            zr = jnp.where(upper, pltpu.roll(two, count, 0), one)
            zi = jnp.where(upper, two, pltpu.roll(one, count, 0))
            terms = (rr * rr + ri * ri, rr * zr + ri * zi, rr * zi - ri * zr, zr * zr + zi * zi)
            total = terms if total is None else [a + b for a, b in zip(total, terms)]
    return total


def tree_sums(layout, start, density, chip, count):
    if count == 1:
        return chip_sums(layout, start, density, chip)
    lower = tree_sums(layout, start, density, chip, count // 2)
    upper = tree_sums(layout, start, density, chip + count // 2, count // 2)
    return [a + b for a, b in zip(lower, upper)]


def scalar_kernel(layout, start, density, guess, factors):
    vectors = layout.vectors
    sums = tree_sums(layout, start, density, 0, layout.devices // 2)
    squares, real, imag, rest = [
        jnp.broadcast_to(jnp.sum(value, 1, keepdims=True) * (1.0 / layout.panels), (vectors, lanes)) for value in sums
    ]
    hint = guess[...]
    scale_sq = squares + eps_norm
    coef_real = (real + hint * squares) / scale_sq
    coef_imag = imag / scale_sq
    more_real, more_imag = coef_real - hint, coef_imag
    update_sq = rest - 2.0 * (more_real * real + more_imag * imag) + (more_real * more_real + more_imag * more_imag) * squares
    scale = jnp.sqrt(scale_sq)
    update_scale = jnp.sqrt(jnp.maximum(update_sq, 0.0) / scale_sq + eps_norm)
    spot = lax.broadcasted_iota(jnp.int32, (vectors, lanes), 0)
    lane = lax.broadcasted_iota(jnp.int32, (vectors, lanes), 1)
    lines = [
        jnp.sum(jnp.where(spot == lane, value, 0.0), 0, keepdims=True)
        for value in (scale, coef_real, coef_imag, update_scale)
    ]
    lines.append(jnp.zeros((vectors - 4, lanes), f32))
    factors[...] = jnp.concatenate([more_real, more_imag, 1.0 / (scale * update_scale)] + lines, 0)


def second_kernel(layout, density, near_own, near_other, far_own, far_other, image_own, image_other, factors, result, scalars):
    vectors, tall = layout.vectors, 2 * layout.vectors
    more_real, more_imag = factors[:vectors, :], factors[vectors : 2 * vectors, :]
    inverse = factors[2 * vectors : 3 * vectors, :]
    scalars[...] = factors[3 * vectors : 3 * vectors + 4, :vectors]
    core = lax.axis_index("wave")
    for i in range(layout.tiles):
        first = i * tall
        far_real, far_imag = all_rows(layout, i, far_own, far_other)
        near_real, near_imag = all_rows(layout, i, near_own, near_other)
        wr, wi = all_rows(layout, i, image_own, image_other)
        zr, zi = chip_rows(layout, i, density, 0, core)
        real = 0.5 * zr + near_real + far_real
        imag = 0.5 * zi + near_imag + far_imag
        result[first : first + vectors, :] = (real - (more_real * wr - more_imag * wi)) * inverse
        result[first + vectors : first + tall, :] = (imag - (more_real * wi + more_imag * wr)) * inverse


def per_device(residual, kernel, offsets, neighbor, frequency, lattice_x, lattice_y, spectral_weight):
    strips, tiles_y, _, vectors, _ = residual.shape
    modes_x, modes_y = spectral_weight.shape[1:]
    layout = Layout(strips, tiles_y, vectors, modes_x)
    tiles, rows, devices = layout.tiles, layout.rows, layout.devices
    vmem = pl.BlockSpec(memory_space=pltpu.VMEM)
    shape = jax.ShapeDtypeStruct
    tall = 2 * vectors * 2 * layout.quarter
    wide = 4 * layout.half
    count = spectral_weight.shape[0]

    def call(body, name, out_shape, in_specs, limit, scratch=(), aliases=None):
        return pl.pallas_call(
            body,
            out_shape=out_shape,
            in_specs=in_specs,
            out_specs=jax.tree.map(lambda _: vmem, out_shape),
            scratch_shapes=scratch,
            input_output_aliases=aliases or {},
            compiler_params=pltpu.CompilerParams(vmem_limit_bytes=int(limit * mib)),
            cost_estimate=pl.CostEstimate(
                flops=int(lengths.get(name, 0) * 1e9), bytes_accessed=0, transcendentals=0
            ),
            name=name,
        )

    head = jnp.concatenate([residual.reshape(rows, lanes), offsets.reshape(2 * tiles, lanes)], 0)
    packed = call(
        lambda *refs: pack_kernel(layout, *refs),
        "pack",
        shape((rows + layout.offset_rows, lanes), bf16),
        [vmem],
        1,
    )(head)
    scale = 1.0 / math.sqrt(modes_x * modes_y * layout.panels)
    integers = jnp.stack([lattice_x, lattice_y, jnp.pad(frequency, (0, lanes - frequency.shape[0]))])

    def spectral(integers):
        return call(
            lambda *refs: spectral_kernel(layout, scale, *refs),
            "spectral",
            (shape((vectors, modes_y, modes_x), f32), shape((vectors, lanes), f32)),
            [vmem, vmem],
            4,
            [
                pltpu.SMEM((1, lanes), jnp.int32),
                pltpu.VMEM(spectral_weight.shape, f32),
                pltpu.SemaphoreType.DMA,
            ],
        )(integers, spectral_weight)

    blocks = kernel.reshape(tiles, 9, 2, lanes, lanes)
    neighbor = neighbor.reshape(tiles, 9)

    def table_shapes(size):
        return (
            shape((size // min(size, 4), wide, min(size, 4) * layout.local), bf16),
            shape((size, 2 * layout.quarter + 8, layout.local), f32),
        )

    def part_call(name, base, part, tables, total, halves, dtype):
        size = part.shape[0]
        high = len(halves) * tall // 2
        given = [part] + list(tables or ()) + ([] if total is None else [total])
        scratch = [pltpu.VMEM((high, min(size, 4) * layout.local), bf16)]
        if dtype != f32:
            scratch.append(pltpu.VMEM((high, wide), f32))
        with_start = total is not None
        return call(
            lambda *refs: part_kernel(layout, base, with_start, not tables, halves, *refs),
            name,
            (shape((high, wide), dtype), *(() if tables else table_shapes(size))),
            [vmem] * len(given),
            24,
            scratch,
            aliases={len(given) - 1: 0} if with_start and len(halves) == 2 else None,
        )(*given)

    def gather_and_project(array, tables):
        array = array[None]
        total, base, made, seen = None, 0, [], []
        for k, mask in enumerate(layout.chip_masks):
            pairs = [(i, i ^ mask) for i in range(devices)]
            arrived = lax.ppermute(array, ("tile", "wave"), pairs)
            array = jnp.concatenate([array, arrived])
            seen.append(array)
            part = arrived if k else array
            if k < len(layout.chip_masks) - 1:
                total, *new = part_call("part", base, part, tables and tables[k], total, (0, 1), f32)
                base += part.shape[0]
                made.append(new or tables[k])
        leaving, *new = part_call("leaving", base, part, tables and tables[-1], total, (1,), bf16)
        made.append(new or tables[-1])

        def stay(first):
            return part_call("staying", base, after(part, first), made[-1], total, (0,), f32)[0]

        return seen, leaving, stay, made

    def make(name, base, density):
        return call(
            lambda *refs: table_kernel(layout, base, *refs),
            name,
            table_shapes(density.shape[0]),
            [vmem],
            8,
        )(density)

    def gather_chips(array, tables, other):
        array = array[None]
        total, base, seen = None, 0, []
        for k, mask in enumerate(layout.chip_masks):
            pairs = [(i, i ^ mask) for i in range(devices)]
            arrived = lax.ppermute(array, ("tile", "wave"), pairs)
            array = jnp.concatenate([array, arrived])
            seen.append(array)
            part = arrived if k else array
            wait = seen[min(k, 1)]
            more = make("tables", devices // 2 + base, after(other, wait)[base : base + part.shape[0]])
            given = [part, *tables[k], *more] + ([] if total is None else [total])
            width = layout.group_of(part) * layout.local
            total = call(
                lambda *refs, base=base, start=total is not None: chips_kernel(layout, base, start, *refs),
                "part" if k < len(layout.chip_masks) - 1 else "whole",
                shape((tall // 2, wide), f32),
                [vmem] * len(given),
                24,
                [pltpu.VMEM((tall // 2, width), bf16)] * 2,
                aliases={} if total is None else {len(given) - 1: 0},
            )(*given)
            base += part.shape[0]
        return seen, total

    def far_field(sums, weight, own_tables, other_tables):
        return call(
            lambda *refs: far_kernel(layout, *refs),
            "far",
            tuple([shape((rows // 2, lanes), f32)] * 2),
            [vmem] * (5 + len(sums)),
            24,
            [
                pltpu.VMEM((tall // 2, wide), f32),
                pltpu.VMEM((tall // 2, wide), bf16),
                pltpu.VMEM((tall // 2, layout.local), f32),
                pltpu.VMEM((tall // 2, layout.local), f32),
            ],
        )(*sums, weight, *own_tables, *other_tables)

    def near_field(density, whole):
        return call(
            lambda *refs: near_kernel(layout, whole, *refs),
            "near",
            tuple([shape((rows // 2, lanes), f32)] * 2),
            [vmem] * 3,
            12,
        )(density.reshape(-1, lanes), blocks, neighbor)

    def with_other_core(array):
        return jnp.concatenate([array, swap_cores(array)])

    seen, leaving, stay, tables = gather_and_project(packed, None)
    other_packed = swap_cores(after(packed, seen[0]))
    beside = make("other_tables", devices // 2, other_packed[None])
    weight, guess = spectral(after(integers, seen[1]))
    start = with_other_core(seen[-1])
    near_own, near_other = near_field(start, True)
    far_own, far_other = far_field((swap_cores(leaving), stay(near_own)), weight, tables[0], beside)
    basis, image_own, image_other = call(
        lambda *refs: first_kernel(layout, *refs),
        "first",
        (shape((rows, lanes), bf16), shape((rows // 2, lanes), f32), shape((rows // 2, lanes), f32)),
        [vmem] * 7,
        2,
    )(packed, other_packed, near_own, swap_cores(near_other), far_own, far_other, guess)
    seen, total = gather_chips(basis, tables, start[devices // 2 :])
    everything = with_other_core(seen[-1])
    factors = call(
        lambda *refs: scalar_kernel(layout, *refs),
        "scalars",
        shape((4 * vectors, lanes), f32),
        [vmem] * 3,
        1 + devices / 8,
    )(start, everything, guess)
    near_own, near_other = near_field(everything, False)
    far_own, far_other = far_field((total,), weight, tables[0], beside)
    result, scalars = call(
        lambda *refs: second_kernel(layout, *refs),
        "second",
        (shape((rows, lanes), f32), shape((4, vectors), f32)),
        [vmem] * 8,
        2,
    )(
        everything,
        near_own,
        near_other,
        far_own,
        swap_cores(far_other),
        image_own,
        swap_cores(image_other),
        factors,
    )
    return result.reshape(residual.shape), scalars


def solution(mesh):
    return jax.shard_map(
        per_device,
        mesh=mesh,
        in_specs=(
            P(("grp", "tile"), "wave", None, None, None),
            P(("grp", "tile"), "wave", None, None, None, None),
            P(("grp", "tile"), "wave", None, None),
            P(("grp", "tile"), "wave", None),
            P("grp"),
            P(),
            P(),
            P(),
        ),
        out_specs=(P(("grp", "tile"), "wave", None, None, None), P("grp", None)),
        check_vma=False,
    )
```

```python
import math

import jax
import jax.numpy as jnp
from jax import lax
from jax.experimental import pallas as pl
from jax.experimental.pallas import tpu as pltpu
from jax.sharding import PartitionSpec as P

eps_norm = 1e-06
lengths = {"part": 1, "leaving": 0.5, "staying": 0.8, "spectral": 2, "other_tables": 0.5, "far": 0.3, "near": 2, "tables": 0.5, "whole": 0.8}
f32 = jnp.float32
bf16 = jnp.bfloat16
lanes = 128
mib = 1024 * 1024

sine_terms = (6.283185160087918, -10.3354137577709, 5.100062753380459, -1.1960903419427114, 0.1544402466966843)
cosine_terms = (0.9999999534659573, -4.93479285858416, 4.058411912342187, -1.331880149557601, 0.21969677520430975)


def horner(terms, value):
    total = jnp.full_like(value, terms[-1])
    for term in terms[-2::-1]:
        total = total * value + term
    return total


def cos_sin(turns):
    turn = turns - jnp.round(turns)
    square = turn * turn
    double = turn * horner(sine_terms, square)
    return 1.0 - 0.5 * (double * double), double * horner(cosine_terms, square)


class Layout:
    def __init__(self, strips, tiles_y, vectors, modes):
        self.strips, self.tiles_y, self.vectors = strips, tiles_y, vectors
        self.tiles = strips * tiles_y
        self.columns, self.waves = lax.axis_size("tile"), lax.axis_size("wave")
        self.devices = self.columns * self.waves
        self.count_x, self.count_y = self.columns * strips, self.waves * tiles_y
        self.panels = self.count_x * self.count_y * lanes
        self.local = self.tiles * lanes
        self.rows = self.tiles * 2 * vectors
        self.offset_rows = -(-4 * self.tiles // 16) * 16
        self.part_v = vectors // 2
        self.x_bits, self.y_bits = (strips - 1).bit_length(), (tiles_y - 1).bit_length()
        assert strips == 1 << self.x_bits and tiles_y == 1 << self.y_bits
        self.half = modes // 2
        self.quarter = modes // 4
        chip_bits = (self.columns - 1).bit_length()
        assert self.columns == 1 << chip_bits and self.waves == 2
        self.chip_masks = [(1 << b) * self.waves + 1 for b in reversed(range(chip_bits))]
        self.masks = self.chip_masks + [1]

    def me(self):
        return lax.axis_index("tile") * self.waves + lax.axis_index("wave")

    def half_index(self):
        column, half = lax.axis_index("tile"), lax.axis_index("wave")
        for b in range(len(self.chip_masks)):
            half = half ^ ((column >> b) & 1)
        return half

    def device_of(self, block):
        device = self.me()
        for k, mask in enumerate(self.masks):
            device = device ^ (((block >> k) & 1) * mask)
        return device

    def group_of(self, density):
        return min(density.shape[0], 4)

    def block_of(self, device):
        rest = device ^ self.me()
        block = 0
        for k, mask in enumerate(self.chip_masks):
            bit = (rest >> (mask.bit_length() - 1)) & 1
            block = block | (bit << k)
            rest = rest ^ (bit * mask)
        block = block | (rest << len(self.chip_masks))
        return block


def swap_cores(array):
    return lax.ppermute(array, "wave", [(0, 1), (1, 0)])


def after(value, *others):
    return lax.optimization_barrier((value, *others))[0]


def two_parts(value):
    first = value.astype(bf16)
    return first, (value - first.astype(f32)).astype(bf16)


def pack_kernel(layout, head, out):
    rows, count = layout.rows, 2 * layout.tiles
    out[:rows, :] = head[:rows, :].astype(bf16)
    first, second = two_parts(head[rows:, :])
    pieces = [first.astype(f32), second.astype(f32)]
    if layout.offset_rows > 2 * count:
        pieces.append(jnp.zeros((layout.offset_rows - 2 * count, lanes), f32))
    out[rows:, :] = jnp.concatenate(pieces, 0).astype(bf16)


def swap(value):
    return pltpu.roll(value, lanes // 2, 1)


def spectral_kernel(layout, scale, integers, table, out, guess, order, moved_all, sem):
    half, quarter = layout.half, layout.quarter
    size = 2 * half
    count = moved_all.shape[0]
    copy = pltpu.make_async_copy(integers.at[2:3], order, sem)
    copy.start()
    spot = lax.broadcasted_iota(jnp.int32, (size, size), 0)
    wanted = jnp.where(spot < half, spot + half, size - 1 - spot)
    pick_x, pick_y = [jnp.where(wanted == integers[k : k + 1], 1.0, 0.0).astype(bf16) for k in range(2)]
    pick_x, pick_y = [jnp.concatenate([pick, pick], 1) for pick in (pick_x, pick_y)]
    for f in range(0, count, 2):
        pair = range(f, min(f + 2, count))
        columns = [jnp.concatenate(two_parts(table[k] * scale), 0) for k in pair]
        moved = jnp.dot(pick_x, jnp.concatenate(columns, 1), preferred_element_type=f32)
        rows = [jnp.concatenate(two_parts(moved[:, n * size : (n + 1) * size]), 1) for n in range(len(pair))]
        moved = lax.dot_general(
            pick_y, jnp.concatenate(rows, 0), (((1,), (1,)), ((), ())), preferred_element_type=f32
        )
        for n, k in enumerate(pair):
            moved_all[k] = moved[:, n * size : (n + 1) * size]
    copy.wait()
    low = lax.broadcasted_iota(jnp.int32, (quarter, lanes), 1) < half
    rows = []
    for v in range(layout.vectors):
        moved = moved_all[order[0, v]]
        mean = jnp.sum(jnp.sum(moved, 0, keepdims=True), 1, keepdims=True)
        rows.append(jnp.broadcast_to(0.5 + mean, (1, lanes)))
        part = [moved[k * quarter : (k + 1) * quarter] for k in range(4)]
        for k, choices in enumerate((((1, 3), (0, 2)), ((2, 0), (3, 1)))):
            chosen = [jnp.where(low, part[one], part[other]) for one, other in choices]
            turned = [swap(value) for value in chosen]
            plus = jnp.where(low, chosen[0] + turned[0], chosen[1] + turned[1])
            minus = jnp.where(low, chosen[0] - turned[0], turned[1] - chosen[1])
            out[v, 2 * k * quarter : 2 * (k + 1) * quarter, :] = jnp.concatenate([plus, minus], 0)
    guess[...] = jnp.concatenate(rows, 0)


def climb(start, step, count):
    (c, s), (step_c, step_s) = start, step
    cosines, sines = [c], [s]
    for _ in range(count - 1):
        c, s = c * step_c - s * step_s, s * step_c + c * step_s
        cosines.append(c)
        sines.append(s)
    return jnp.concatenate(cosines, 0), jnp.concatenate(sines, 0)


def make_tables(layout, base, group, k, density, table_x, table_y):
    tiles, half, quarter = layout.tiles, layout.half, layout.quarter
    block = layout.group_of(density) * group + k
    device = layout.device_of(base + block)
    column, row_index = device // layout.waves, device % layout.waves
    pieces = density[block, layout.rows :, :].astype(f32)
    spot = lax.broadcasted_iota(jnp.int32, (2 * tiles, lanes), 0)
    along_x = (spot & 1) == 0
    tile = spot >> 1
    corner = jnp.where(
        along_x,
        column * layout.strips + (tile >> layout.y_bits),
        row_index * layout.tiles_y + (tile & (layout.tiles_y - 1)),
    )
    size = jnp.where(along_x, 1.0 / layout.count_x, 1.0 / layout.count_y)
    position = (pieces[: 2 * tiles] + pieces[2 * tiles : 4 * tiles] + corner.astype(f32)) * size
    steps = cos_sin(8.0 * position)
    phases = cos_sin(0.5 * (position + pltpu.roll(position, 2 * tiles - 1, 0)))
    eight = lax.broadcasted_iota(jnp.int32, (8, lanes), 0).astype(f32) + 0.5

    def row(array, index):
        return jnp.broadcast_to(array[index : index + 1], (8, lanes))

    for i in range(tiles):
        x, y = row(position, 2 * i), row(position, 2 * i + 1)
        step_x, step_y = [[row(step, 2 * i + n) for step in steps] for n in range(2)]
        span = slice(i * lanes, (i + 1) * lanes)
        wide = slice(k * layout.local + i * lanes, k * layout.local + (i + 1) * lanes)
        for e, shift in ((0, quarter / 2), (1, -quarter / 2)):
            cosines, sines = climb(cos_sin(eight * x + shift * y), step_x, half // 8)
            table_x[group, half * e : half * (e + 1), wide] = cosines.astype(bf16)
            table_x[group, half * (e + 2) : half * (e + 3), wide] = sines.astype(bf16)
        cosines, sines = climb(cos_sin((eight + quarter / 2) * y), step_y, quarter // 8)
        last = [phase[2 * i : 2 * i + 1] for phase in phases]
        table_y[block, :, span] = jnp.concatenate([cosines, sines] + last + [jnp.zeros((6, lanes), f32)], 0)


def pick_half(layout, rows, other):
    count = layout.part_v
    core = layout.half_index()
    upper = jnp.broadcast_to(1 - core if other else core, (count, lanes)) == 1
    return jnp.where(upper, rows[count:], rows[:count])


def both_halves(layout, own, other):
    upper = jnp.broadcast_to(layout.half_index(), own.shape) == 1
    return jnp.concatenate([jnp.where(upper, other, own), jnp.where(upper, own, other)], 0)


def twist(layout, block, k, density, table_y, out, halves):
    vectors, group = layout.vectors, 2 * layout.quarter
    for i in range(layout.tiles):
        span = slice(i * lanes, (i + 1) * lanes)
        wide = slice(k * layout.local + i * lanes, k * layout.local + (i + 1) * lanes)
        values = density[block, i * 2 * vectors : (i + 1) * 2 * vectors, :].astype(f32)
        waves = table_y[block, :group, span]
        c, s = table_y[block, group : group + 1, span], table_y[block, group + 1 : group + 2, span]
        start = 0
        for other in halves:
            real, imag = pick_half(layout, values[:vectors], other), pick_half(layout, values[vectors:], other)
            turned = (real * c - imag * s, imag * c + real * s)
            for v in range(layout.part_v):
                for part in range(2):
                    out[start : start + group, wide] = (turned[part][v : v + 1] * waves).astype(bf16)
                    start += group


def project(layout, base, density, table_x, table_y, twisted, total, start, halves, with_tables):
    size = layout.group_of(density)

    def step(group, before):
        for k in range(size):
            if with_tables:
                make_tables(layout, base, group, k, density, table_x, table_y)
            twist(layout, size * group + k, k, density, table_y, twisted, halves)
        product = lax.dot_general(
            twisted[...], table_x[group], (((1,), (1,)), ((), ())), preferred_element_type=f32
        )
        total[...] = product if before is None else before[...] + product

    step(0, start)
    groups = density.shape[0] // size
    if groups > 1:
        lax.fori_loop(1, groups, lambda group, carry: step(group, total) or carry, 0)


def of_core(core, rows):
    return jnp.where(jnp.broadcast_to(core, (rows.shape[0] // 2, lanes)) == 1, rows[rows.shape[0] // 2 :], rows[: rows.shape[0] // 2])


def twist_chip(layout, block, core, k, density, table_y, out):
    count, group = layout.part_v, 2 * layout.quarter
    for i in range(layout.tiles):
        span = slice(i * lanes, (i + 1) * lanes)
        wide = slice(k * layout.local + i * lanes, k * layout.local + (i + 1) * lanes)
        values = of_core(core, density[block, i * 4 * count : (i + 1) * 4 * count, :].astype(f32))
        waves = table_y[block, :group, span]
        c, s = table_y[block, group : group + 1, span], table_y[block, group + 1 : group + 2, span]
        real, imag = values[:count], values[count:]
        turned = (real * c - imag * s, imag * c + real * s)
        for v in range(count):
            for part in range(2):
                start = (2 * v + part) * group
                out[start : start + group, wide] = (turned[part][v : v + 1] * waves).astype(bf16)


def chips_kernel(layout, base, with_start, density, own_x, own_y, other_x, other_y, *refs):
    start = refs[0] if with_start else None
    total, own_twisted, other_twisted = refs[-3:]
    size = layout.group_of(density)

    def step(group, before):
        for k in range(size):
            block = size * group + k
            core = layout.device_of(base + block) & 1
            twist_chip(layout, block, core, k, density, own_y, own_twisted)
            twist_chip(layout, block, 1 - core, k, density, other_y, other_twisted)
        product = 0.0
        for twisted, table in ((own_twisted, own_x), (other_twisted, other_x)):
            product = product + lax.dot_general(
                twisted[...], table[group], (((1,), (1,)), ((), ())), preferred_element_type=f32
            )
        total[...] = product if before is None else before[...] + product

    step(0, start)
    groups = density.shape[0] // size
    if groups > 1:
        lax.fori_loop(1, groups, lambda group, carry: step(group, total) or carry, 0)


def part_kernel(layout, base, with_start, with_tables, halves, *refs):
    refs = list(refs)
    density = refs.pop(0)
    tables = None if with_tables else (refs.pop(0), refs.pop(0))
    start = refs.pop(0) if with_start else None
    total = refs.pop(0)
    table_x, table_y = tables or (refs.pop(0), refs.pop(0))
    twisted = refs.pop(0)
    if len(halves) == 1:
        size = twisted.shape[0]
        start = start.at[size * halves[0] : size * (halves[0] + 1)]
    held = refs.pop(0) if refs else total
    project(layout, base, density, table_x, table_y, twisted, held, start, halves, with_tables)
    if held is not total:
        total[...] = held[...].astype(total.dtype)


def table_kernel(layout, base, density, table_x, table_y):
    size = layout.group_of(density)

    def step(group, carry):
        for k in range(size):
            make_tables(layout, base, group, k, density, table_x, table_y)
        return carry

    step(0, 0)
    groups = density.shape[0] // size
    if groups > 1:
        lax.fori_loop(1, groups, step, 0)


def weigh(layout, total, weight, scaled):
    quarter = layout.quarter
    first = layout.half_index() * layout.part_v
    for v in range(layout.part_v):
        plus_sum, plus_rest, minus_sum, minus_rest = [
            weight[first + v, k * quarter : (k + 1) * quarter, :] for k in range(4)
        ]
        starts = [(4 * v + k) * quarter for k in range(4)]
        cc, cs = [[total[starts[2 * part + k] : starts[2 * part + k] + quarter, :lanes] for part in range(2)] for k in range(2)]
        sc, ss = [[total[starts[2 * part + k] : starts[2 * part + k] + quarter, lanes:] for part in range(2)] for k in range(2)]
        ur, ui = [cc[part] - ss[part] for part in range(2)]
        vr, vi = [sc[part] + cs[part] for part in range(2)]
        one = plus_sum * ur + plus_rest * vi, plus_sum * ui - plus_rest * vr
        one_sine = plus_sum * vr - plus_rest * ui, plus_sum * vi + plus_rest * ur
        ur, ui = [cc[part] + ss[part] for part in range(2)]
        vr, vi = [sc[part] - cs[part] for part in range(2)]
        two = minus_sum * ur + minus_rest * vi, minus_sum * ui - minus_rest * vr
        two_sine = minus_sum * vr - minus_rest * ui, minus_sum * vi + minus_rest * ur
        for part in range(2):
            cosine, sine = [slice(start, start + quarter) for start in starts[2 * part : 2 * part + 2]]
            scaled[cosine, :lanes] = (one[part] + two[part]).astype(bf16)
            scaled[cosine, lanes:] = (one_sine[part] + two_sine[part]).astype(bf16)
            scaled[sine, :lanes] = (one_sine[part] - two_sine[part]).astype(bf16)
            scaled[sine, lanes:] = (two[part] - one[part]).astype(bf16)


def expand(layout, scaled, table_x, table_y, summed, result):
    count, group = layout.part_v, 2 * layout.quarter
    summed[...] = jnp.dot(scaled[...], table_x[0, :, : layout.local], preferred_element_type=f32)
    for i in range(layout.tiles):
        span = slice(i * lanes, (i + 1) * lanes)
        waves = table_y[0, :group, span]
        rows = []
        for k in range(2 * count):
            rows.append(jnp.sum(summed[k * group : (k + 1) * group, span] * waves, 0, keepdims=True))
        real, imag = jnp.concatenate(rows[0::2], 0), jnp.concatenate(rows[1::2], 0)
        c, s = table_y[0, group : group + 1, span], table_y[0, group + 1 : group + 2, span]
        result[2 * count * i : 2 * count * (i + 1), :] = jnp.concatenate([real * c + imag * s, imag * c - real * s], 0)


def far_kernel(layout, *refs):
    own, weight, own_x, own_y, other_x, other_y, far_own, far_other, total, scaled, summed, summed_other = refs[-12:]
    if len(refs) > 12:
        total[...] = own[...] + refs[0][...].astype(f32)
        own = total
    weigh(layout, own, weight, scaled)
    expand(layout, scaled, other_x, other_y, summed_other, far_other)
    expand(layout, scaled, own_x, own_y, summed, far_own)


def all_rows(layout, i, own, other):
    count = layout.part_v
    real, imag = [
        both_halves(layout, own[start : start + count, :], other[start : start + count, :])
        for start in (2 * count * i, 2 * count * i + count)
    ]
    return real, imag


def near_places(layout, neighbor, block_rows, mask):
    tile = lax.broadcasted_iota(jnp.int32, neighbor.shape, 0)
    step_x = (neighbor * 11) >> 5
    gx = lax.axis_index("tile") * layout.strips + (tile >> layout.y_bits) + step_x - 1
    hy = lax.axis_index("wave") * layout.tiles_y + (tile & (layout.tiles_y - 1)) + neighbor - 3 * step_x - 1
    gx, hy = gx & (layout.count_x - 1), hy & (layout.count_y - 1)
    core = hy >> layout.y_bits
    block = layout.block_of((gx >> layout.x_bits) * layout.waves + core) & mask
    source = ((gx & (layout.strips - 1)) << layout.y_bits) + (hy & (layout.tiles_y - 1))
    return 2 * (block * block_rows + source * 2 * layout.vectors) + core


def near_tile(layout, i, places, values_of, kernel):
    values = [values_of(places[i, j]) for j in range(9)]
    total = 0.0
    for j in range(0, 9, 2):
        span = range(j, min(j + 2, 9))
        left = jnp.concatenate([values[k] for k in span], 1)
        right = jnp.concatenate([jnp.concatenate([kernel[i, k, 0], kernel[i, k, 1]], 1) for k in span], 0)
        total += jnp.dot(left, right, preferred_element_type=f32)
    return total


def turn(upper, lower):
    return upper[:, :lanes] - lower[:, lanes:], upper[:, lanes:] + lower[:, :lanes]


def near_kernel(layout, whole, density, blocks, neighbor, near_own, near_other):
    count, vectors, tall = layout.part_v, layout.vectors, 2 * layout.vectors
    chips = layout.devices // 2
    block_rows = density.shape[0] // layout.devices
    places = near_places(layout, neighbor[...], block_rows, layout.devices - 1 if whole else chips - 1)

    def of_device(place):
        return density[pl.ds(pl.multiple_of(place >> 1, tall), tall), :]

    def of_chip(place):
        start = place >> 1
        parts = [
            density[pl.ds(pl.multiple_of(start + first, tall), tall), :].astype(f32) for first in (0, chips * block_rows)
        ]
        return jnp.concatenate([of_core(place & 1, part) for part in parts], 0).astype(bf16)

    for i in range(layout.tiles):
        total = near_tile(layout, i, places, of_device if whole else of_chip, blocks)
        span = slice(i * 2 * count, (i + 1) * 2 * count)
        if whole:
            parts = turn(total[:vectors], total[vectors:])
            near_own[span, :] = jnp.concatenate([pick_half(layout, part, False) for part in parts], 0)
            near_other[span, :] = jnp.concatenate([pick_half(layout, part, True) for part in parts], 0)
        else:
            near_own[span, :] = jnp.concatenate(turn(total[:count], total[count : 2 * count]), 0)
            near_other[span, :] = jnp.concatenate(turn(total[2 * count : 3 * count], total[3 * count :]), 0)


def first_kernel(layout, own, other, near_own, near_other, far_own, far_other, guess, basis, image_own, image_other):
    count, vectors, tall = layout.part_v, layout.vectors, 2 * layout.vectors
    hint = pick_half(layout, guess[...], False)
    core = lax.axis_index("wave")
    for i in range(layout.tiles):
        span = slice(i * 2 * count, (i + 1) * 2 * count)
        rests = []
        for density, near, far, image in ((own, near_own, far_own, image_own), (other, near_other, far_other, image_other)):
            values = density[i * tall : (i + 1) * tall, :].astype(f32)
            rr, ri = pick_half(layout, values[:vectors], False), pick_half(layout, values[vectors:], False)
            value = 0.5 * jnp.concatenate([rr, ri], 0) + near[span, :] + far[span, :]
            image[span, :] = value
            rests.append(value - jnp.concatenate([hint * rr, hint * ri], 0))
        upper = jnp.broadcast_to(core, rests[0].shape) == 1
        lines = [jnp.where(upper, rests[1], rests[0]), jnp.where(upper, rests[0], rests[1])]
        basis[i * tall : (i + 1) * tall, :] = jnp.concatenate(lines, 0).astype(bf16)


def chip_rows(layout, i, density, block, core):
    count, tall = layout.part_v, 2 * layout.vectors
    chips = layout.devices // 2
    halves = [
        of_core(core, density[block + first, i * tall : (i + 1) * tall, :].astype(f32)) for first in (0, chips)
    ]
    return [both_halves(layout, *[half[start : start + count] for half in halves]) for start in (0, count)]


def chip_sums(layout, start, density, chip):
    vectors, tall, count = layout.vectors, 2 * layout.vectors, layout.part_v
    chips = layout.devices // 2
    swapped = layout.device_of(chip) & 1
    half = layout.half_index()
    upper = lax.broadcasted_iota(jnp.int32, (vectors, lanes), 0) >= count
    total = None
    for i in range(layout.tiles):
        span = slice(i * tall, (i + 1) * tall)
        low, high = [density[chip + chips * which, span, :].astype(f32) for which in (half, 1 - half)]
        for core in range(2):
            r = start[chip + chips * (core ^ swapped), span, :].astype(f32)
            rr, ri = r[:vectors], r[vectors:]
            one, two = [z[core * vectors : (core + 1) * vectors] for z in (low, high)]
            zr = jnp.where(upper, pltpu.roll(two, count, 0), one)
            zi = jnp.where(upper, two, pltpu.roll(one, count, 0))
            terms = (rr * rr + ri * ri, rr * zr + ri * zi, rr * zi - ri * zr, zr * zr + zi * zi)
            total = terms if total is None else [a + b for a, b in zip(total, terms)]
    return total


def tree_sums(layout, start, density, chip, count):
    if count == 1:
        return chip_sums(layout, start, density, chip)
    lower = tree_sums(layout, start, density, chip, count // 2)
    upper = tree_sums(layout, start, density, chip + count // 2, count // 2)
    return [a + b for a, b in zip(lower, upper)]


def scalar_kernel(layout, start, density, guess, factors):
    vectors = layout.vectors
    sums = tree_sums(layout, start, density, 0, layout.devices // 2)
    squares, real, imag, rest = [
        jnp.broadcast_to(jnp.sum(value, 1, keepdims=True) * (1.0 / layout.panels), (vectors, lanes)) for value in sums
    ]
    hint = guess[...]
    scale_sq = squares + eps_norm
    coef_real = (real + hint * squares) / scale_sq
    coef_imag = imag / scale_sq
    more_real, more_imag = coef_real - hint, coef_imag
    update_sq = rest - 2.0 * (more_real * real + more_imag * imag) + (more_real * more_real + more_imag * more_imag) * squares
    scale = jnp.sqrt(scale_sq)
    update_scale = jnp.sqrt(jnp.maximum(update_sq, 0.0) / scale_sq + eps_norm)
    spot = lax.broadcasted_iota(jnp.int32, (vectors, lanes), 0)
    lane = lax.broadcasted_iota(jnp.int32, (vectors, lanes), 1)
    lines = [
        jnp.sum(jnp.where(spot == lane, value, 0.0), 0, keepdims=True)
        for value in (scale, coef_real, coef_imag, update_scale)
    ]
    lines.append(jnp.zeros((vectors - 4, lanes), f32))
    factors[...] = jnp.concatenate([more_real, more_imag, 1.0 / (scale * update_scale)] + lines, 0)


def second_kernel(layout, density, near_own, near_other, far_own, far_other, image_own, image_other, factors, result, scalars):
    vectors, tall = layout.vectors, 2 * layout.vectors
    more_real, more_imag = factors[:vectors, :], factors[vectors : 2 * vectors, :]
    inverse = factors[2 * vectors : 3 * vectors, :]
    scalars[...] = factors[3 * vectors : 3 * vectors + 4, :vectors]
    core = lax.axis_index("wave")
    for i in range(layout.tiles):
        first = i * tall
        far_real, far_imag = all_rows(layout, i, far_own, far_other)
        near_real, near_imag = all_rows(layout, i, near_own, near_other)
        wr, wi = all_rows(layout, i, image_own, image_other)
        zr, zi = chip_rows(layout, i, density, 0, core)
        real = 0.5 * zr + near_real + far_real
        imag = 0.5 * zi + near_imag + far_imag
        result[first : first + vectors, :] = (real - (more_real * wr - more_imag * wi)) * inverse
        result[first + vectors : first + tall, :] = (imag - (more_real * wi + more_imag * wr)) * inverse


def per_device(residual, kernel, offsets, neighbor, frequency, lattice_x, lattice_y, spectral_weight):
    strips, tiles_y, _, vectors, _ = residual.shape
    modes_x, modes_y = spectral_weight.shape[1:]
    layout = Layout(strips, tiles_y, vectors, modes_x)
    tiles, rows, devices = layout.tiles, layout.rows, layout.devices
    vmem = pl.BlockSpec(memory_space=pltpu.VMEM)
    shape = jax.ShapeDtypeStruct
    tall = 2 * vectors * 2 * layout.quarter
    wide = 4 * layout.half
    count = spectral_weight.shape[0]

    def call(body, name, out_shape, in_specs, limit, scratch=(), aliases=None):
        return pl.pallas_call(
            body,
            out_shape=out_shape,
            in_specs=in_specs,
            out_specs=jax.tree.map(lambda _: vmem, out_shape),
            scratch_shapes=scratch,
            input_output_aliases=aliases or {},
            compiler_params=pltpu.CompilerParams(vmem_limit_bytes=int(limit * mib)),
            cost_estimate=pl.CostEstimate(
                flops=int(lengths.get(name, 0) * 1e9), bytes_accessed=0, transcendentals=0
            ),
            name=name,
        )

    head = jnp.concatenate([residual.reshape(rows, lanes), offsets.reshape(2 * tiles, lanes)], 0)
    packed = call(
        lambda *refs: pack_kernel(layout, *refs),
        "pack",
        shape((rows + layout.offset_rows, lanes), bf16),
        [vmem],
        1,
    )(head)
    scale = 1.0 / math.sqrt(modes_x * modes_y * layout.panels)
    integers = jnp.stack([lattice_x, lattice_y, jnp.pad(frequency, (0, lanes - frequency.shape[0]))])

    def spectral(integers):
        return call(
            lambda *refs: spectral_kernel(layout, scale, *refs),
            "spectral",
            (shape((vectors, modes_y, modes_x), f32), shape((vectors, lanes), f32)),
            [vmem, vmem],
            4,
            [
                pltpu.SMEM((1, lanes), jnp.int32),
                pltpu.VMEM(spectral_weight.shape, f32),
                pltpu.SemaphoreType.DMA,
            ],
        )(integers, spectral_weight)

    blocks = kernel.reshape(tiles, 9, 2, lanes, lanes)
    neighbor = neighbor.reshape(tiles, 9)

    def table_shapes(size):
        return (
            shape((size // min(size, 4), wide, min(size, 4) * layout.local), bf16),
            shape((size, 2 * layout.quarter + 8, layout.local), f32),
        )

    def part_call(name, base, part, tables, total, halves, dtype):
        size = part.shape[0]
        high = len(halves) * tall // 2
        given = [part] + list(tables or ()) + ([] if total is None else [total])
        scratch = [pltpu.VMEM((high, min(size, 4) * layout.local), bf16)]
        if dtype != f32:
            scratch.append(pltpu.VMEM((high, wide), f32))
        with_start = total is not None
        return call(
            lambda *refs: part_kernel(layout, base, with_start, not tables, halves, *refs),
            name,
            (shape((high, wide), dtype), *(() if tables else table_shapes(size))),
            [vmem] * len(given),
            24,
            scratch,
            aliases={len(given) - 1: 0} if with_start and len(halves) == 2 else None,
        )(*given)

    def make(name, base, density):
        return call(
            lambda *refs: table_kernel(layout, base, *refs),
            name,
            table_shapes(density.shape[0]),
            [vmem],
            8,
        )(density)

    def gather_and_project(array, tables):
        array = array[None]
        total, base, made, seen = None, 0, [], []
        for k, mask in enumerate(layout.chip_masks):
            pairs = [(i, i ^ mask) for i in range(devices)]
            arrived = lax.ppermute(array, ("tile", "wave"), pairs)
            array = jnp.concatenate([array, arrived])
            seen.append(array)
            part = arrived if k else array
            if k < len(layout.chip_masks) - 1:
                total, *new = part_call("part", base, part, tables and tables[k], total, (0, 1), f32)
                base += part.shape[0]
                made.append(new or tables[k])
        made.append(make("tables", base, part))
        (leaving,) = part_call("leaving", base, part, made[-1], total, (1,), bf16)

        def stay(first):
            return part_call("staying", base, after(part, first), made[-1], total, (0,), f32)[0]

        return seen, leaving, stay, made

    def gather_chips(array, tables, other):
        array = array[None]
        total, base, seen = None, 0, []
        for k, mask in enumerate(layout.chip_masks):
            pairs = [(i, i ^ mask) for i in range(devices)]
            arrived = lax.ppermute(array, ("tile", "wave"), pairs)
            array = jnp.concatenate([array, arrived])
            seen.append(array)
            part = arrived if k else array
            wait = seen[min(k, 1)]
            more = make("tables", devices // 2 + base, after(other, wait)[base : base + part.shape[0]])
            given = [part, *tables[k], *more] + ([] if total is None else [total])
            width = layout.group_of(part) * layout.local
            total = call(
                lambda *refs, base=base, start=total is not None: chips_kernel(layout, base, start, *refs),
                "part" if k < len(layout.chip_masks) - 1 else "whole",
                shape((tall // 2, wide), f32),
                [vmem] * len(given),
                24,
                [pltpu.VMEM((tall // 2, width), bf16)] * 2,
                aliases={} if total is None else {len(given) - 1: 0},
            )(*given)
            base += part.shape[0]
        return seen, total

    def far_field(sums, weight, own_tables, other_tables):
        return call(
            lambda *refs: far_kernel(layout, *refs),
            "far",
            tuple([shape((rows // 2, lanes), f32)] * 2),
            [vmem] * (5 + len(sums)),
            24,
            [
                pltpu.VMEM((tall // 2, wide), f32),
                pltpu.VMEM((tall // 2, wide), bf16),
                pltpu.VMEM((tall // 2, layout.local), f32),
                pltpu.VMEM((tall // 2, layout.local), f32),
            ],
        )(*sums, weight, *own_tables, *other_tables)

    def near_field(density, whole):
        return call(
            lambda *refs: near_kernel(layout, whole, *refs),
            "near",
            tuple([shape((rows // 2, lanes), f32)] * 2),
            [vmem] * 3,
            12,
        )(density.reshape(-1, lanes), blocks, neighbor)

    def with_other_core(array):
        return jnp.concatenate([array, swap_cores(array)])

    seen, leaving, stay, tables = gather_and_project(packed, None)
    other_packed = swap_cores(after(packed, seen[0]))
    beside = make("other_tables", devices // 2, other_packed[None])
    weight, guess = spectral(after(integers, seen[1]))
    start = with_other_core(seen[-1])
    near_own, near_other = near_field(start, True)
    far_own, far_other = far_field((swap_cores(leaving), stay(near_own)), weight, tables[0], beside)
    basis, image_own, image_other = call(
        lambda *refs: first_kernel(layout, *refs),
        "first",
        (shape((rows, lanes), bf16), shape((rows // 2, lanes), f32), shape((rows // 2, lanes), f32)),
        [vmem] * 7,
        2,
    )(packed, other_packed, near_own, swap_cores(near_other), far_own, far_other, guess)
    seen, total = gather_chips(basis, tables, start[devices // 2 :])
    everything = with_other_core(seen[-1])
    factors = call(
        lambda *refs: scalar_kernel(layout, *refs),
        "scalars",
        shape((4 * vectors, lanes), f32),
        [vmem] * 3,
        1 + devices / 8,
    )(start, everything, guess)
    near_own, near_other = near_field(everything, False)
    far_own, far_other = far_field((total,), weight, tables[0], beside)
    result, scalars = call(
        lambda *refs: second_kernel(layout, *refs),
        "second",
        (shape((rows, lanes), f32), shape((4, vectors), f32)),
        [vmem] * 8,
        2,
    )(
        everything,
        near_own,
        near_other,
        far_own,
        swap_cores(far_other),
        image_own,
        swap_cores(image_other),
        factors,
    )
    return result.reshape(residual.shape), scalars


def solution(mesh):
    return jax.shard_map(
        per_device,
        mesh=mesh,
        in_specs=(
            P(("grp", "tile"), "wave", None, None, None),
            P(("grp", "tile"), "wave", None, None, None, None),
            P(("grp", "tile"), "wave", None, None),
            P(("grp", "tile"), "wave", None),
            P("grp"),
            P(),
            P(),
            P(),
        ),
        out_specs=(P(("grp", "tile"), "wave", None, None, None), P("grp", None)),
        check_vma=False,
    )
```

```python
import math

import jax
import jax.numpy as jnp
from jax import lax
from jax.experimental import pallas as pl
from jax.experimental.pallas import tpu as pltpu
from jax.sharding import PartitionSpec as P

eps_norm = 1e-06
lengths = {"part": 1, "leaving": 0.5, "staying": 0.8, "spectral": 2, "other_tables": 0.5, "far": 0.3, "near": 2, "tables": 0.5, "whole": 0.8}
f32 = jnp.float32
bf16 = jnp.bfloat16
lanes = 128
mib = 1024 * 1024

sine_terms = (6.2831640439986325, -10.334285583027317, 5.083797977378017, -1.1092722161777626)
cosine_terms = (0.9999932951314766, -4.933938004239768, 4.041283709560866, -1.2221267509458762)


def horner(terms, value):
    total = jnp.full_like(value, terms[-1])
    for term in terms[-2::-1]:
        total = total * value + term
    return total


def cos_sin(turns):
    turn = turns - jnp.round(turns)
    square = turn * turn
    double = turn * horner(sine_terms, square)
    return 1.0 - 0.5 * (double * double), double * horner(cosine_terms, square)


class Layout:
    def __init__(self, strips, tiles_y, vectors, modes):
        self.strips, self.tiles_y, self.vectors = strips, tiles_y, vectors
        self.tiles = strips * tiles_y
        self.columns, self.waves = lax.axis_size("tile"), lax.axis_size("wave")
        self.devices = self.columns * self.waves
        self.count_x, self.count_y = self.columns * strips, self.waves * tiles_y
        self.panels = self.count_x * self.count_y * lanes
        self.local = self.tiles * lanes
        self.rows = self.tiles * 2 * vectors
        self.offset_rows = -(-4 * self.tiles // 16) * 16
        self.part_v = vectors // 2
        self.x_bits, self.y_bits = (strips - 1).bit_length(), (tiles_y - 1).bit_length()
        assert strips == 1 << self.x_bits and tiles_y == 1 << self.y_bits
        self.half = modes // 2
        self.quarter = modes // 4
        chip_bits = (self.columns - 1).bit_length()
        assert self.columns == 1 << chip_bits and self.waves == 2
        self.chip_masks = [(1 << b) * self.waves + 1 for b in reversed(range(chip_bits))]
        self.masks = self.chip_masks + [1]

    def me(self):
        return lax.axis_index("tile") * self.waves + lax.axis_index("wave")

    def half_index(self):
        column, half = lax.axis_index("tile"), lax.axis_index("wave")
        for b in range(len(self.chip_masks)):
            half = half ^ ((column >> b) & 1)
        return half

    def device_of(self, block):
        device = self.me()
        for k, mask in enumerate(self.masks):
            device = device ^ (((block >> k) & 1) * mask)
        return device

    def group_of(self, density):
        return min(density.shape[0], 4)

    def block_of(self, device):
        rest = device ^ self.me()
        block = 0
        for k, mask in enumerate(self.chip_masks):
            bit = (rest >> (mask.bit_length() - 1)) & 1
            block = block | (bit << k)
            rest = rest ^ (bit * mask)
        block = block | (rest << len(self.chip_masks))
        return block


def swap_cores(array):
    return lax.ppermute(array, "wave", [(0, 1), (1, 0)])


def after(value, *others):
    return lax.optimization_barrier((value, *others))[0]


def two_parts(value):
    first = value.astype(bf16)
    return first, (value - first.astype(f32)).astype(bf16)


def pack_kernel(layout, head, out):
    rows, count = layout.rows, 2 * layout.tiles
    out[:rows, :] = head[:rows, :].astype(bf16)
    first, second = two_parts(head[rows:, :])
    pieces = [first.astype(f32), second.astype(f32)]
    if layout.offset_rows > 2 * count:
        pieces.append(jnp.zeros((layout.offset_rows - 2 * count, lanes), f32))
    out[rows:, :] = jnp.concatenate(pieces, 0).astype(bf16)


def swap(value):
    return pltpu.roll(value, lanes // 2, 1)


def spectral_kernel(layout, scale, integers, table, out, guess, order, moved_all, sem):
    half, quarter = layout.half, layout.quarter
    size = 2 * half
    count = moved_all.shape[0]
    copy = pltpu.make_async_copy(integers.at[2:3], order, sem)
    copy.start()
    spot = lax.broadcasted_iota(jnp.int32, (size, size), 0)
    wanted = jnp.where(spot < half, spot + half, size - 1 - spot)
    pick_x, pick_y = [jnp.where(wanted == integers[k : k + 1], 1.0, 0.0).astype(bf16) for k in range(2)]
    pick_x, pick_y = [jnp.concatenate([pick, pick], 1) for pick in (pick_x, pick_y)]
    for f in range(0, count, 2):
        pair = range(f, min(f + 2, count))
        columns = [jnp.concatenate(two_parts(table[k] * scale), 0) for k in pair]
        moved = jnp.dot(pick_x, jnp.concatenate(columns, 1), preferred_element_type=f32)
        rows = [jnp.concatenate(two_parts(moved[:, n * size : (n + 1) * size]), 1) for n in range(len(pair))]
        moved = lax.dot_general(
            pick_y, jnp.concatenate(rows, 0), (((1,), (1,)), ((), ())), preferred_element_type=f32
        )
        for n, k in enumerate(pair):
            moved_all[k] = moved[:, n * size : (n + 1) * size]
    copy.wait()
    low = lax.broadcasted_iota(jnp.int32, (quarter, lanes), 1) < half
    rows = []
    for v in range(layout.vectors):
        moved = moved_all[order[0, v]]
        mean = jnp.sum(jnp.sum(moved, 0, keepdims=True), 1, keepdims=True)
        rows.append(jnp.broadcast_to(0.5 + mean, (1, lanes)))
        part = [moved[k * quarter : (k + 1) * quarter] for k in range(4)]
        for k, choices in enumerate((((1, 3), (0, 2)), ((2, 0), (3, 1)))):
            chosen = [jnp.where(low, part[one], part[other]) for one, other in choices]
            turned = [swap(value) for value in chosen]
            plus = jnp.where(low, chosen[0] + turned[0], chosen[1] + turned[1])
            minus = jnp.where(low, chosen[0] - turned[0], turned[1] - chosen[1])
            out[v, 2 * k * quarter : 2 * (k + 1) * quarter, :] = jnp.concatenate([plus, minus], 0)
    guess[...] = jnp.concatenate(rows, 0)


def climb(start, step, count):
    (c, s), (step_c, step_s) = start, step
    cosines, sines = [c], [s]
    for _ in range(count - 1):
        c, s = c * step_c - s * step_s, s * step_c + c * step_s
        cosines.append(c)
        sines.append(s)
    return jnp.concatenate(cosines, 0), jnp.concatenate(sines, 0)


def make_tables(layout, base, group, k, density, table_x, table_y):
    tiles, half, quarter = layout.tiles, layout.half, layout.quarter
    block = layout.group_of(density) * group + k
    device = layout.device_of(base + block)
    column, row_index = device // layout.waves, device % layout.waves
    pieces = density[block, layout.rows :, :].astype(f32)
    spot = lax.broadcasted_iota(jnp.int32, (2 * tiles, lanes), 0)
    along_x = (spot & 1) == 0
    tile = spot >> 1
    corner = jnp.where(
        along_x,
        column * layout.strips + (tile >> layout.y_bits),
        row_index * layout.tiles_y + (tile & (layout.tiles_y - 1)),
    )
    size = jnp.where(along_x, 1.0 / layout.count_x, 1.0 / layout.count_y)
    position = (pieces[: 2 * tiles] + pieces[2 * tiles : 4 * tiles] + corner.astype(f32)) * size
    steps = cos_sin(8.0 * position)
    phases = cos_sin(0.5 * (position + pltpu.roll(position, 2 * tiles - 1, 0)))
    eight = lax.broadcasted_iota(jnp.int32, (8, lanes), 0).astype(f32) + 0.5

    def row(array, index):
        return jnp.broadcast_to(array[index : index + 1], (8, lanes))

    for i in range(tiles):
        x, y = row(position, 2 * i), row(position, 2 * i + 1)
        step_x, step_y = [[row(step, 2 * i + n) for step in steps] for n in range(2)]
        span = slice(i * lanes, (i + 1) * lanes)
        wide = slice(k * layout.local + i * lanes, k * layout.local + (i + 1) * lanes)
        for e, shift in ((0, quarter / 2), (1, -quarter / 2)):
            cosines, sines = climb(cos_sin(eight * x + shift * y), step_x, half // 8)
            table_x[group, half * e : half * (e + 1), wide] = cosines.astype(bf16)
            table_x[group, half * (e + 2) : half * (e + 3), wide] = sines.astype(bf16)
        cosines, sines = climb(cos_sin((eight + quarter / 2) * y), step_y, quarter // 8)
        last = [phase[2 * i : 2 * i + 1] for phase in phases]
        table_y[block, :, span] = jnp.concatenate([cosines, sines] + last + [jnp.zeros((6, lanes), f32)], 0)


def pick_half(layout, rows, other):
    count = layout.part_v
    core = layout.half_index()
    upper = jnp.broadcast_to(1 - core if other else core, (count, lanes)) == 1
    return jnp.where(upper, rows[count:], rows[:count])


def both_halves(layout, own, other):
    upper = jnp.broadcast_to(layout.half_index(), own.shape) == 1
    return jnp.concatenate([jnp.where(upper, other, own), jnp.where(upper, own, other)], 0)


def twist(layout, block, k, density, table_y, out, halves):
    vectors, group = layout.vectors, 2 * layout.quarter
    for i in range(layout.tiles):
        span = slice(i * lanes, (i + 1) * lanes)
        wide = slice(k * layout.local + i * lanes, k * layout.local + (i + 1) * lanes)
        values = density[block, i * 2 * vectors : (i + 1) * 2 * vectors, :].astype(f32)
        waves = table_y[block, :group, span]
        c, s = table_y[block, group : group + 1, span], table_y[block, group + 1 : group + 2, span]
        start = 0
        for other in halves:
            real, imag = pick_half(layout, values[:vectors], other), pick_half(layout, values[vectors:], other)
            turned = (real * c - imag * s, imag * c + real * s)
            for v in range(layout.part_v):
                for part in range(2):
                    out[start : start + group, wide] = (turned[part][v : v + 1] * waves).astype(bf16)
                    start += group


def project(layout, base, density, table_x, table_y, twisted, total, start, halves, with_tables):
    size = layout.group_of(density)

    def step(group, before):
        for k in range(size):
            if with_tables:
                make_tables(layout, base, group, k, density, table_x, table_y)
            twist(layout, size * group + k, k, density, table_y, twisted, halves)
        product = lax.dot_general(
            twisted[...], table_x[group], (((1,), (1,)), ((), ())), preferred_element_type=f32
        )
        total[...] = product if before is None else before[...] + product

    step(0, start)
    groups = density.shape[0] // size
    if groups > 1:
        lax.fori_loop(1, groups, lambda group, carry: step(group, total) or carry, 0)


def of_core(core, rows):
    return jnp.where(jnp.broadcast_to(core, (rows.shape[0] // 2, lanes)) == 1, rows[rows.shape[0] // 2 :], rows[: rows.shape[0] // 2])


def twist_chip(layout, block, core, k, density, table_y, out):
    count, group = layout.part_v, 2 * layout.quarter
    for i in range(layout.tiles):
        span = slice(i * lanes, (i + 1) * lanes)
        wide = slice(k * layout.local + i * lanes, k * layout.local + (i + 1) * lanes)
        values = of_core(core, density[block, i * 4 * count : (i + 1) * 4 * count, :].astype(f32))
        waves = table_y[block, :group, span]
        c, s = table_y[block, group : group + 1, span], table_y[block, group + 1 : group + 2, span]
        real, imag = values[:count], values[count:]
        turned = (real * c - imag * s, imag * c + real * s)
        for v in range(count):
            for part in range(2):
                start = (2 * v + part) * group
                out[start : start + group, wide] = (turned[part][v : v + 1] * waves).astype(bf16)


def chips_kernel(layout, base, with_start, density, own_x, own_y, other_x, other_y, *refs):
    start = refs[0] if with_start else None
    total, own_twisted, other_twisted = refs[-3:]
    size = layout.group_of(density)

    def step(group, before):
        for k in range(size):
            block = size * group + k
            core = layout.device_of(base + block) & 1
            twist_chip(layout, block, core, k, density, own_y, own_twisted)
            twist_chip(layout, block, 1 - core, k, density, other_y, other_twisted)
        product = 0.0
        for twisted, table in ((own_twisted, own_x), (other_twisted, other_x)):
            product = product + lax.dot_general(
                twisted[...], table[group], (((1,), (1,)), ((), ())), preferred_element_type=f32
            )
        total[...] = product if before is None else before[...] + product

    step(0, start)
    groups = density.shape[0] // size
    if groups > 1:
        lax.fori_loop(1, groups, lambda group, carry: step(group, total) or carry, 0)


def part_kernel(layout, base, with_start, with_tables, halves, *refs):
    refs = list(refs)
    density = refs.pop(0)
    tables = None if with_tables else (refs.pop(0), refs.pop(0))
    start = refs.pop(0) if with_start else None
    total = refs.pop(0)
    table_x, table_y = tables or (refs.pop(0), refs.pop(0))
    twisted = refs.pop(0)
    if len(halves) == 1:
        size = twisted.shape[0]
        start = start.at[size * halves[0] : size * (halves[0] + 1)]
    held = refs.pop(0) if refs else total
    project(layout, base, density, table_x, table_y, twisted, held, start, halves, with_tables)
    if held is not total:
        total[...] = held[...].astype(total.dtype)


def table_kernel(layout, base, density, table_x, table_y):
    size = layout.group_of(density)

    def step(group, carry):
        for k in range(size):
            make_tables(layout, base, group, k, density, table_x, table_y)
        return carry

    step(0, 0)
    groups = density.shape[0] // size
    if groups > 1:
        lax.fori_loop(1, groups, step, 0)


def weigh(layout, total, weight, scaled):
    quarter = layout.quarter
    first = layout.half_index() * layout.part_v
    for v in range(layout.part_v):
        plus_sum, plus_rest, minus_sum, minus_rest = [
            weight[first + v, k * quarter : (k + 1) * quarter, :] for k in range(4)
        ]
        starts = [(4 * v + k) * quarter for k in range(4)]
        cc, cs = [[total[starts[2 * part + k] : starts[2 * part + k] + quarter, :lanes] for part in range(2)] for k in range(2)]
        sc, ss = [[total[starts[2 * part + k] : starts[2 * part + k] + quarter, lanes:] for part in range(2)] for k in range(2)]
        ur, ui = [cc[part] - ss[part] for part in range(2)]
        vr, vi = [sc[part] + cs[part] for part in range(2)]
        one = plus_sum * ur + plus_rest * vi, plus_sum * ui - plus_rest * vr
        one_sine = plus_sum * vr - plus_rest * ui, plus_sum * vi + plus_rest * ur
        ur, ui = [cc[part] + ss[part] for part in range(2)]
        vr, vi = [sc[part] - cs[part] for part in range(2)]
        two = minus_sum * ur + minus_rest * vi, minus_sum * ui - minus_rest * vr
        two_sine = minus_sum * vr - minus_rest * ui, minus_sum * vi + minus_rest * ur
        for part in range(2):
            cosine, sine = [slice(start, start + quarter) for start in starts[2 * part : 2 * part + 2]]
            scaled[cosine, :lanes] = (one[part] + two[part]).astype(bf16)
            scaled[cosine, lanes:] = (one_sine[part] + two_sine[part]).astype(bf16)
            scaled[sine, :lanes] = (one_sine[part] - two_sine[part]).astype(bf16)
            scaled[sine, lanes:] = (two[part] - one[part]).astype(bf16)


def expand(layout, scaled, table_x, table_y, summed, result):
    count, group = layout.part_v, 2 * layout.quarter
    summed[...] = jnp.dot(scaled[...], table_x[0, :, : layout.local], preferred_element_type=f32)
    for i in range(layout.tiles):
        span = slice(i * lanes, (i + 1) * lanes)
        waves = table_y[0, :group, span]
        rows = []
        for k in range(2 * count):
            rows.append(jnp.sum(summed[k * group : (k + 1) * group, span] * waves, 0, keepdims=True))
        real, imag = jnp.concatenate(rows[0::2], 0), jnp.concatenate(rows[1::2], 0)
        c, s = table_y[0, group : group + 1, span], table_y[0, group + 1 : group + 2, span]
        result[2 * count * i : 2 * count * (i + 1), :] = jnp.concatenate([real * c + imag * s, imag * c - real * s], 0)


def far_kernel(layout, *refs):
    own, weight, own_x, own_y, other_x, other_y, far_own, far_other, total, scaled, summed, summed_other = refs[-12:]
    if len(refs) > 12:
        total[...] = own[...] + refs[0][...].astype(f32)
        own = total
    weigh(layout, own, weight, scaled)
    expand(layout, scaled, other_x, other_y, summed_other, far_other)
    expand(layout, scaled, own_x, own_y, summed, far_own)


def all_rows(layout, i, own, other):
    count = layout.part_v
    real, imag = [
        both_halves(layout, own[start : start + count, :], other[start : start + count, :])
        for start in (2 * count * i, 2 * count * i + count)
    ]
    return real, imag


def near_places(layout, neighbor, block_rows, mask):
    tile = lax.broadcasted_iota(jnp.int32, neighbor.shape, 0)
    step_x = (neighbor * 11) >> 5
    gx = lax.axis_index("tile") * layout.strips + (tile >> layout.y_bits) + step_x - 1
    hy = lax.axis_index("wave") * layout.tiles_y + (tile & (layout.tiles_y - 1)) + neighbor - 3 * step_x - 1
    gx, hy = gx & (layout.count_x - 1), hy & (layout.count_y - 1)
    core = hy >> layout.y_bits
    block = layout.block_of((gx >> layout.x_bits) * layout.waves + core) & mask
    source = ((gx & (layout.strips - 1)) << layout.y_bits) + (hy & (layout.tiles_y - 1))
    return 2 * (block * block_rows + source * 2 * layout.vectors) + core


def near_tile(layout, i, places, values_of, kernel):
    values = [values_of(places[i, j]) for j in range(9)]
    total = 0.0
    for j in range(0, 9, 2):
        span = range(j, min(j + 2, 9))
        left = jnp.concatenate([values[k] for k in span], 1)
        right = jnp.concatenate([jnp.concatenate([kernel[i, k, 0], kernel[i, k, 1]], 1) for k in span], 0)
        total += jnp.dot(left, right, preferred_element_type=f32)
    return total


def turn(upper, lower):
    return upper[:, :lanes] - lower[:, lanes:], upper[:, lanes:] + lower[:, :lanes]


def near_kernel(layout, whole, density, blocks, neighbor, near_own, near_other):
    count, vectors, tall = layout.part_v, layout.vectors, 2 * layout.vectors
    chips = layout.devices // 2
    block_rows = density.shape[0] // layout.devices
    places = near_places(layout, neighbor[...], block_rows, layout.devices - 1 if whole else chips - 1)

    def of_device(place):
        return density[pl.ds(pl.multiple_of(place >> 1, tall), tall), :]

    def of_chip(place):
        start = place >> 1
        parts = [
            density[pl.ds(pl.multiple_of(start + first, tall), tall), :].astype(f32) for first in (0, chips * block_rows)
        ]
        return jnp.concatenate([of_core(place & 1, part) for part in parts], 0).astype(bf16)

    for i in range(layout.tiles):
        total = near_tile(layout, i, places, of_device if whole else of_chip, blocks)
        span = slice(i * 2 * count, (i + 1) * 2 * count)
        if whole:
            parts = turn(total[:vectors], total[vectors:])
            near_own[span, :] = jnp.concatenate([pick_half(layout, part, False) for part in parts], 0)
            near_other[span, :] = jnp.concatenate([pick_half(layout, part, True) for part in parts], 0)
        else:
            near_own[span, :] = jnp.concatenate(turn(total[:count], total[count : 2 * count]), 0)
            near_other[span, :] = jnp.concatenate(turn(total[2 * count : 3 * count], total[3 * count :]), 0)


def first_kernel(layout, own, other, near_own, near_other, far_own, far_other, guess, basis, image_own, image_other):
    count, vectors, tall = layout.part_v, layout.vectors, 2 * layout.vectors
    hint = pick_half(layout, guess[...], False)
    core = lax.axis_index("wave")
    for i in range(layout.tiles):
        span = slice(i * 2 * count, (i + 1) * 2 * count)
        rests = []
        for density, near, far, image in ((own, near_own, far_own, image_own), (other, near_other, far_other, image_other)):
            values = density[i * tall : (i + 1) * tall, :].astype(f32)
            rr, ri = pick_half(layout, values[:vectors], False), pick_half(layout, values[vectors:], False)
            value = 0.5 * jnp.concatenate([rr, ri], 0) + near[span, :] + far[span, :]
            image[span, :] = value
            rests.append(value - jnp.concatenate([hint * rr, hint * ri], 0))
        upper = jnp.broadcast_to(core, rests[0].shape) == 1
        lines = [jnp.where(upper, rests[1], rests[0]), jnp.where(upper, rests[0], rests[1])]
        basis[i * tall : (i + 1) * tall, :] = jnp.concatenate(lines, 0).astype(bf16)


def chip_rows(layout, i, density, block, core):
    count, tall = layout.part_v, 2 * layout.vectors
    chips = layout.devices // 2
    halves = [
        of_core(core, density[block + first, i * tall : (i + 1) * tall, :].astype(f32)) for first in (0, chips)
    ]
    return [both_halves(layout, *[half[start : start + count] for half in halves]) for start in (0, count)]


def chip_sums(layout, start, density, chip):
    vectors, tall, count = layout.vectors, 2 * layout.vectors, layout.part_v
    chips = layout.devices // 2
    swapped = layout.device_of(chip) & 1
    half = layout.half_index()
    upper = lax.broadcasted_iota(jnp.int32, (vectors, lanes), 0) >= count
    total = None
    for i in range(layout.tiles):
        span = slice(i * tall, (i + 1) * tall)
        low, high = [density[chip + chips * which, span, :].astype(f32) for which in (half, 1 - half)]
        for core in range(2):
            r = start[chip + chips * (core ^ swapped), span, :].astype(f32)
            rr, ri = r[:vectors], r[vectors:]
            one, two = [z[core * vectors : (core + 1) * vectors] for z in (low, high)]
            zr = jnp.where(upper, pltpu.roll(two, count, 0), one)
            zi = jnp.where(upper, two, pltpu.roll(one, count, 0))
            terms = (rr * rr + ri * ri, rr * zr + ri * zi, rr * zi - ri * zr, zr * zr + zi * zi)
            total = terms if total is None else [a + b for a, b in zip(total, terms)]
    return total


def tree_sums(layout, start, density, chip, count):
    if count == 1:
        return chip_sums(layout, start, density, chip)
    lower = tree_sums(layout, start, density, chip, count // 2)
    upper = tree_sums(layout, start, density, chip + count // 2, count // 2)
    return [a + b for a, b in zip(lower, upper)]


def scalar_kernel(layout, start, density, guess, factors):
    vectors = layout.vectors
    sums = tree_sums(layout, start, density, 0, layout.devices // 2)
    squares, real, imag, rest = [
        jnp.broadcast_to(jnp.sum(value, 1, keepdims=True) * (1.0 / layout.panels), (vectors, lanes)) for value in sums
    ]
    hint = guess[...]
    scale_sq = squares + eps_norm
    coef_real = (real + hint * squares) / scale_sq
    coef_imag = imag / scale_sq
    more_real, more_imag = coef_real - hint, coef_imag
    update_sq = rest - 2.0 * (more_real * real + more_imag * imag) + (more_real * more_real + more_imag * more_imag) * squares
    scale = jnp.sqrt(scale_sq)
    update_scale = jnp.sqrt(jnp.maximum(update_sq, 0.0) / scale_sq + eps_norm)
    spot = lax.broadcasted_iota(jnp.int32, (vectors, lanes), 0)
    lane = lax.broadcasted_iota(jnp.int32, (vectors, lanes), 1)
    lines = [
        jnp.sum(jnp.where(spot == lane, value, 0.0), 0, keepdims=True)
        for value in (scale, coef_real, coef_imag, update_scale)
    ]
    lines.append(jnp.zeros((vectors - 4, lanes), f32))
    factors[...] = jnp.concatenate([more_real, more_imag, 1.0 / (scale * update_scale)] + lines, 0)


def second_kernel(layout, density, near_own, near_other, far_own, far_other, image_own, image_other, factors, result, scalars):
    vectors, tall = layout.vectors, 2 * layout.vectors
    more_real, more_imag = factors[:vectors, :], factors[vectors : 2 * vectors, :]
    inverse = factors[2 * vectors : 3 * vectors, :]
    scalars[...] = factors[3 * vectors : 3 * vectors + 4, :vectors]
    core = lax.axis_index("wave")
    for i in range(layout.tiles):
        first = i * tall
        far_real, far_imag = all_rows(layout, i, far_own, far_other)
        near_real, near_imag = all_rows(layout, i, near_own, near_other)
        wr, wi = all_rows(layout, i, image_own, image_other)
        zr, zi = chip_rows(layout, i, density, 0, core)
        real = 0.5 * zr + near_real + far_real
        imag = 0.5 * zi + near_imag + far_imag
        result[first : first + vectors, :] = (real - (more_real * wr - more_imag * wi)) * inverse
        result[first + vectors : first + tall, :] = (imag - (more_real * wi + more_imag * wr)) * inverse


def per_device(residual, kernel, offsets, neighbor, frequency, lattice_x, lattice_y, spectral_weight):
    strips, tiles_y, _, vectors, _ = residual.shape
    modes_x, modes_y = spectral_weight.shape[1:]
    layout = Layout(strips, tiles_y, vectors, modes_x)
    tiles, rows, devices = layout.tiles, layout.rows, layout.devices
    vmem = pl.BlockSpec(memory_space=pltpu.VMEM)
    shape = jax.ShapeDtypeStruct
    tall = 2 * vectors * 2 * layout.quarter
    wide = 4 * layout.half
    count = spectral_weight.shape[0]

    def call(body, name, out_shape, in_specs, limit, scratch=(), aliases=None):
        return pl.pallas_call(
            body,
            out_shape=out_shape,
            in_specs=in_specs,
            out_specs=jax.tree.map(lambda _: vmem, out_shape),
            scratch_shapes=scratch,
            input_output_aliases=aliases or {},
            compiler_params=pltpu.CompilerParams(vmem_limit_bytes=int(limit * mib)),
            cost_estimate=pl.CostEstimate(
                flops=int(lengths.get(name, 0) * 1e9), bytes_accessed=0, transcendentals=0
            ),
            name=name,
        )

    head = jnp.concatenate([residual.reshape(rows, lanes), offsets.reshape(2 * tiles, lanes)], 0)
    packed = call(
        lambda *refs: pack_kernel(layout, *refs),
        "pack",
        shape((rows + layout.offset_rows, lanes), bf16),
        [vmem],
        1,
    )(head)
    scale = 1.0 / math.sqrt(modes_x * modes_y * layout.panels)
    integers = jnp.stack([lattice_x, lattice_y, jnp.pad(frequency, (0, lanes - frequency.shape[0]))])

    def spectral(integers):
        return call(
            lambda *refs: spectral_kernel(layout, scale, *refs),
            "spectral",
            (shape((vectors, modes_y, modes_x), f32), shape((vectors, lanes), f32)),
            [vmem, vmem],
            4,
            [
                pltpu.SMEM((1, lanes), jnp.int32),
                pltpu.VMEM(spectral_weight.shape, f32),
                pltpu.SemaphoreType.DMA,
            ],
        )(integers, spectral_weight)

    blocks = kernel.reshape(tiles, 9, 2, lanes, lanes)
    neighbor = neighbor.reshape(tiles, 9)

    def table_shapes(size):
        return (
            shape((size // min(size, 4), wide, min(size, 4) * layout.local), bf16),
            shape((size, 2 * layout.quarter + 8, layout.local), f32),
        )

    def part_call(name, base, part, tables, total, halves, dtype):
        size = part.shape[0]
        high = len(halves) * tall // 2
        given = [part] + list(tables or ()) + ([] if total is None else [total])
        scratch = [pltpu.VMEM((high, min(size, 4) * layout.local), bf16)]
        if dtype != f32:
            scratch.append(pltpu.VMEM((high, wide), f32))
        with_start = total is not None
        return call(
            lambda *refs: part_kernel(layout, base, with_start, not tables, halves, *refs),
            name,
            (shape((high, wide), dtype), *(() if tables else table_shapes(size))),
            [vmem] * len(given),
            24,
            scratch,
            aliases={len(given) - 1: 0} if with_start and len(halves) == 2 else None,
        )(*given)

    def make(name, base, density):
        return call(
            lambda *refs: table_kernel(layout, base, *refs),
            name,
            table_shapes(density.shape[0]),
            [vmem],
            8,
        )(density)

    def gather_and_project(array, tables):
        array = array[None]
        total, base, made, seen = None, 0, [], []
        for k, mask in enumerate(layout.chip_masks):
            pairs = [(i, i ^ mask) for i in range(devices)]
            arrived = lax.ppermute(array, ("tile", "wave"), pairs)
            array = jnp.concatenate([array, arrived])
            seen.append(array)
            part = arrived if k else array
            if k < len(layout.chip_masks) - 1:
                total, *new = part_call("part", base, part, tables and tables[k], total, (0, 1), f32)
                base += part.shape[0]
                made.append(new or tables[k])
        made.append(make("tables", base, part))
        (leaving,) = part_call("leaving", base, part, made[-1], total, (1,), bf16)

        def stay(first):
            return part_call("staying", base, after(part, first), made[-1], total, (0,), f32)[0]

        return seen, leaving, stay, made

    def gather_chips(array, tables, other):
        array = array[None]
        total, base, seen = None, 0, []
        for k, mask in enumerate(layout.chip_masks):
            pairs = [(i, i ^ mask) for i in range(devices)]
            arrived = lax.ppermute(array, ("tile", "wave"), pairs)
            array = jnp.concatenate([array, arrived])
            seen.append(array)
            part = arrived if k else array
            wait = seen[min(k, 1)]
            more = make("tables", devices // 2 + base, after(other, wait)[base : base + part.shape[0]])
            given = [part, *tables[k], *more] + ([] if total is None else [total])
            width = layout.group_of(part) * layout.local
            total = call(
                lambda *refs, base=base, start=total is not None: chips_kernel(layout, base, start, *refs),
                "part" if k < len(layout.chip_masks) - 1 else "whole",
                shape((tall // 2, wide), f32),
                [vmem] * len(given),
                24,
                [pltpu.VMEM((tall // 2, width), bf16)] * 2,
                aliases={} if total is None else {len(given) - 1: 0},
            )(*given)
            base += part.shape[0]
        return seen, total

    def far_field(sums, weight, own_tables, other_tables):
        return call(
            lambda *refs: far_kernel(layout, *refs),
            "far",
            tuple([shape((rows // 2, lanes), f32)] * 2),
            [vmem] * (5 + len(sums)),
            24,
            [
                pltpu.VMEM((tall // 2, wide), f32),
                pltpu.VMEM((tall // 2, wide), bf16),
                pltpu.VMEM((tall // 2, layout.local), f32),
                pltpu.VMEM((tall // 2, layout.local), f32),
            ],
        )(*sums, weight, *own_tables, *other_tables)

    def near_field(density, whole):
        return call(
            lambda *refs: near_kernel(layout, whole, *refs),
            "near",
            tuple([shape((rows // 2, lanes), f32)] * 2),
            [vmem] * 3,
            12,
        )(density.reshape(-1, lanes), blocks, neighbor)

    def with_other_core(array):
        return jnp.concatenate([array, swap_cores(array)])

    seen, leaving, stay, tables = gather_and_project(packed, None)
    other_packed = swap_cores(after(packed, seen[0]))
    beside = make("other_tables", devices // 2, other_packed[None])
    weight, guess = spectral(after(integers, seen[1]))
    start = with_other_core(seen[-1])
    near_own, near_other = near_field(start, True)
    far_own, far_other = far_field((swap_cores(leaving), stay(near_own)), weight, tables[0], beside)
    basis, image_own, image_other = call(
        lambda *refs: first_kernel(layout, *refs),
        "first",
        (shape((rows, lanes), bf16), shape((rows // 2, lanes), f32), shape((rows // 2, lanes), f32)),
        [vmem] * 7,
        2,
    )(packed, other_packed, near_own, swap_cores(near_other), far_own, far_other, guess)
    seen, total = gather_chips(basis, tables, start[devices // 2 :])
    everything = with_other_core(seen[-1])
    factors = call(
        lambda *refs: scalar_kernel(layout, *refs),
        "scalars",
        shape((4 * vectors, lanes), f32),
        [vmem] * 3,
        1 + devices / 8,
    )(start, everything, guess)
    near_own, near_other = near_field(everything, False)
    far_own, far_other = far_field((total,), weight, tables[0], beside)
    result, scalars = call(
        lambda *refs: second_kernel(layout, *refs),
        "second",
        (shape((rows, lanes), f32), shape((4, vectors), f32)),
        [vmem] * 8,
        2,
    )(
        everything,
        near_own,
        near_other,
        far_own,
        swap_cores(far_other),
        image_own,
        swap_cores(image_other),
        factors,
    )
    return result.reshape(residual.shape), scalars


def solution(mesh):
    return jax.shard_map(
        per_device,
        mesh=mesh,
        in_specs=(
            P(("grp", "tile"), "wave", None, None, None),
            P(("grp", "tile"), "wave", None, None, None, None),
            P(("grp", "tile"), "wave", None, None),
            P(("grp", "tile"), "wave", None),
            P("grp"),
            P(),
            P(),
            P(),
        ),
        out_specs=(P(("grp", "tile"), "wave", None, None, None), P("grp", None)),
        check_vma=False,
    )
```
